32 devices in a mesh: tm: 4 (over x, core), gy: 2 (over y), gx: 4 (over z).
Axes of the slice: x: 2, y: 2, z: 4, core: 2. Of those that a mesh axis runs over, the one named last changes fastest.
Arguments:
- initial_state: float32 [2, 8, 64, 128], P(None, 'gy', 'gx'), may hold values from 0 to 1
- slice_guess: float32 [4, 2, 8, 64, 128], P('tm', None, 'gy', 'gx'), may hold values from 0 to 1
- feed_rate: float32 [8, 64, 128], P('gy', 'gx'), may hold values from 0.02 to 0.2
- kill_rate: float32 [8, 64, 128], P('gy', 'gx'), may hold values from 0.03 to 0.12
Outputs:
- final_states: float32 [4, 2, 8, 64, 128], P('tm', None, 'gy', 'gx')
The draws below stay inside these ranges and needn't reach their ends.
All inputs are finite; a program needn't handle non-finite values.
Results may differ from the reference program's by a relative error of at most 0.0001.
Values sent between devices are 32-bit elements; how exact they have to be, the bound alone decides.
No kernel may reach another device: no remote copies, remote signals or barrier semaphores. Data moves between devices by JAX's collectives and lax.ppermute only.
A program may use at most 64 MiB of HBM per device.

```python
import math
import jax
import jax.numpy as jnp

ITERS = 3
SLICES = 4
NX = 8
NY = 64
NZ = 128


def level_of(own_key, extent, shards, low, top_value):
    factor_of, own = 1.0, jax.random.fold_in(own_key, 6)
    for axis_at, blocks in shards:
        steps = jnp.exp(jax.random.uniform(jax.random.fold_in(own, axis_at), (blocks,), jnp.float32, low / len(shards), top_value / len(shards)))
        factor_of = factor_of * jnp.repeat(steps, extent[axis_at] // blocks).reshape([-1 if axis == axis_at else 1 for axis in range(len(extent))])
    return factor_of


def setup_inputs(seed: int = 0) -> dict:
    seeds = jax.random.split(jax.random.key(seed), 5)
    initial_state = jnp.clip(1.0 * jax.random.uniform(seeds[0], (2, NX, NY, NZ), jnp.float32) ** level_of(seeds[0], (2, NX, NY, NZ), ((1, 2), (2, 4)), -0.2, 0.2), 0.0, 1.0)
    slice_guess = jnp.clip(1.0 * jax.random.uniform(seeds[1], (SLICES, 2, NX, NY, NZ), jnp.float32) ** level_of(seeds[1], (SLICES, 2, NX, NY, NZ), ((0, 4), (2, 2), (3, 4)), -0.2, 0.2), 0.0, 1.0)
    feed_rate = jnp.clip(jnp.exp(math.log(0.2) - 2.3025851 * jax.random.uniform(seeds[2], (NX, NY, NZ), jnp.float32) ** level_of(seeds[2], (NX, NY, NZ), ((0, 2), (1, 4)), -0.2, 0.2)), 0.02, 0.2)
    kill_rate = jnp.clip(jnp.exp(math.log(0.12) - 1.3862944 * jax.random.uniform(seeds[3], (NX, NY, NZ), jnp.float32) ** level_of(seeds[3], (NX, NY, NZ), ((0, 2), (1, 4)), -0.2, 0.2)), 0.03, 0.12)
    return dict(initial_state=initial_state, slice_guess=slice_guess, feed_rate=feed_rate, kill_rate=kill_rate)


DIFF_U = 0.2
DIFF_V = 0.1
HALF_STEP = 0.5
WEIGHTS = ((5.0 / 24.0, 8.0 / 24.0, -1.0 / 24.0), (-1.0 / 24.0, 8.0 / 24.0, 5.0 / 24.0))


def restrict(grid_field):
    leading = grid_field.shape[:-3]
    size_x, size_y, size_z = grid_field.shape[-3:]
    blocks = grid_field.reshape(leading + (size_x // 2, 2, size_y // 2, 2, size_z // 2, 2))
    return 0.125 * jnp.sum(blocks, axis=(-5, -3, -1))


def prolong(grid_field):
    return jnp.repeat(jnp.repeat(jnp.repeat(grid_field, 2, axis=-3), 2, axis=-2), 2, axis=-1)


def source_terms(laplacian, state, feed_rate, kill_rate):
    conc_u = state[..., 0, :, :, :]
    conc_v = state[..., 1, :, :, :]
    reaction = conc_u * conc_v * conc_v
    rate_u = DIFF_U * laplacian[..., 0, :, :, :] - reaction + feed_rate * (1.0 - conc_u)
    rate_v = DIFF_V * laplacian[..., 1, :, :, :] + reaction - (feed_rate + kill_rate) * conc_v
    return jnp.stack([rate_u, rate_v], axis=-4)


def reaction_rates(state, feed_rate, kill_rate, spacing):
    summed = -6.0 * state
    for axis_index in (-3, -2, -1):
        summed = summed + jnp.roll(state, 1, axis_index) + jnp.roll(state, -1, axis_index)
    return source_terms(summed / (spacing * spacing), state, feed_rate, kill_rate)


def quadrature(values, interval):
    return WEIGHTS[interval][0] * values[0] + WEIGHTS[interval][1] * values[1] + WEIGHTS[interval][2] * values[2]


def reference(initial_state, slice_guess, feed_rate, kill_rate):
    coarse_feed = restrict(feed_rate)
    coarse_kill = restrict(kill_rate)
    guess_rates = jnp.zeros_like(slice_guess)
    node_values = [slice_guess, slice_guess, slice_guess]
    values = [guess_rates, guess_rates, guess_rates]
    coarse_end = restrict(slice_guess)
    coarse_anchor = restrict(initial_state)
    for sweep_index in range(ITERS):
        integral_zero = quadrature(values, 0)
        integral_one = quadrature(values, 1)
        start_state = jnp.concatenate([initial_state[None], node_values[2][:-1]], axis=0)
        coarse_start = jnp.concatenate([coarse_anchor[None], coarse_end[:-1]], axis=0)
        rate_zero = reaction_rates(start_state, feed_rate, kill_rate, 1.0)
        node_one = start_state + HALF_STEP * (rate_zero - values[0]) + integral_zero
        rate_one = reaction_rates(node_one, feed_rate, kill_rate, 1.0)
        node_two = node_one + HALF_STEP * (rate_one - values[1]) + integral_one
        rate_two = reaction_rates(node_two, feed_rate, kill_rate, 1.0)
        fresh = [rate_zero, rate_one, rate_two]
        fine_zero = quadrature(fresh, 0)
        fine_one = quadrature(fresh, 1)
        rest_zero = restrict(start_state)
        rest_one = restrict(node_one)
        rest_two = restrict(node_two)
        coarse_rate_zero = reaction_rates(rest_zero, coarse_feed, coarse_kill, 2.0)
        coarse_rate_one = reaction_rates(rest_one, coarse_feed, coarse_kill, 2.0)
        coarse_one = coarse_start + HALF_STEP * (reaction_rates(coarse_start, coarse_feed, coarse_kill, 2.0) - coarse_rate_zero) + restrict(fine_zero)
        coarse_two = coarse_one + HALF_STEP * (reaction_rates(coarse_one, coarse_feed, coarse_kill, 2.0) - coarse_rate_one) + restrict(fine_one)
        node_one = node_one + prolong(coarse_one - rest_one)
        node_two = node_two + prolong(coarse_two - rest_two)
        if sweep_index + 1 < ITERS:
            values = [rate_zero, reaction_rates(node_one, feed_rate, kill_rate, 1.0), reaction_rates(node_two, feed_rate, kill_rate, 1.0)]
        node_values = [start_state, node_one, node_two]
        coarse_end = coarse_two
    return node_values[2]
```

```python
import functools

import jax
import jax.numpy as jnp
from jax import lax
from jax.experimental import pallas as pl
from jax.experimental.pallas import tpu as pltpu
from jax.sharding import PartitionSpec as P

ITERS = 3
DIFF_U = 0.2
DIFF_V = 0.1
HALF_STEP = 0.5
WEIGHTS = ((5.0 / 24.0, 8.0 / 24.0, -1.0 / 24.0), (-1.0 / 24.0, 8.0 / 24.0, 5.0 / 24.0))

AXES = ("tm", "gy", "gx")
HALO = 5
RATE_HALO = 4
PACK = 6


def shifted(value, by_tm, by_gy, by_gx):
    n_tm, n_gy, n_gx = (lax.axis_size(axis) for axis in AXES)
    pairs = []
    for t in range(n_tm):
        for y in range(n_gy):
            for x in range(n_gx):
                target = ((t + by_tm) % n_tm * n_gy + (y + by_gy) % n_gy) * n_gx + (x + by_gx) % n_gx
                pairs.append(((t * n_gy + y) * n_gx + x, target))
    return lax.ppermute(value, AXES, pairs)


def near(row, distance, axis):
    size = row.shape[axis]
    return pltpu.roll(row, distance % size, axis) + pltpu.roll(row, -distance % size, axis)


def rates_of(state, feed, feed_kill, spacing):
    scale = 1.0 / (spacing * spacing)

    @functools.cache
    def at(r):
        (u, v), (ub, vb), (ua, va) = state(r), state(r - 1), state(r + 1)
        around_u = (ub + ua) + near(u, int(spacing), 0) + near(u, int(spacing), 1)
        around_v = (vb + va) + near(v, int(spacing), 0) + near(v, int(spacing), 1)
        reaction = u * (v * v)
        rate_u = (DIFF_U * scale) * around_u + feed(r) - (6.0 * DIFF_U * scale + feed(r)) * u - reaction
        rate_v = (DIFF_V * scale) * around_v - (6.0 * DIFF_V * scale + feed_kill(r)) * v + reaction
        return rate_u, rate_v

    return at


def half_sum(low, high):
    x, z = low.shape
    total = low + high
    total = total + pltpu.roll(total, z - 1, 1)
    total = total + pltpu.roll(total, x - 1, 0)
    return 0.125 * total


def restricted(state):
    @functools.cache
    def at(c):
        return tuple(half_sum(a, b) for a, b in zip(state(2 * c), state(2 * c + 1)))

    return at


def spread(row):
    even_x = lax.broadcasted_iota(jnp.int32, row.shape, 0) % 2 == 0
    even_z = lax.broadcasted_iota(jnp.int32, row.shape, 1) % 2 == 0
    row = jnp.where(even_z, row, pltpu.roll(row, 1, 1))
    return jnp.where(even_x, row, pltpu.roll(row, 1, 0))


def quadrature(values, interval):
    def at(r):
        zero, one, two = (value(r) for value in values)
        w = WEIGHTS[interval]
        return tuple(w[0] * a + w[1] * b + w[2] * c for a, b, c in zip(zero, one, two))

    return at


def iteration(start, feed, kill, old_rates):
    feed_kill = functools.cache(lambda r: feed(r) + kill(r))
    coarse_feed = functools.cache(lambda c: half_sum(feed(2 * c), feed(2 * c + 1)))
    coarse_sum = functools.cache(lambda c: half_sum(feed_kill(2 * c), feed_kill(2 * c + 1)))

    def stepped(state, rate, interval):
        @functools.cache
        def at(r):
            out = [s + HALF_STEP * f for s, f in zip(state(r), rate(r))]
            if old_rates is not None:
                integral = quadrature(old_rates, interval)(r)
                old = old_rates[interval](r)
                out = [o + (q - HALF_STEP * f) for o, q, f in zip(out, integral, old)]
            return tuple(out)

        return at

    fine = lambda state: rates_of(state, feed, feed_kill, 1.0)
    coarse = lambda state: rates_of(state, coarse_feed, coarse_sum, 2.0)
    rate_zero = fine(start)
    node_one = stepped(start, rate_zero, 0)
    rate_one = fine(node_one)
    node_two = stepped(node_one, rate_one, 1)
    rate_two = fine(node_two)
    fresh = (rate_zero, rate_one, rate_two)
    rest_zero, rest_one, rest_two = restricted(start), restricted(node_one), restricted(node_two)
    rest_integral = [restricted(quadrature(fresh, interval)) for interval in (0, 1)]
    coarse_start = rest_zero

    def coarse_stepped(state, rate, rest_rate, integral):
        @functools.cache
        def at(c):
            return tuple(
                s + HALF_STEP * (f - g) + q for s, f, g, q in zip(state(c), rate(c), rest_rate(c), integral(c))
            )

        return at

    coarse_one = coarse_stepped(coarse_start, coarse(coarse_start), coarse(rest_zero), rest_integral[0])
    coarse_two = coarse_stepped(coarse_one, coarse(coarse_one), coarse(rest_one), rest_integral[1])

    def corrected(node, coarse_node, rest):
        change = functools.cache(lambda c: tuple(spread(w - m) for w, m in zip(coarse_node(c), rest(c))))

        @functools.cache
        def at(r):
            return tuple(n + d for n, d in zip(node(r), change(r // 2)))

        return at

    return rate_zero, corrected(node_one, coarse_one, rest_one), corrected(node_two, coarse_two, rest_two)


def rows_of(ref, width, first):
    @functools.cache
    def at(r):
        assert 0 <= (r - first) * width < ref.shape[1]
        return tuple(ref[field, pl.ds((r - first) * width, width), :] for field in range(2))

    return at


def pack_kernel(last_ref, initial_ref, guess_ref, feed_ref, kill_ref, state_ref, all_ref, low_ref, high_ref):
    _, n_x, n_y, _ = initial_ref.shape
    is_last = last_ref[0] == 1
    for x in range(n_x):
        rows = pl.ds(x, n_y, stride=n_x)
        for field in range(2):
            tile = jnp.where(is_last, initial_ref[field, x], guess_ref[field, x])
            state_ref[field, rows, :] = tile
            all_ref[field, rows, :] = tile
        all_ref[2, rows, :] = feed_ref[x]
        all_ref[3, rows, :] = kill_ref[x]
    for field in range(4):
        low_ref[field] = all_ref[field, pl.ds(0, PACK * n_x), :]
        high_ref[field] = all_ref[field, pl.ds((n_y - PACK) * n_x, PACK * n_x), :]


def first_kernel(n_gy, n_x, n_y, *refs):
    state_ref, local_ref = refs[:2]
    others, lows, highs = refs[2 : 1 + n_gy], refs[1 + n_gy : 1 + 2 * n_gy], refs[1 + 2 * n_gy : 1 + 3 * n_gy]
    start_ref, params_ref, zero_ref, one_ref, two_ref, two_low, two_high, low_ref, high_ref = refs[1 + 3 * n_gy :]
    width = n_gy * n_x

    def collect(out_ref, field, source_field, middles):
        for gy in range(n_gy):
            pieces = [(-PACK, lows[gy], PACK), (0, middles[gy], n_y), (n_y, highs[gy], PACK)]
            for first, ref, count in pieces:
                for k in range(count):
                    if -HALO <= first + k < n_y + HALO:
                        place = pl.ds((first + k + HALO) * width + gy * n_x, n_x)
                        out_ref[field, place, :] = ref[source_field, pl.ds(k * n_x, n_x), :]

    for field in range(2):
        collect(start_ref, field, field, [state_ref, *others])
        collect(params_ref, field, 2 + field, [local_ref, *others])
    start = rows_of(start_ref, width, -HALO)
    params = rows_of(params_ref, width, -HALO)
    results = iteration(start, lambda r: params(r)[0], lambda r: params(r)[1], None)
    write_nodes(results, width, n_y, zero_ref, one_ref, two_ref, two_low, two_high, low_ref, high_ref)


def write_nodes(results, width, n_y, zero_ref, one_ref, two_ref, two_low, two_high, low_ref, high_ref):
    rate_zero, node_one, node_two = results
    for r in range(-RATE_HALO, n_y + RATE_HALO):
        if 0 <= r < n_y:
            place = pl.ds(r * width, width)
            for field, (one, two) in enumerate(zip(node_one(r), node_two(r))):
                one_ref[field, place, :] = one
                two_ref[field, place, :] = two
                for edge, pair_ref, edge_ref in ((0, two_low, low_ref), (n_y - HALO, two_high, high_ref)):
                    if edge <= r < edge + HALO:
                        beside = pl.ds((r - edge) * width, width)
                        pair_ref[field, beside, :] = two
                        edge_ref[field, beside, :] = one
                        edge_ref[2 + field, beside, :] = two
        for field, zero in enumerate(rate_zero(r)):
            zero_ref[field, pl.ds((r + RATE_HALO) * width, width), :] = zero


def later_kernel(
    width, n_y, out_x, first_ref, start_ref, params_ref, zero_ref, one_ref, two_ref, got_ref, got_low, got_high, low_ref, high_ref, *outs
):
    is_first = first_ref[0] == 1
    params = rows_of(params_ref, width, -HALO)
    feed, kill = (lambda r: params(r)[0]), (lambda r: params(r)[1])
    kept = rows_of(start_ref, width, -HALO)
    sources = [rows_of(got_low, width, -HALO), rows_of(got_ref, width, 0), rows_of(got_high, width, n_y)]

    def pick(r):
        return 0 if r < 0 else 1 if r < n_y else 2

    @functools.cache
    def start(r):
        return tuple(jnp.where(is_first, a, b) for a, b in zip(kept(r), sources[pick(r)](r)))

    def own(tile_ref, offset):
        pieces = [
            rows_of(low_ref.at[pl.ds(offset, 2)], width, -HALO),
            rows_of(tile_ref, width, 0),
            rows_of(high_ref.at[pl.ds(offset, 2)], width, n_y),
        ]
        return lambda r: pieces[pick(r)](r)

    old_zero = rows_of(zero_ref, width, -RATE_HALO)
    feed_kill = functools.cache(lambda r: feed(r) + kill(r))
    old_one, old_two = (rates_of(own(ref, offset), feed, feed_kill, 1.0) for ref, offset in ((one_ref, 0), (two_ref, 2)))
    results = iteration(start, feed, kill, (old_zero, old_one, old_two))
    if out_x is None:
        write_nodes(results, width, n_y, *outs)
    else:
        out_ref, scratch = outs
        for r in range(n_y):
            for field, value in enumerate(results[2](r)):
                scratch[field, pl.ds(r * width, width), :] = value
        for x in range(out_x):
            for field in range(2):
                out_ref[field, x] = scratch[field, pl.ds(x, n_y, stride=width), :]


def call(kernel, name, n_scalars, operands, shapes, scratch=()):
    specs = [pl.BlockSpec(memory_space=pltpu.SMEM)] * n_scalars
    specs += [pl.BlockSpec(memory_space=pltpu.VMEM)] * (len(operands) - n_scalars)
    return pl.pallas_call(
        kernel,
        name=name,
        out_shape=[jax.ShapeDtypeStruct(shape, jnp.float32) for shape in shapes],
        in_specs=specs,
        out_specs=[pl.BlockSpec(memory_space=pltpu.VMEM)] * len(shapes),
        scratch_shapes=scratch,
        compiler_params=pltpu.CompilerParams(vmem_limit_bytes=32 * 1024 * 1024),
    )(*operands)


def shards(initial_state, slice_guess, feed_rate, kill_rate):
    n_gy, n_tm = lax.axis_size("gy"), lax.axis_size("tm")
    _, n_x, n_y, n_z = initial_state.shape
    width = n_gy * n_x
    place = lax.axis_index("tm")
    is_first = (place == 0).astype(jnp.int32)[None]
    is_last = (place == n_tm - 1).astype(jnp.int32)[None]

    state, local, low, high = call(
        pack_kernel,
        "pack",
        1,
        (is_last, initial_state, slice_guess[0], feed_rate, kill_rate),
        [(2, n_y * n_x, n_z), (4, n_y * n_x, n_z), (4, PACK * n_x, n_z), (4, PACK * n_x, n_z)],
    )
    got = [shifted(state, 1, 0, 0), local]
    got += [shifted(local, 1, -gy, 0) for gy in range(1, n_gy)]
    got += [shifted(high, 1, -gy, 1) for gy in range(n_gy)]
    got += [shifted(low, 1, -gy, -1) for gy in range(n_gy)]

    tile, edge = (2, n_y * width, n_z), (2, HALO * width, n_z)
    node_shapes = [(2, (n_y + 2 * RATE_HALO) * width, n_z), tile, tile, edge, edge, (4, *edge[1:]), (4, *edge[1:])]
    window = (2, (n_y + 2 * HALO) * width, n_z)
    start, params, *nodes = call(
        functools.partial(first_kernel, n_gy, n_x, n_y), "first", 0, got, [window, window, *node_shapes]
    )
    for sweep_index in range(1, ITERS):
        zero, one, two, two_low, two_high, low, high = nodes
        got = [shifted(two, 1, 0, 0), shifted(two_high, 1, 0, 1), shifted(two_low, 1, 0, -1)]
        got += [shifted(high, 0, 0, 1), shifted(low, 0, 0, -1)]
        done = sweep_index + 1 == ITERS
        nodes = call(
            functools.partial(later_kernel, width, n_y, n_x if done else None),
            "last" if done else "later",
            1,
            (is_first, start, params, zero, one, two, *got),
            [initial_state.shape] if done else node_shapes,
            [pltpu.VMEM(tile, jnp.float32)] if done else (),
        )
    return nodes[0][None]


def solution(mesh):
    in_specs = (
        P(None, "gy", "gx", None),
        P("tm", None, "gy", "gx", None),
        P("gy", "gx", None),
        P("gy", "gx", None),
    )
    out_specs = P("tm", None, "gy", "gx", None)
    return jax.shard_map(shards, mesh=mesh, in_specs=in_specs, out_specs=out_specs, check_vma=False)
```

```python
import functools

import jax
import jax.numpy as jnp
from jax import lax
from jax.experimental import pallas as pl
from jax.experimental.pallas import tpu as pltpu
from jax.sharding import PartitionSpec as P

ITERS = 3
DIFF_U = 0.2
DIFF_V = 0.1
HALF_STEP = 0.5
WEIGHTS = ((5.0 / 24.0, 8.0 / 24.0, -1.0 / 24.0), (-1.0 / 24.0, 8.0 / 24.0, 5.0 / 24.0))

AXES = ("tm", "gy", "gx")
HALO = 5
RATE_HALO = 4
PACK = 6


def shifted(value, by_tm, by_gy, by_gx):
    n_tm, n_gy, n_gx = (lax.axis_size(axis) for axis in AXES)
    pairs = []
    for t in range(n_tm):
        for y in range(n_gy):
            for x in range(n_gx):
                target = ((t + by_tm) % n_tm * n_gy + (y + by_gy) % n_gy) * n_gx + (x + by_gx) % n_gx
                pairs.append(((t * n_gy + y) * n_gx + x, target))
    return lax.ppermute(value, AXES, pairs)


def near(row, distance, axis):
    size = row.shape[axis]
    return pltpu.roll(row, distance % size, axis) + pltpu.roll(row, -distance % size, axis)


def rates_of(state, feed, feed_kill, spacing):
    scale = 1.0 / (spacing * spacing)

    @functools.cache
    def at(r):
        (u, v), (ub, vb), (ua, va) = state(r), state(r - 1), state(r + 1)
        around_u = (ub + ua) + near(u, int(spacing), 0) + near(u, int(spacing), 1)
        around_v = (vb + va) + near(v, int(spacing), 0) + near(v, int(spacing), 1)
        reaction = u * (v * v)
        rate_u = (DIFF_U * scale) * around_u + feed(r) - (6.0 * DIFF_U * scale + feed(r)) * u - reaction
        rate_v = (DIFF_V * scale) * around_v - (6.0 * DIFF_V * scale + feed_kill(r)) * v + reaction
        return rate_u, rate_v

    return at


def half_sum(low, high):
    x, z = low.shape
    total = low + high
    total = total + pltpu.roll(total, z - 1, 1)
    total = total + pltpu.roll(total, x - 1, 0)
    return 0.125 * total


def restricted(state):
    @functools.cache
    def at(c):
        return tuple(half_sum(a, b) for a, b in zip(state(2 * c), state(2 * c + 1)))

    return at


def spread(row):
    even_x = lax.broadcasted_iota(jnp.int32, row.shape, 0) % 2 == 0
    even_z = lax.broadcasted_iota(jnp.int32, row.shape, 1) % 2 == 0
    row = jnp.where(even_z, row, pltpu.roll(row, 1, 1))
    return jnp.where(even_x, row, pltpu.roll(row, 1, 0))


def quadrature(values, interval):
    def at(r):
        zero, one, two = (value(r) for value in values)
        w = WEIGHTS[interval]
        return tuple(w[0] * a + w[1] * b + w[2] * c for a, b, c in zip(zero, one, two))

    return at


def iteration(start, feed, kill, old_rates):
    feed_kill = functools.cache(lambda r: feed(r) + kill(r))
    coarse_feed = functools.cache(lambda c: half_sum(feed(2 * c), feed(2 * c + 1)))
    coarse_sum = functools.cache(lambda c: half_sum(feed_kill(2 * c), feed_kill(2 * c + 1)))

    def stepped(state, rate, interval):
        @functools.cache
        def at(r):
            out = [s + HALF_STEP * f for s, f in zip(state(r), rate(r))]
            if old_rates is not None:
                integral = quadrature(old_rates, interval)(r)
                old = old_rates[interval](r)
                out = [o + (q - HALF_STEP * f) for o, q, f in zip(out, integral, old)]
            return tuple(out)

        return at

    fine = lambda state: rates_of(state, feed, feed_kill, 1.0)
    coarse = lambda state: rates_of(state, coarse_feed, coarse_sum, 2.0)
    rate_zero = fine(start)
    node_one = stepped(start, rate_zero, 0)
    rate_one = fine(node_one)
    node_two = stepped(node_one, rate_one, 1)
    rate_two = fine(node_two)
    fresh = (rate_zero, rate_one, rate_two)
    rest_zero, rest_one, rest_two = restricted(start), restricted(node_one), restricted(node_two)
    rest_integral = [restricted(quadrature(fresh, interval)) for interval in (0, 1)]
    coarse_start = rest_zero

    def coarse_stepped(state, rate, rest_rate, integral):
        @functools.cache
        def at(c):
            return tuple(
                s + HALF_STEP * (f - g) + q for s, f, g, q in zip(state(c), rate(c), rest_rate(c), integral(c))
            )

        return at

    coarse_one = coarse_stepped(coarse_start, coarse(coarse_start), coarse(rest_zero), rest_integral[0])
    coarse_two = coarse_stepped(coarse_one, coarse(coarse_one), coarse(rest_one), rest_integral[1])

    def corrected(node, coarse_node, rest):
        change = functools.cache(lambda c: tuple(spread(w - m) for w, m in zip(coarse_node(c), rest(c))))

        @functools.cache
        def at(r):
            return tuple(n + d for n, d in zip(node(r), change(r // 2)))

        return at

    return rate_zero, corrected(node_one, coarse_one, rest_one), corrected(node_two, coarse_two, rest_two)


def rows_of(ref, width, first):
    @functools.cache
    def at(r):
        assert 0 <= (r - first) * width < ref.shape[1]
        return tuple(ref[field, pl.ds((r - first) * width, width), :] for field in range(2))

    return at


def pack_kernel(last_ref, initial_hbm, guess_hbm, feed_hbm, kill_hbm, state_ref, all_ref, low_ref, high_ref, *scratch):
    initial_ref, guess_ref, feed_ref, kill_ref, arrived = scratch
    _, n_x, n_y, _ = initial_ref.shape
    is_last = last_ref[0] == 1
    pairs = ((initial_hbm, initial_ref), (guess_hbm, guess_ref), (feed_hbm, feed_ref), (kill_hbm, kill_ref))
    copies = [pltpu.make_async_copy(src, dst, arrived.at[i]) for i, (src, dst) in enumerate(pairs)]
    for copy in copies:
        copy.start()
    for copy in copies:
        copy.wait()
    for x in range(n_x):
        rows = pl.ds(x, n_y, stride=n_x)
        for field in range(2):
            tile = jnp.where(is_last, initial_ref[field, x], guess_ref[field, x])
            state_ref[field, rows, :] = tile
            all_ref[field, rows, :] = tile
        all_ref[2, rows, :] = feed_ref[x]
        all_ref[3, rows, :] = kill_ref[x]
    for field in range(4):
        low_ref[field] = all_ref[field, pl.ds(0, PACK * n_x), :]
        high_ref[field] = all_ref[field, pl.ds((n_y - PACK) * n_x, PACK * n_x), :]


def first_kernel(n_gy, n_x, n_y, *refs):
    state_ref, local_ref = refs[:2]
    others, lows, highs = refs[2 : 1 + n_gy], refs[1 + n_gy : 1 + 2 * n_gy], refs[1 + 2 * n_gy : 1 + 3 * n_gy]
    start_ref, params_ref, zero_ref, one_ref, two_ref, two_low, two_high, low_ref, high_ref = refs[1 + 3 * n_gy :]
    width = n_gy * n_x

    def collect(out_ref, field, source_field, middles):
        for gy in range(n_gy):
            pieces = [(-PACK, lows[gy], PACK), (0, middles[gy], n_y), (n_y, highs[gy], PACK)]
            for first, ref, count in pieces:
                for k in range(count):
                    if -HALO <= first + k < n_y + HALO:
                        place = pl.ds((first + k + HALO) * width + gy * n_x, n_x)
                        out_ref[field, place, :] = ref[source_field, pl.ds(k * n_x, n_x), :]

    for field in range(2):
        collect(start_ref, field, field, [state_ref, *others])
        collect(params_ref, field, 2 + field, [local_ref, *others])
    start = rows_of(start_ref, width, -HALO)
    params = rows_of(params_ref, width, -HALO)
    results = iteration(start, lambda r: params(r)[0], lambda r: params(r)[1], None)
    write_nodes(results, width, n_y, zero_ref, one_ref, two_ref, two_low, two_high, low_ref, high_ref)


def write_nodes(results, width, n_y, zero_ref, one_ref, two_ref, two_low, two_high, low_ref, high_ref):
    rate_zero, node_one, node_two = results
    for r in range(-RATE_HALO, n_y + RATE_HALO):
        if 0 <= r < n_y:
            place = pl.ds(r * width, width)
            for field, (one, two) in enumerate(zip(node_one(r), node_two(r))):
                one_ref[field, place, :] = one
                two_ref[field, place, :] = two
                for edge, pair_ref, edge_ref in ((0, two_low, low_ref), (n_y - HALO, two_high, high_ref)):
                    if edge <= r < edge + HALO:
                        beside = pl.ds((r - edge) * width, width)
                        pair_ref[field, beside, :] = two
                        edge_ref[field, beside, :] = one
                        edge_ref[2 + field, beside, :] = two
        for field, zero in enumerate(rate_zero(r)):
            zero_ref[field, pl.ds((r + RATE_HALO) * width, width), :] = zero


def later_kernel(
    width, n_y, out_x, first_ref, start_ref, params_ref, zero_ref, one_ref, two_ref, got_ref, got_low, got_high, low_ref, high_ref, *outs
):
    is_first = first_ref[0] == 1
    params = rows_of(params_ref, width, -HALO)
    feed, kill = (lambda r: params(r)[0]), (lambda r: params(r)[1])
    kept = rows_of(start_ref, width, -HALO)
    sources = [rows_of(got_low, width, -HALO), rows_of(got_ref, width, 0), rows_of(got_high, width, n_y)]

    def pick(r):
        return 0 if r < 0 else 1 if r < n_y else 2

    @functools.cache
    def start(r):
        return tuple(jnp.where(is_first, a, b) for a, b in zip(kept(r), sources[pick(r)](r)))

    def own(tile_ref, offset):
        pieces = [
            rows_of(low_ref.at[pl.ds(offset, 2)], width, -HALO),
            rows_of(tile_ref, width, 0),
            rows_of(high_ref.at[pl.ds(offset, 2)], width, n_y),
        ]
        return lambda r: pieces[pick(r)](r)

    old_zero = rows_of(zero_ref, width, -RATE_HALO)
    feed_kill = functools.cache(lambda r: feed(r) + kill(r))
    old_one, old_two = (rates_of(own(ref, offset), feed, feed_kill, 1.0) for ref, offset in ((one_ref, 0), (two_ref, 2)))
    results = iteration(start, feed, kill, (old_zero, old_one, old_two))
    if out_x is None:
        write_nodes(results, width, n_y, *outs)
    else:
        out_ref, scratch = outs
        for r in range(n_y):
            for field, value in enumerate(results[2](r)):
                scratch[field, pl.ds(r * width, width), :] = value
        for x in range(out_x):
            for field in range(2):
                out_ref[field, x] = scratch[field, pl.ds(x, n_y, stride=width), :]


def call(kernel, name, n_scalars, operands, shapes, scratch=(), space=pltpu.VMEM):
    specs = [pl.BlockSpec(memory_space=pltpu.SMEM)] * n_scalars
    specs += [pl.BlockSpec(memory_space=space)] * (len(operands) - n_scalars)
    return pl.pallas_call(
        kernel,
        name=name,
        out_shape=[jax.ShapeDtypeStruct(shape, jnp.float32) for shape in shapes],
        in_specs=specs,
        out_specs=[pl.BlockSpec(memory_space=pltpu.VMEM)] * len(shapes),
        scratch_shapes=scratch,
        compiler_params=pltpu.CompilerParams(vmem_limit_bytes=32 * 1024 * 1024),
    )(*operands)


def shards(initial_state, slice_guess, feed_rate, kill_rate):
    n_gy, n_tm = lax.axis_size("gy"), lax.axis_size("tm")
    _, n_x, n_y, n_z = initial_state.shape
    width = n_gy * n_x
    place = lax.axis_index("tm")
    is_first = (place == 0).astype(jnp.int32)[None]
    is_last = (place == n_tm - 1).astype(jnp.int32)[None]

    state, local, low, high = call(
        pack_kernel,
        "pack",
        1,
        (is_last, initial_state, slice_guess[0], feed_rate, kill_rate),
        [(2, n_y * n_x, n_z), (4, n_y * n_x, n_z), (4, PACK * n_x, n_z), (4, PACK * n_x, n_z)],
        [pltpu.VMEM(a.shape, jnp.float32) for a in (initial_state, slice_guess[0], feed_rate, kill_rate)]
        + [pltpu.SemaphoreType.DMA((4,))],
        pltpu.HBM,
    )
    got = [shifted(state, 1, 0, 0), local]
    got += [shifted(local, 1, -gy, 0) for gy in range(1, n_gy)]
    got += [shifted(high, 1, -gy, 1) for gy in range(n_gy)]
    got += [shifted(low, 1, -gy, -1) for gy in range(n_gy)]

    tile, edge = (2, n_y * width, n_z), (2, HALO * width, n_z)
    node_shapes = [(2, (n_y + 2 * RATE_HALO) * width, n_z), tile, tile, edge, edge, (4, *edge[1:]), (4, *edge[1:])]
    window = (2, (n_y + 2 * HALO) * width, n_z)
    start, params, *nodes = call(
        functools.partial(first_kernel, n_gy, n_x, n_y), "first", 0, got, [window, window, *node_shapes]
    )
    for sweep_index in range(1, ITERS):
        zero, one, two, two_low, two_high, low, high = nodes
        got = [shifted(two, 1, 0, 0), shifted(two_high, 1, 0, 1), shifted(two_low, 1, 0, -1)]
        got += [shifted(high, 0, 0, 1), shifted(low, 0, 0, -1)]
        done = sweep_index + 1 == ITERS
        nodes = call(
            functools.partial(later_kernel, width, n_y, n_x if done else None),
            "last" if done else "later",
            1,
            (is_first, start, params, zero, one, two, *got),
            [initial_state.shape] if done else node_shapes,
            [pltpu.VMEM(tile, jnp.float32)] if done else (),
        )
    return nodes[0][None]


def solution(mesh):
    in_specs = (
        P(None, "gy", "gx", None),
        P("tm", None, "gy", "gx", None),
        P("gy", "gx", None),
        P("gy", "gx", None),
    )
    out_specs = P("tm", None, "gy", "gx", None)
    return jax.shard_map(shards, mesh=mesh, in_specs=in_specs, out_specs=out_specs, check_vma=False)
```

```python
import functools

import jax
import jax.numpy as jnp
from jax import lax
from jax.experimental import pallas as pl
from jax.experimental.pallas import tpu as pltpu
from jax.sharding import PartitionSpec as P

ITERS = 3
DIFF_U = 0.2
DIFF_V = 0.1
HALF_STEP = 0.5
WEIGHTS = ((5.0 / 24.0, 8.0 / 24.0, -1.0 / 24.0), (-1.0 / 24.0, 8.0 / 24.0, 5.0 / 24.0))

AXES = ("tm", "gy", "gx")
HALO = 5
RATE_HALO = 4
PACK = 6


def shifted(value, by_tm, by_gy, by_gx):
    n_tm, n_gy, n_gx = (lax.axis_size(axis) for axis in AXES)
    pairs = []
    for t in range(n_tm):
        for y in range(n_gy):
            for x in range(n_gx):
                target = ((t + by_tm) % n_tm * n_gy + (y + by_gy) % n_gy) * n_gx + (x + by_gx) % n_gx
                pairs.append(((t * n_gy + y) * n_gx + x, target))
    return lax.ppermute(value, AXES, pairs)


def near(row, distance, axis):
    size = row.shape[axis]
    return pltpu.roll(row, distance % size, axis) + pltpu.roll(row, -distance % size, axis)


def rates_of(state, feed, feed_kill, spacing):
    scale = 1.0 / (spacing * spacing)

    @functools.cache
    def at(r):
        (u, v), (ub, vb), (ua, va) = state(r), state(r - 1), state(r + 1)
        around_u = (ub + ua) + near(u, int(spacing), 0) + near(u, int(spacing), 1)
        around_v = (vb + va) + near(v, int(spacing), 0) + near(v, int(spacing), 1)
        reaction = u * (v * v)
        rate_u = (DIFF_U * scale) * around_u + feed(r) - (6.0 * DIFF_U * scale + feed(r)) * u - reaction
        rate_v = (DIFF_V * scale) * around_v - (6.0 * DIFF_V * scale + feed_kill(r)) * v + reaction
        return rate_u, rate_v

    return at


def half_sum(low, high):
    x, z = low.shape
    total = low + high
    total = total + pltpu.roll(total, z - 1, 1)
    total = total + pltpu.roll(total, x - 1, 0)
    return 0.125 * total


def restricted(state):
    @functools.cache
    def at(c):
        return tuple(half_sum(a, b) for a, b in zip(state(2 * c), state(2 * c + 1)))

    return at


def spread(row):
    even_x = lax.broadcasted_iota(jnp.int32, row.shape, 0) % 2 == 0
    even_z = lax.broadcasted_iota(jnp.int32, row.shape, 1) % 2 == 0
    row = jnp.where(even_z, row, pltpu.roll(row, 1, 1))
    return jnp.where(even_x, row, pltpu.roll(row, 1, 0))


def quadrature(values, interval):
    def at(r):
        zero, one, two = (value(r) for value in values)
        w = WEIGHTS[interval]
        return tuple(w[0] * a + w[1] * b + w[2] * c for a, b, c in zip(zero, one, two))

    return at


def iteration(start, feed, kill, old_rates):
    feed_kill = functools.cache(lambda r: feed(r) + kill(r))
    coarse_feed = functools.cache(lambda c: half_sum(feed(2 * c), feed(2 * c + 1)))
    coarse_sum = functools.cache(lambda c: half_sum(feed_kill(2 * c), feed_kill(2 * c + 1)))

    def stepped(state, rate, interval):
        @functools.cache
        def at(r):
            out = [s + HALF_STEP * f for s, f in zip(state(r), rate(r))]
            if old_rates is not None:
                integral = quadrature(old_rates, interval)(r)
                old = old_rates[interval](r)
                out = [o + (q - HALF_STEP * f) for o, q, f in zip(out, integral, old)]
            return tuple(out)

        return at

    fine = lambda state: rates_of(state, feed, feed_kill, 1.0)
    coarse = lambda state: rates_of(state, coarse_feed, coarse_sum, 2.0)
    rate_zero = fine(start)
    node_one = stepped(start, rate_zero, 0)
    rate_one = fine(node_one)
    node_two = stepped(node_one, rate_one, 1)
    rate_two = fine(node_two)
    fresh = (rate_zero, rate_one, rate_two)
    rest_zero, rest_one, rest_two = restricted(start), restricted(node_one), restricted(node_two)
    rest_integral = [restricted(quadrature(fresh, interval)) for interval in (0, 1)]
    coarse_start = rest_zero

    def coarse_stepped(state, rate, rest_rate, integral):
        @functools.cache
        def at(c):
            return tuple(
                s + HALF_STEP * (f - g) + q for s, f, g, q in zip(state(c), rate(c), rest_rate(c), integral(c))
            )

        return at

    coarse_one = coarse_stepped(coarse_start, coarse(coarse_start), coarse(rest_zero), rest_integral[0])
    coarse_two = coarse_stepped(coarse_one, coarse(coarse_one), coarse(rest_one), rest_integral[1])

    def corrected(node, coarse_node, rest):
        change = functools.cache(lambda c: tuple(spread(w - m) for w, m in zip(coarse_node(c), rest(c))))

        @functools.cache
        def at(r):
            return tuple(n + d for n, d in zip(node(r), change(r // 2)))

        return at

    return rate_zero, corrected(node_one, coarse_one, rest_one), corrected(node_two, coarse_two, rest_two)


def rows_of(ref, width, first):
    @functools.cache
    def at(r):
        assert 0 <= (r - first) * width < ref.shape[1]
        return tuple(ref[field, pl.ds((r - first) * width, width), :] for field in range(2))

    return at


def pack_kernel(tiles_ref, state_ref, all_ref, low_ref, high_ref):
    n_fields, n_x, n_y, _ = tiles_ref.shape
    for field in range(n_fields):
        for x in range(n_x):
            all_ref[field, pl.ds(x, n_y, stride=n_x), :] = tiles_ref[field, x]
        low_ref[field] = all_ref[field, pl.ds(0, PACK * n_x), :]
        high_ref[field] = all_ref[field, pl.ds((n_y - PACK) * n_x, PACK * n_x), :]
    for field in range(2):
        state_ref[field] = all_ref[field]


def first_kernel(n_gy, n_x, n_y, *refs):
    state_ref, local_ref = refs[:2]
    others, lows, highs = refs[2 : 1 + n_gy], refs[1 + n_gy : 1 + 2 * n_gy], refs[1 + 2 * n_gy : 1 + 3 * n_gy]
    start_ref, params_ref, zero_ref, one_ref, two_ref, two_low, two_high, low_ref, high_ref = refs[1 + 3 * n_gy :]
    width = n_gy * n_x

    def collect(out_ref, field, source_field, middles):
        for gy in range(n_gy):
            pieces = [(-PACK, lows[gy], PACK), (0, middles[gy], n_y), (n_y, highs[gy], PACK)]
            for first, ref, count in pieces:
                for k in range(count):
                    if -HALO <= first + k < n_y + HALO:
                        place = pl.ds((first + k + HALO) * width + gy * n_x, n_x)
                        out_ref[field, place, :] = ref[source_field, pl.ds(k * n_x, n_x), :]

    for field in range(2):
        collect(start_ref, field, field, [state_ref, *others])
        collect(params_ref, field, 2 + field, [local_ref, *others])
    start = rows_of(start_ref, width, -HALO)
    params = rows_of(params_ref, width, -HALO)
    results = iteration(start, lambda r: params(r)[0], lambda r: params(r)[1], None)
    write_nodes(results, width, n_y, zero_ref, one_ref, two_ref, two_low, two_high, low_ref, high_ref)


def write_nodes(results, width, n_y, zero_ref, one_ref, two_ref, two_low, two_high, low_ref, high_ref):
    rate_zero, node_one, node_two = results
    for r in range(-RATE_HALO, n_y + RATE_HALO):
        if 0 <= r < n_y:
            place = pl.ds(r * width, width)
            for field, (one, two) in enumerate(zip(node_one(r), node_two(r))):
                one_ref[field, place, :] = one
                two_ref[field, place, :] = two
                for edge, pair_ref, edge_ref in ((0, two_low, low_ref), (n_y - HALO, two_high, high_ref)):
                    if edge <= r < edge + HALO:
                        beside = pl.ds((r - edge) * width, width)
                        pair_ref[field, beside, :] = two
                        edge_ref[field, beside, :] = one
                        edge_ref[2 + field, beside, :] = two
        for field, zero in enumerate(rate_zero(r)):
            zero_ref[field, pl.ds((r + RATE_HALO) * width, width), :] = zero


def later_kernel(
    width, n_y, out_x, first_ref, start_ref, params_ref, zero_ref, one_ref, two_ref, got_ref, got_low, got_high, low_ref, high_ref, *outs
):
    is_first = first_ref[0] == 1
    params = rows_of(params_ref, width, -HALO)
    feed, kill = (lambda r: params(r)[0]), (lambda r: params(r)[1])
    kept = rows_of(start_ref, width, -HALO)
    sources = [rows_of(got_low, width, -HALO), rows_of(got_ref, width, 0), rows_of(got_high, width, n_y)]

    def pick(r):
        return 0 if r < 0 else 1 if r < n_y else 2

    @functools.cache
    def start(r):
        return tuple(jnp.where(is_first, a, b) for a, b in zip(kept(r), sources[pick(r)](r)))

    def own(tile_ref, offset):
        pieces = [
            rows_of(low_ref.at[pl.ds(offset, 2)], width, -HALO),
            rows_of(tile_ref, width, 0),
            rows_of(high_ref.at[pl.ds(offset, 2)], width, n_y),
        ]
        return lambda r: pieces[pick(r)](r)

    old_zero = rows_of(zero_ref, width, -RATE_HALO)
    feed_kill = functools.cache(lambda r: feed(r) + kill(r))
    old_one, old_two = (rates_of(own(ref, offset), feed, feed_kill, 1.0) for ref, offset in ((one_ref, 0), (two_ref, 2)))
    results = iteration(start, feed, kill, (old_zero, old_one, old_two))
    if out_x is None:
        write_nodes(results, width, n_y, *outs)
    else:
        out_ref, scratch = outs
        for r in range(n_y):
            for field, value in enumerate(results[2](r)):
                scratch[field, pl.ds(r * width, width), :] = value
        for x in range(out_x):
            for field in range(2):
                out_ref[field, x] = scratch[field, pl.ds(x, n_y, stride=width), :]


def call(kernel, name, n_scalars, operands, shapes, scratch=()):
    specs = [pl.BlockSpec(memory_space=pltpu.SMEM)] * n_scalars
    specs += [pl.BlockSpec(memory_space=pltpu.VMEM)] * (len(operands) - n_scalars)
    return pl.pallas_call(
        kernel,
        name=name,
        out_shape=[jax.ShapeDtypeStruct(shape, jnp.float32) for shape in shapes],
        in_specs=specs,
        out_specs=[pl.BlockSpec(memory_space=pltpu.VMEM)] * len(shapes),
        scratch_shapes=scratch,
        compiler_params=pltpu.CompilerParams(vmem_limit_bytes=32 * 1024 * 1024),
    )(*operands)


def shards(initial_state, slice_guess, feed_rate, kill_rate):
    n_gy, n_tm = lax.axis_size("gy"), lax.axis_size("tm")
    _, n_x, n_y, n_z = initial_state.shape
    width = n_gy * n_x
    place = lax.axis_index("tm")
    is_first = (place == 0).astype(jnp.int32)[None]

    sent = jnp.where(place == n_tm - 1, initial_state, slice_guess[0])
    state, local, low, high = call(
        pack_kernel,
        "pack",
        0,
        (jnp.concatenate([sent, feed_rate[None], kill_rate[None]]),),
        [(2, n_y * n_x, n_z), (4, n_y * n_x, n_z), (4, PACK * n_x, n_z), (4, PACK * n_x, n_z)],
    )
    got = [shifted(state, 1, 0, 0), local]
    got += [shifted(local, 1, -gy, 0) for gy in range(1, n_gy)]
    got += [shifted(high, 1, -gy, 1) for gy in range(n_gy)]
    got += [shifted(low, 1, -gy, -1) for gy in range(n_gy)]

    tile, edge = (2, n_y * width, n_z), (2, HALO * width, n_z)
    node_shapes = [(2, (n_y + 2 * RATE_HALO) * width, n_z), tile, tile, edge, edge, (4, *edge[1:]), (4, *edge[1:])]
    window = (2, (n_y + 2 * HALO) * width, n_z)
    start, params, *nodes = call(
        functools.partial(first_kernel, n_gy, n_x, n_y), "first", 0, got, [window, window, *node_shapes]
    )
    for sweep_index in range(1, ITERS):
        zero, one, two, two_low, two_high, low, high = nodes
        got = [shifted(two, 1, 0, 0), shifted(two_high, 1, 0, 1), shifted(two_low, 1, 0, -1)]
        got += [shifted(high, 0, 0, 1), shifted(low, 0, 0, -1)]
        done = sweep_index + 1 == ITERS
        nodes = call(
            functools.partial(later_kernel, width, n_y, n_x if done else None),
            "last" if done else "later",
            1,
            (is_first, start, params, zero, one, two, *got),
            [initial_state.shape] if done else node_shapes,
            [pltpu.VMEM(tile, jnp.float32)] if done else (),
        )
    return nodes[0][None]


def solution(mesh):
    in_specs = (
        P(None, "gy", "gx", None),
        P("tm", None, "gy", "gx", None),
        P("gy", "gx", None),
        P("gy", "gx", None),
    )
    out_specs = P("tm", None, "gy", "gx", None)
    return jax.shard_map(shards, mesh=mesh, in_specs=in_specs, out_specs=out_specs, check_vma=False)
```

```python
import functools

import jax
import jax.numpy as jnp
from jax import lax
from jax.experimental import pallas as pl
from jax.experimental.pallas import tpu as pltpu
from jax.sharding import PartitionSpec as P

ITERS = 3
DIFF_U = 0.2
DIFF_V = 0.1
HALF_STEP = 0.5
WEIGHTS = ((5.0 / 24.0, 8.0 / 24.0, -1.0 / 24.0), (-1.0 / 24.0, 8.0 / 24.0, 5.0 / 24.0))

AXES = ("tm", "gy", "gx")
HALO = 5
RATE_HALO = 4
DRIFT = 6
TAKE = HALO + DRIFT
BELOW, ABOVE = TAKE + 1, HALO + 1


def shifted(value, by_tm, by_gy, by_gx):
    n_tm, n_gy, n_gx = (lax.axis_size(axis) for axis in AXES)
    pairs = []
    for t in range(n_tm):
        for y in range(n_gy):
            for x in range(n_gx):
                target = ((t + by_tm) % n_tm * n_gy + (y + by_gy) % n_gy) * n_gx + (x + by_gx) % n_gx
                pairs.append(((t * n_gy + y) * n_gx + x, target))
    return lax.ppermute(value, AXES, pairs)


def near(row, distance, axis):
    size = row.shape[axis]
    return pltpu.roll(row, distance % size, axis) + pltpu.roll(row, -distance % size, axis)


def rates_of(state, feed, feed_kill, spacing):
    scale = 1.0 / (spacing * spacing)

    @functools.cache
    def at(r):
        (u, v), (ub, vb), (ua, va) = state(r), state(r - 1), state(r + 1)
        around_u = (ub + ua) + near(u, int(spacing), 0) + near(u, int(spacing), 1)
        around_v = (vb + va) + near(v, int(spacing), 0) + near(v, int(spacing), 1)
        reaction = u * (v * v)
        rate_u = (DIFF_U * scale) * around_u + feed(r) - (6.0 * DIFF_U * scale + feed(r)) * u - reaction
        rate_v = (DIFF_V * scale) * around_v - (6.0 * DIFF_V * scale + feed_kill(r)) * v + reaction
        return rate_u, rate_v

    return at


def half_sum(low, high):
    x, z = low.shape
    total = low + high
    total = total + pltpu.roll(total, z - 1, 1)
    total = total + pltpu.roll(total, x - 1, 0)
    return 0.125 * total


def restricted(state):
    @functools.cache
    def at(c):
        return tuple(half_sum(a, b) for a, b in zip(state(2 * c), state(2 * c + 1)))

    return at


def spread(row):
    even_x = lax.broadcasted_iota(jnp.int32, row.shape, 0) % 2 == 0
    even_z = lax.broadcasted_iota(jnp.int32, row.shape, 1) % 2 == 0
    row = jnp.where(even_z, row, pltpu.roll(row, 1, 1))
    return jnp.where(even_x, row, pltpu.roll(row, 1, 0))


def quadrature(values, interval):
    def at(r):
        zero, one, two = (value(r) for value in values)
        w = WEIGHTS[interval]
        return tuple(w[0] * a + w[1] * b + w[2] * c for a, b, c in zip(zero, one, two))

    return at


def iteration(start, feed, kill, old_rates):
    feed_kill = functools.cache(lambda r: feed(r) + kill(r))
    coarse_feed = functools.cache(lambda c: half_sum(feed(2 * c), feed(2 * c + 1)))
    coarse_sum = functools.cache(lambda c: half_sum(feed_kill(2 * c), feed_kill(2 * c + 1)))

    def stepped(state, rate, interval):
        @functools.cache
        def at(r):
            out = [s + HALF_STEP * f for s, f in zip(state(r), rate(r))]
            if old_rates is not None:
                integral = quadrature(old_rates, interval)(r)
                old = old_rates[interval](r)
                out = [o + (q - HALF_STEP * f) for o, q, f in zip(out, integral, old)]
            return tuple(out)

        return at

    fine = lambda state: rates_of(state, feed, feed_kill, 1.0)
    coarse = lambda state: rates_of(state, coarse_feed, coarse_sum, 2.0)
    rate_zero = fine(start)
    node_one = stepped(start, rate_zero, 0)
    rate_one = fine(node_one)
    node_two = stepped(node_one, rate_one, 1)
    rate_two = fine(node_two)
    fresh = (rate_zero, rate_one, rate_two)
    rest_zero, rest_one, rest_two = restricted(start), restricted(node_one), restricted(node_two)
    rest_integral = [restricted(quadrature(fresh, interval)) for interval in (0, 1)]
    coarse_start = rest_zero

    def coarse_stepped(state, rate, rest_rate, integral):
        @functools.cache
        def at(c):
            return tuple(
                s + HALF_STEP * (f - g) + q for s, f, g, q in zip(state(c), rate(c), rest_rate(c), integral(c))
            )

        return at

    coarse_one = coarse_stepped(coarse_start, coarse(coarse_start), coarse(rest_zero), rest_integral[0])
    coarse_two = coarse_stepped(coarse_one, coarse(coarse_one), coarse(rest_one), rest_integral[1])

    def corrected(node, coarse_node, rest):
        change = functools.cache(lambda c: tuple(spread(w - m) for w, m in zip(coarse_node(c), rest(c))))

        @functools.cache
        def at(r):
            return tuple(n + d for n, d in zip(node(r), change(r // 2)))

        return at

    return rate_zero, corrected(node_one, coarse_one, rest_one), corrected(node_two, coarse_two, rest_two)


def rows_of(ref, width, first):
    @functools.cache
    def at(r):
        assert 0 <= (r - first) * width < ref.shape[1]
        return tuple(ref[field, pl.ds((r - first) * width, width), :] for field in range(2))

    return at


def pack_kernel(tiles_ref, state_ref, all_ref, low_ref, high_ref):
    n_fields, n_x, n_y, _ = tiles_ref.shape
    for field in range(n_fields):
        for x in range(n_x):
            all_ref[field, pl.ds(x, n_y, stride=n_x), :] = tiles_ref[field, x]
        low_ref[field] = all_ref[field, pl.ds(0, ABOVE * n_x), :]
        high_ref[field] = all_ref[field, pl.ds((n_y - BELOW) * n_x, BELOW * n_x), :]
    for field in range(2):
        state_ref[field] = all_ref[field]


def first_kernel(n_gy, n_x, n_y, *refs):
    state_ref, local_ref = refs[:2]
    others, lows, highs = refs[2 : 1 + n_gy], refs[1 + n_gy : 1 + 2 * n_gy], refs[1 + 2 * n_gy : 1 + 3 * n_gy]
    start_ref, params_ref, *outs = refs[1 + 3 * n_gy :]
    width = n_gy * n_x

    def collect(out_ref, field, source_field, middles):
        for gy in range(n_gy):
            pieces = [(-BELOW, lows[gy], BELOW), (0, middles[gy], n_y), (n_y, highs[gy], ABOVE)]
            for first, ref, count in pieces:
                for k in range(count):
                    if -TAKE <= first + k < n_y + HALO:
                        place = pl.ds((first + k + TAKE) * width + gy * n_x, n_x)
                        out_ref[field, place, :] = ref[source_field, pl.ds(k * n_x, n_x), :]

    for field in range(2):
        collect(start_ref, field, field, [state_ref, *others])
        collect(params_ref, field, 2 + field, [local_ref, *others])
    start = rows_of(start_ref, width, -TAKE)
    params = rows_of(params_ref, width, -TAKE)
    results = iteration(start, lambda r: params(r)[0], lambda r: params(r)[1], None)
    write_nodes(results, width, n_y, -1, -RATE_HALO - DRIFT, *outs)


def write_nodes(results, width, n_y, toward, zero_first, zero_ref, one_ref, two_ref, two_edge, edge_ref):
    rate_zero, node_one, node_two = results
    edge = 0 if toward > 0 else n_y - TAKE
    zero_edge = RATE_HALO if toward > 0 else n_y - RATE_HALO - DRIFT
    for r in range(zero_first, n_y + RATE_HALO):
        if 0 <= r < n_y:
            place = pl.ds(r * width, width)
            for field, (one, two) in enumerate(zip(node_one(r), node_two(r))):
                one_ref[field, place, :] = one
                two_ref[field, place, :] = two
                if edge <= r < edge + TAKE:
                    two_edge[field, pl.ds((r - edge) * width, width), :] = two
                    edge_ref[pl.ds((field * TAKE + r - edge) * width, width), :] = one
                    edge_ref[pl.ds(((2 + field) * TAKE + r - edge) * width, width), :] = two
        for field, zero in enumerate(rate_zero(r)):
            zero_ref[field, pl.ds((r - zero_first) * width, width), :] = zero
            if zero_first == -RATE_HALO and zero_edge <= r < zero_edge + DRIFT:
                edge_ref[pl.ds((4 * TAKE + field * DRIFT + r - zero_edge) * width, width), :] = zero


def later_kernel(width, n_y, out_x, toward, offset, zero_first, *refs):
    first_ref, start_ref, params_ref, zero_ref, one_ref, two_ref, got_ref, got_edge, edge_ref, *outs = refs
    is_first = first_ref[0] == 1
    params = rows_of(params_ref, width, -TAKE)
    feed, kill = (lambda r: params(r + offset)[0]), (lambda r: params(r + offset)[1])
    kept = rows_of(start_ref, width, -TAKE)
    beside = -TAKE if toward < 0 else n_y

    def edge_rows(place, first, count):
        @functools.cache
        def at(r):
            assert 0 <= r - first < count
            return tuple(edge_ref[pl.ds((place + f * count + r - first) * width, width), :] for f in range(2))

        return at

    def moved(inside, outside, low, high):
        return lambda r: (inside if low <= r + toward * DRIFT < high else outside)(r + toward * DRIFT)

    got = moved(rows_of(got_ref, width, 0), rows_of(got_edge, width, beside), 0, n_y)

    @functools.cache
    def start(r):
        return tuple(jnp.where(is_first, a, b) for a, b in zip(kept(r + offset), got(r)))

    zero_beside = -RATE_HALO - DRIFT if toward < 0 else n_y + RATE_HALO
    old_zero = moved(
        rows_of(zero_ref, width, zero_first),
        edge_rows(4 * TAKE, zero_beside, DRIFT),
        zero_first,
        n_y + RATE_HALO,
    )
    feed_kill = functools.cache(lambda r: feed(r) + kill(r))
    old_one, old_two = (
        rates_of(
            moved(rows_of(ref, width, 0), edge_rows(field * TAKE, beside, TAKE), 0, n_y), feed, feed_kill, 1.0
        )
        for field, ref in ((0, one_ref), (2, two_ref))
    )
    results = iteration(start, feed, kill, (old_zero, old_one, old_two))
    if out_x is None:
        write_nodes(results, width, n_y, -toward, -RATE_HALO, *outs)
    else:
        out_ref, scratch = outs
        for r in range(n_y):
            for field, value in enumerate(results[2](r)):
                scratch[field, pl.ds(r * width, width), :] = value
        for x in range(out_x):
            for field in range(2):
                out_ref[field, x] = scratch[field, pl.ds(x, n_y, stride=width), :]


def call(kernel, name, n_scalars, operands, shapes, scratch=()):
    specs = [pl.BlockSpec(memory_space=pltpu.SMEM)] * n_scalars
    specs += [pl.BlockSpec(memory_space=pltpu.VMEM)] * (len(operands) - n_scalars)
    return pl.pallas_call(
        kernel,
        name=name,
        out_shape=[jax.ShapeDtypeStruct(shape, jnp.float32) for shape in shapes],
        in_specs=specs,
        out_specs=[pl.BlockSpec(memory_space=pltpu.VMEM)] * len(shapes),
        scratch_shapes=scratch,
        compiler_params=pltpu.CompilerParams(vmem_limit_bytes=32 * 1024 * 1024),
    )(*operands)


def shards(initial_state, slice_guess, feed_rate, kill_rate):
    n_gy, n_tm = lax.axis_size("gy"), lax.axis_size("tm")
    _, n_x, n_y, n_z = initial_state.shape
    width = n_gy * n_x
    place = lax.axis_index("tm")
    is_first = (place == 0).astype(jnp.int32)[None]

    sent = jnp.where(place == n_tm - 1, initial_state, slice_guess[0])
    state, local, low, high = call(
        pack_kernel,
        "pack",
        0,
        (jnp.concatenate([sent, feed_rate[None], kill_rate[None]]),),
        [(2, n_y * n_x, n_z), (4, n_y * n_x, n_z), (4, ABOVE * n_x, n_z), (4, BELOW * n_x, n_z)],
    )
    got = [shifted(state, 1, 0, 0), local]
    got += [shifted(local, 1, -gy, 0) for gy in range(1, n_gy)]
    got += [shifted(high, 1, -gy, 1) for gy in range(n_gy)]
    got += [shifted(low, 1, -gy, -1) for gy in range(n_gy)]

    def node_shapes(zero_rows, edge_rows):
        tile = (2, n_y * width, n_z)
        return [(2, zero_rows * width, n_z), tile, tile, (2, TAKE * width, n_z), (edge_rows * width, n_z)]

    window = (2, (TAKE + n_y + HALO) * width, n_z)
    start, params, *nodes = call(
        functools.partial(first_kernel, n_gy, n_x, n_y),
        "first",
        0,
        got,
        [window, window, *node_shapes(n_y + 2 * RATE_HALO + DRIFT, 4 * TAKE)],
    )
    zero_first = -RATE_HALO - DRIFT
    for sweep_index in range(1, ITERS):
        toward = -1 if sweep_index % 2 else 1
        zero, one, two, two_edge, edge = nodes
        got = [shifted(two, 1, 0, 0), shifted(two_edge, 1, 0, -toward), shifted(edge, 0, 0, -toward)]
        done = sweep_index + 1 == ITERS
        offset = -DRIFT if toward < 0 else 0
        nodes = call(
            functools.partial(later_kernel, width, n_y, n_x if done else None, toward, offset, zero_first),
            "last" if done else "later",
            1,
            (is_first, start, params, zero, one, two, *got),
            [initial_state.shape] if done else node_shapes(n_y + 2 * RATE_HALO, 4 * TAKE + 2 * DRIFT),
            [pltpu.VMEM((2, n_y * width, n_z), jnp.float32)] if done else (),
        )
        zero_first = -RATE_HALO
    return nodes[0][None]


def solution(mesh):
    in_specs = (
        P(None, "gy", "gx", None),
        P("tm", None, "gy", "gx", None),
        P("gy", "gx", None),
        P("gy", "gx", None),
    )
    out_specs = P("tm", None, "gy", "gx", None)
    return jax.shard_map(shards, mesh=mesh, in_specs=in_specs, out_specs=out_specs, check_vma=False)
```

```python
import functools

import jax
import jax.numpy as jnp
from jax import lax
from jax.experimental import pallas as pl
from jax.experimental.pallas import tpu as pltpu
from jax.sharding import PartitionSpec as P

ITERS = 3
DIFF_U = 0.2
DIFF_V = 0.1
HALF_STEP = 0.5
WEIGHTS = ((5.0 / 24.0, 8.0 / 24.0, -1.0 / 24.0), (-1.0 / 24.0, 8.0 / 24.0, 5.0 / 24.0))

AXES = ("tm", "gy", "gx")
HALO = 5
RATE_HALO = 4
DRIFT = 6
TAKE = HALO + DRIFT
BELOW, ABOVE = TAKE + 1, HALO + 1


def shifted(value, by_tm, by_gy, by_gx):
    n_tm, n_gy, n_gx = (lax.axis_size(axis) for axis in AXES)
    pairs = []
    for t in range(n_tm):
        for y in range(n_gy):
            for x in range(n_gx):
                target = ((t + by_tm) % n_tm * n_gy + (y + by_gy) % n_gy) * n_gx + (x + by_gx) % n_gx
                pairs.append(((t * n_gy + y) * n_gx + x, target))
    return lax.ppermute(value, AXES, pairs)


def near(row, distance, axis):
    size = row.shape[axis]
    return pltpu.roll(row, distance % size, axis) + pltpu.roll(row, -distance % size, axis)


def rates_of(state, feed, feed_kill, spacing):
    scale = 1.0 / (spacing * spacing)

    @functools.cache
    def at(r):
        (u, v), (ub, vb), (ua, va) = state(r), state(r - 1), state(r + 1)
        around_u = (ub + ua) + near(u, int(spacing), 0) + near(u, int(spacing), 1)
        around_v = (vb + va) + near(v, int(spacing), 0) + near(v, int(spacing), 1)
        reaction = u * (v * v)
        rate_u = (DIFF_U * scale) * around_u + feed(r) - (6.0 * DIFF_U * scale + feed(r)) * u - reaction
        rate_v = (DIFF_V * scale) * around_v - (6.0 * DIFF_V * scale + feed_kill(r)) * v + reaction
        return rate_u, rate_v

    return at


def half_sum(low, high):
    x, z = low.shape
    total = low + high
    total = total + pltpu.roll(total, z - 1, 1)
    total = total + pltpu.roll(total, x - 1, 0)
    return 0.125 * total


def restricted(state):
    @functools.cache
    def at(c):
        return tuple(half_sum(a, b) for a, b in zip(state(2 * c), state(2 * c + 1)))

    return at


def spread(row):
    even_x = lax.broadcasted_iota(jnp.int32, row.shape, 0) % 2 == 0
    even_z = lax.broadcasted_iota(jnp.int32, row.shape, 1) % 2 == 0
    row = jnp.where(even_z, row, pltpu.roll(row, 1, 1))
    return jnp.where(even_x, row, pltpu.roll(row, 1, 0))


def quadrature(values, interval):
    def at(r):
        zero, one, two = (value(r) for value in values)
        w = WEIGHTS[interval]
        return tuple(w[0] * a + w[1] * b + w[2] * c for a, b, c in zip(zero, one, two))

    return at


def iteration(start, feed, kill, old_rates):
    feed_kill = functools.cache(lambda r: feed(r) + kill(r))
    coarse_feed = functools.cache(lambda c: half_sum(feed(2 * c), feed(2 * c + 1)))
    coarse_sum = functools.cache(lambda c: half_sum(feed_kill(2 * c), feed_kill(2 * c + 1)))

    def stepped(state, rate, interval):
        @functools.cache
        def at(r):
            out = [s + HALF_STEP * f for s, f in zip(state(r), rate(r))]
            if old_rates is not None:
                integral = quadrature(old_rates, interval)(r)
                old = old_rates[interval](r)
                out = [o + (q - HALF_STEP * f) for o, q, f in zip(out, integral, old)]
            return tuple(out)

        return at

    fine = lambda state: rates_of(state, feed, feed_kill, 1.0)
    coarse = lambda state: rates_of(state, coarse_feed, coarse_sum, 2.0)
    rate_zero = fine(start)
    node_one = stepped(start, rate_zero, 0)
    rate_one = fine(node_one)
    node_two = stepped(node_one, rate_one, 1)
    rate_two = fine(node_two)
    fresh = (rate_zero, rate_one, rate_two)
    rest_zero, rest_one, rest_two = restricted(start), restricted(node_one), restricted(node_two)
    rest_integral = [restricted(quadrature(fresh, interval)) for interval in (0, 1)]
    coarse_start = rest_zero

    def coarse_stepped(state, rate, rest_rate, integral):
        @functools.cache
        def at(c):
            return tuple(
                s + HALF_STEP * (f - g) + q for s, f, g, q in zip(state(c), rate(c), rest_rate(c), integral(c))
            )

        return at

    coarse_one = coarse_stepped(coarse_start, coarse(coarse_start), coarse(rest_zero), rest_integral[0])
    coarse_two = coarse_stepped(coarse_one, coarse(coarse_one), coarse(rest_one), rest_integral[1])

    def corrected(node, coarse_node, rest):
        change = functools.cache(lambda c: tuple(spread(w - m) for w, m in zip(coarse_node(c), rest(c))))

        @functools.cache
        def at(r):
            return tuple(n + d for n, d in zip(node(r), change(r // 2)))

        return at

    return rate_zero, corrected(node_one, coarse_one, rest_one), corrected(node_two, coarse_two, rest_two)


def rows_of(ref, width, first):
    @functools.cache
    def at(r):
        assert 0 <= (r - first) * width < ref.shape[1]
        return tuple(ref[field, pl.ds((r - first) * width, width), :] for field in range(2))

    return at


def pack_kernel(tiles_ref, state_ref, all_ref, low_ref, high_ref):
    n_fields, n_x, n_y, _ = tiles_ref.shape
    for field in range(n_fields):
        for x in range(n_x):
            all_ref[field, pl.ds(x, n_y, stride=n_x), :] = tiles_ref[field, x]
        low_ref[field] = all_ref[field, pl.ds(0, ABOVE * n_x), :]
        high_ref[field] = all_ref[field, pl.ds((n_y - BELOW) * n_x, BELOW * n_x), :]
    for field in range(2):
        state_ref[field] = all_ref[field]


def collect(out_ref, field, source_field, n_x, lowest, pieces):
    width = n_x * len(pieces[0][1])
    for first, refs, count in pieces:
        for gy, ref in enumerate(refs):
            for k in range(count):
                if first + k >= lowest:
                    place = pl.ds((first + k - lowest) * width + gy * n_x, n_x)
                    out_ref[field, place, :] = ref[source_field, pl.ds(k * n_x, n_x), :]


def first_kernel(n_gy, n_x, n_y, *refs):
    state_ref, local_ref = refs[:2]
    others, lows = refs[2 : 1 + n_gy], refs[1 + n_gy : 1 + 2 * n_gy]
    start_ref, params_ref, *outs = refs[1 + 2 * n_gy :]
    width = n_gy * n_x
    for field in range(2):
        collect(start_ref, field, field, n_x, -TAKE, [(-BELOW, lows, BELOW), (0, [state_ref, *others], n_y)])
        collect(params_ref, field, 2 + field, n_x, -TAKE, [(-BELOW, lows, BELOW), (0, [local_ref, *others], n_y)])
    start = rows_of(start_ref, width, -HALO)
    params = rows_of(params_ref, width, -HALO)
    results = iteration(start, lambda r: params(r)[0], lambda r: params(r)[1], None)
    write_nodes(results, width, n_y, [(0, TAKE)], *outs)


def write_nodes(results, width, n_y, edges, zero_ref, one_ref, two_ref, *edge_refs):
    rate_zero, node_one, node_two = results
    for r in range(-RATE_HALO, n_y + RATE_HALO):
        if 0 <= r < n_y:
            place = pl.ds(r * width, width)
            for field, (one, two) in enumerate(zip(node_one(r), node_two(r))):
                one_ref[field, place, :] = one
                two_ref[field, place, :] = two
                for i, (first, count) in enumerate(edges):
                    if first <= r < first + count:
                        beside = pl.ds((r - first) * width, width)
                        edge_refs[2 * i][field, beside, :] = two
                        edge_refs[2 * i + 1][field, beside, :] = one
                        edge_refs[2 * i + 1][2 + field, beside, :] = two
        for field, zero in enumerate(rate_zero(r)):
            zero_ref[field, pl.ds((r + RATE_HALO) * width, width), :] = zero


def joined(*parts):
    def at(r):
        return [rows for first, rows in parts if first <= r][-1](r)

    return at


def pair_of(ref, field):
    return ref.at[pl.ds(field, 2)]


def later_iteration(width, n_y, is_first, kept, params, got, old_zero, ones, twos):
    feed, kill = (lambda r: params(r)[0]), (lambda r: params(r)[1])
    feed_kill = functools.cache(lambda r: feed(r) + kill(r))

    @functools.cache
    def start(r):
        return tuple(jnp.where(is_first, a, b) for a, b in zip(kept(r), got(r)))

    old_rates = (
        old_zero(feed, feed_kill),
        rates_of(ones, feed, feed_kill, 1.0),
        rates_of(twos, feed, feed_kill, 1.0),
    )
    return iteration(start, feed, kill, old_rates)


def second_kernel(n_gy, n_x, n_y, first_ref, start_ref, params_ref, *refs):
    highs, refs = refs[:n_gy], refs[n_gy:]
    zero_ref, one_ref, two_ref, got_ref, got_edge, pair_edge, top_ref, *outs = refs
    width = n_gy * n_x
    for field in range(4):
        collect(top_ref, field, field, n_x, n_y, [(n_y, highs, ABOVE)])
    kept = joined((-TAKE, rows_of(start_ref, width, -TAKE)), (n_y, rows_of(pair_of(top_ref, 0), width, n_y)))
    params = joined((-TAKE, rows_of(params_ref, width, -TAKE)), (n_y, rows_of(pair_of(top_ref, 2), width, n_y)))
    end = n_y - DRIFT

    def moved(tile_ref, edge_ref):
        return joined((-DRIFT, rows_of(tile_ref, width, -DRIFT)), (end, rows_of(edge_ref, width, end)))

    def old_zero(feed, feed_kill):
        inside = rows_of(zero_ref, width, -RATE_HALO - DRIFT)
        return joined((-RATE_HALO - DRIFT, inside), (end + RATE_HALO, rates_of(kept, feed, feed_kill, 1.0)))

    ones, twos = moved(one_ref, pair_of(pair_edge, 0)), moved(two_ref, pair_of(pair_edge, 2))
    results = later_iteration(
        width, n_y, first_ref[0] == 1, kept, params, moved(got_ref, got_edge), old_zero, ones, twos
    )
    write_nodes(results, width, n_y, [(0, HALO), (n_y - HALO, HALO)], *outs)


def later_kernel(width, n_y, out_x, first_ref, start_ref, params_ref, top_ref, *refs):
    zero_ref, one_ref, two_ref, got_ref, got_low, got_high, pair_low, pair_high, *outs = refs
    kept = joined((-TAKE, rows_of(start_ref, width, -TAKE)), (n_y, rows_of(pair_of(top_ref, 0), width, n_y)))
    params = joined((-TAKE, rows_of(params_ref, width, -TAKE)), (n_y, rows_of(pair_of(top_ref, 2), width, n_y)))

    def window(low_ref, tile_ref, high_ref):
        refs = ((-HALO, low_ref), (0, tile_ref), (n_y, high_ref))
        return joined(*((first, rows_of(ref, width, first)) for first, ref in refs))

    ones = window(pair_of(pair_low, 0), one_ref, pair_of(pair_high, 0))
    twos = window(pair_of(pair_low, 2), two_ref, pair_of(pair_high, 2))
    old_zero = rows_of(zero_ref, width, -RATE_HALO)
    got = window(got_low, got_ref, got_high)
    results = later_iteration(
        width, n_y, first_ref[0] == 1, kept, params, got, lambda feed, feed_kill: old_zero, ones, twos
    )
    if out_x is None:
        write_nodes(results, width, n_y, [(0, HALO), (n_y - HALO, HALO)], *outs)
    else:
        out_ref, scratch = outs
        for r in range(n_y):
            for field, value in enumerate(results[2](r)):
                scratch[field, pl.ds(r * width, width), :] = value
        for x in range(out_x):
            for field in range(2):
                out_ref[field, x] = scratch[field, pl.ds(x, n_y, stride=width), :]


def call(kernel, name, n_scalars, operands, shapes, scratch=()):
    specs = [pl.BlockSpec(memory_space=pltpu.SMEM)] * n_scalars
    specs += [pl.BlockSpec(memory_space=pltpu.VMEM)] * (len(operands) - n_scalars)
    return pl.pallas_call(
        kernel,
        name=name,
        out_shape=[jax.ShapeDtypeStruct(shape, jnp.float32) for shape in shapes],
        in_specs=specs,
        out_specs=[pl.BlockSpec(memory_space=pltpu.VMEM)] * len(shapes),
        scratch_shapes=scratch,
        compiler_params=pltpu.CompilerParams(vmem_limit_bytes=32 * 1024 * 1024),
    )(*operands)


def shards(initial_state, slice_guess, feed_rate, kill_rate):
    n_gy, n_tm = lax.axis_size("gy"), lax.axis_size("tm")
    _, n_x, n_y, n_z = initial_state.shape
    width = n_gy * n_x
    place = lax.axis_index("tm")
    is_first = (place == 0).astype(jnp.int32)[None]

    sent = jnp.where(place == n_tm - 1, initial_state, slice_guess[0])
    state, local, low, high = call(
        pack_kernel,
        "pack",
        0,
        (jnp.concatenate([sent, feed_rate[None], kill_rate[None]]),),
        [(2, n_y * n_x, n_z), (4, n_y * n_x, n_z), (4, ABOVE * n_x, n_z), (4, BELOW * n_x, n_z)],
    )
    got = [shifted(state, 1, 0, 0), local]
    got += [shifted(local, 1, -gy, 0) for gy in range(1, n_gy)]
    got += [shifted(high, 1, -gy, 1) for gy in range(n_gy)]
    above = [shifted(low, 1, -gy, -1) for gy in range(n_gy)]

    tile, window = (2, n_y * width, n_z), (2, (TAKE + n_y) * width, n_z)
    nodes_only = [(2, (n_y + 2 * RATE_HALO) * width, n_z), tile, tile]
    edge = lambda rows: [(2, rows * width, n_z), (4, rows * width, n_z)]
    start, params, *nodes = call(
        functools.partial(first_kernel, n_gy, n_x, n_y),
        "first",
        0,
        got,
        [window, window, *nodes_only, *edge(TAKE)],
    )
    zero, one, two, two_edge, pair_edge = nodes
    got = [shifted(two, 1, 0, 0), shifted(two_edge, 1, 0, -1), shifted(pair_edge, 0, 0, -1)]
    top, *nodes = call(
        functools.partial(second_kernel, n_gy, n_x, n_y),
        "second",
        1,
        (is_first, start, params, *above, zero, one, two, *got),
        [(4, ABOVE * width, n_z), *nodes_only, *edge(HALO), *edge(HALO)],
    )
    for sweep_index in range(2, ITERS):
        zero, one, two, two_low, pair_low, two_high, pair_high = nodes
        got = [shifted(two, 1, 0, 0), shifted(two_high, 1, 0, 1), shifted(two_low, 1, 0, -1)]
        got += [shifted(pair_high, 0, 0, 1), shifted(pair_low, 0, 0, -1)]
        done = sweep_index + 1 == ITERS
        nodes = call(
            functools.partial(later_kernel, width, n_y, n_x if done else None),
            "last" if done else "later",
            1,
            (is_first, start, params, top, zero, one, two, *got),
            [initial_state.shape] if done else [*nodes_only, *edge(HALO), *edge(HALO)],
            [pltpu.VMEM(tile, jnp.float32)] if done else (),
        )
    return nodes[0][None]


def solution(mesh):
    in_specs = (
        P(None, "gy", "gx", None),
        P("tm", None, "gy", "gx", None),
        P("gy", "gx", None),
        P("gy", "gx", None),
    )
    out_specs = P("tm", None, "gy", "gx", None)
    return jax.shard_map(shards, mesh=mesh, in_specs=in_specs, out_specs=out_specs, check_vma=False)
```

```python
import functools

import jax
import jax.numpy as jnp
from jax import lax
from jax.experimental import pallas as pl
from jax.experimental.pallas import tpu as pltpu
from jax.sharding import PartitionSpec as P

ITERS = 3
DIFF_U = 0.2
DIFF_V = 0.1
HALF_STEP = 0.5
WEIGHTS = ((5.0 / 24.0, 8.0 / 24.0, -1.0 / 24.0), (-1.0 / 24.0, 8.0 / 24.0, 5.0 / 24.0))

AXES = ("tm", "gy", "gx")
HALO = 5
RATE_HALO = 4
DRIFT = 6
TAKE = HALO + DRIFT
BELOW = TAKE + 1


def shifted(value, by_tm, by_gy, by_gx):
    n_tm, n_gy, n_gx = (lax.axis_size(axis) for axis in AXES)
    pairs = []
    for t in range(n_tm):
        for y in range(n_gy):
            for x in range(n_gx):
                target = ((t + by_tm) % n_tm * n_gy + (y + by_gy) % n_gy) * n_gx + (x + by_gx) % n_gx
                pairs.append(((t * n_gy + y) * n_gx + x, target))
    return lax.ppermute(value, AXES, pairs)


def near(row, distance, axis):
    size = row.shape[axis]
    return pltpu.roll(row, distance % size, axis) + pltpu.roll(row, -distance % size, axis)


def rates_of(state, feed, feed_kill, spacing):
    scale = 1.0 / (spacing * spacing)

    @functools.cache
    def at(r):
        (u, v), (ub, vb), (ua, va) = state(r), state(r - 1), state(r + 1)
        around_u = (ub + ua) + near(u, int(spacing), 0) + near(u, int(spacing), 1)
        around_v = (vb + va) + near(v, int(spacing), 0) + near(v, int(spacing), 1)
        reaction = u * (v * v)
        rate_u = (DIFF_U * scale) * around_u + feed(r) - (6.0 * DIFF_U * scale + feed(r)) * u - reaction
        rate_v = (DIFF_V * scale) * around_v - (6.0 * DIFF_V * scale + feed_kill(r)) * v + reaction
        return rate_u, rate_v

    return at


def half_sum(low, high):
    x, z = low.shape
    total = low + high
    total = total + pltpu.roll(total, z - 1, 1)
    total = total + pltpu.roll(total, x - 1, 0)
    return 0.125 * total


def restricted(state):
    @functools.cache
    def at(c):
        return tuple(half_sum(a, b) for a, b in zip(state(2 * c), state(2 * c + 1)))

    return at


def spread(row):
    even_x = lax.broadcasted_iota(jnp.int32, row.shape, 0) % 2 == 0
    even_z = lax.broadcasted_iota(jnp.int32, row.shape, 1) % 2 == 0
    row = jnp.where(even_z, row, pltpu.roll(row, 1, 1))
    return jnp.where(even_x, row, pltpu.roll(row, 1, 0))


def quadrature(values, interval):
    def at(r):
        zero, one, two = (value(r) for value in values)
        w = WEIGHTS[interval]
        return tuple(w[0] * a + w[1] * b + w[2] * c for a, b, c in zip(zero, one, two))

    return at


def iteration(start, feed, kill, old_rates):
    feed_kill = functools.cache(lambda r: feed(r) + kill(r))
    coarse_feed = functools.cache(lambda c: half_sum(feed(2 * c), feed(2 * c + 1)))
    coarse_sum = functools.cache(lambda c: half_sum(feed_kill(2 * c), feed_kill(2 * c + 1)))

    def stepped(state, rate, interval):
        @functools.cache
        def at(r):
            out = [s + HALF_STEP * f for s, f in zip(state(r), rate(r))]
            if old_rates is not None:
                integral = quadrature(old_rates, interval)(r)
                old = old_rates[interval](r)
                out = [o + (q - HALF_STEP * f) for o, q, f in zip(out, integral, old)]
            return tuple(out)

        return at

    fine = lambda state: rates_of(state, feed, feed_kill, 1.0)
    coarse = lambda state: rates_of(state, coarse_feed, coarse_sum, 2.0)
    rate_zero = fine(start)
    node_one = stepped(start, rate_zero, 0)
    rate_one = fine(node_one)
    node_two = stepped(node_one, rate_one, 1)
    rate_two = fine(node_two)
    fresh = (rate_zero, rate_one, rate_two)
    rest_zero, rest_one, rest_two = restricted(start), restricted(node_one), restricted(node_two)
    rest_integral = [restricted(quadrature(fresh, interval)) for interval in (0, 1)]
    coarse_start = rest_zero

    def coarse_stepped(state, rate, rest_rate, integral):
        @functools.cache
        def at(c):
            return tuple(
                s + HALF_STEP * (f - g) + q for s, f, g, q in zip(state(c), rate(c), rest_rate(c), integral(c))
            )

        return at

    coarse_one = coarse_stepped(coarse_start, coarse(coarse_start), coarse(rest_zero), rest_integral[0])
    coarse_two = coarse_stepped(coarse_one, coarse(coarse_one), coarse(rest_one), rest_integral[1])

    def corrected(node, coarse_node, rest):
        change = functools.cache(lambda c: tuple(spread(w - m) for w, m in zip(coarse_node(c), rest(c))))

        @functools.cache
        def at(r):
            return tuple(n + d for n, d in zip(node(r), change(r // 2)))

        return at

    return rate_zero, corrected(node_one, coarse_one, rest_one), corrected(node_two, coarse_two, rest_two)


def rows_of(ref, width, first):
    @functools.cache
    def at(r):
        assert 0 <= (r - first) * width < ref.shape[1]
        return tuple(ref[field, pl.ds((r - first) * width, width), :] for field in range(2))

    return at


def pack_kernel(tiles_ref, state_ref, all_ref, high_ref):
    n_fields, n_x, n_y, _ = tiles_ref.shape
    for field in range(n_fields):
        for x in range(n_x):
            all_ref[field, pl.ds(x, n_y, stride=n_x), :] = tiles_ref[field, x]
        high_ref[field] = all_ref[field, pl.ds((n_y - BELOW) * n_x, BELOW * n_x), :]
    for field in range(2):
        state_ref[field] = all_ref[field]


def collect(out_ref, field, source_field, n_x, lowest, pieces):
    width = n_x * len(pieces[0][1])
    for first, refs, count in pieces:
        for gy, ref in enumerate(refs):
            for k in range(count):
                if first + k >= lowest:
                    place = pl.ds((first + k - lowest) * width + gy * n_x, n_x)
                    out_ref[field, place, :] = ref[source_field, pl.ds(k * n_x, n_x), :]


def first_kernel(n_gy, n_x, n_y, *refs):
    state_ref, local_ref = refs[:2]
    others, lows = refs[2 : 1 + n_gy], refs[1 + n_gy : 1 + 2 * n_gy]
    start_ref, params_ref, *outs = refs[1 + 2 * n_gy :]
    width = n_gy * n_x
    for field in range(2):
        collect(start_ref, field, field, n_x, -TAKE, [(-BELOW, lows, BELOW), (0, [state_ref, *others], n_y)])
        collect(params_ref, field, 2 + field, n_x, -TAKE, [(-BELOW, lows, BELOW), (0, [local_ref, *others], n_y)])
    start = rows_of(start_ref, width, -HALO)
    params = rows_of(params_ref, width, -HALO)
    results = iteration(start, lambda r: params(r)[0], lambda r: params(r)[1], None)
    write_nodes(results, width, n_y, [(0, TAKE)], *outs)
    for r in range(HALO):
        for field, value in enumerate((*start(r + DRIFT), *params(r + DRIFT))):
            outs[-1][pl.ds((4 * TAKE + field * HALO + r) * width, width), :] = value


def write_nodes(results, width, n_y, edges, zero_ref, one_ref, two_ref, *edge_refs):
    rate_zero, node_one, node_two = results
    for r in range(-RATE_HALO, n_y + RATE_HALO):
        if 0 <= r < n_y:
            place = pl.ds(r * width, width)
            for field, (one, two) in enumerate(zip(node_one(r), node_two(r))):
                one_ref[field, place, :] = one
                two_ref[field, place, :] = two
                for i, (first, count) in enumerate(edges):
                    if first <= r < first + count:
                        beside = pl.ds((r - first) * width, width)
                        edge_refs[2 * i][field, beside, :] = two
                        for at, value in ((field, one), (2 + field, two)):
                            edge_refs[2 * i + 1][pl.ds((at * count + r - first) * width, width), :] = value
        for field, zero in enumerate(rate_zero(r)):
            zero_ref[field, pl.ds((r + RATE_HALO) * width, width), :] = zero


def joined(*parts):
    def at(r):
        return [rows for first, rows in parts if first <= r][-1](r)

    return at


def flat_rows(ref, width, place, first, count):
    @functools.cache
    def at(r):
        assert 0 <= r - first < count
        return tuple(ref[pl.ds((place + field * count + r - first) * width, width), :] for field in range(2))

    return at


def known(width, n_y, start_ref, params_ref, edge_ref):
    return (
        joined(
            (-TAKE, rows_of(ref, width, -TAKE)), (n_y, flat_rows(edge_ref, width, 4 * TAKE + place * HALO, n_y, HALO))
        )
        for ref, place in ((start_ref, 0), (params_ref, 2))
    )


def later_iteration(width, n_y, is_first, kept, params, got, old_zero, ones, twos):
    feed, kill = (lambda r: params(r)[0]), (lambda r: params(r)[1])
    feed_kill = functools.cache(lambda r: feed(r) + kill(r))

    @functools.cache
    def start(r):
        return tuple(jnp.where(is_first, a, b) for a, b in zip(kept(r), got(r)))

    old_rates = (
        old_zero(feed, feed_kill),
        rates_of(ones, feed, feed_kill, 1.0),
        rates_of(twos, feed, feed_kill, 1.0),
    )
    return iteration(start, feed, kill, old_rates)


def second_kernel(width, n_y, first_ref, start_ref, params_ref, *refs):
    zero_ref, one_ref, two_ref, got_ref, got_edge, pair_edge, *outs = refs
    kept, params = known(width, n_y, start_ref, params_ref, pair_edge)
    end = n_y - DRIFT

    def moved(tile_ref, beside):
        return joined((-DRIFT, rows_of(tile_ref, width, -DRIFT)), (end, beside))

    def pair(place):
        return flat_rows(pair_edge, width, place * TAKE, end, TAKE)

    def old_zero(feed, feed_kill):
        inside = rows_of(zero_ref, width, -RATE_HALO - DRIFT)
        return joined((-RATE_HALO - DRIFT, inside), (end + RATE_HALO, rates_of(kept, feed, feed_kill, 1.0)))

    ones, twos = moved(one_ref, pair(0)), moved(two_ref, pair(2))
    got = moved(got_ref, rows_of(got_edge, width, end))
    results = later_iteration(width, n_y, first_ref[0] == 1, kept, params, got, old_zero, ones, twos)
    write_nodes(results, width, n_y, [(0, HALO), (n_y - HALO, HALO)], *outs)


def later_kernel(width, n_y, out_x, first_ref, start_ref, params_ref, known_ref, *refs):
    zero_ref, one_ref, two_ref, got_ref, got_low, got_high, pair_low, pair_high, *outs = refs
    kept, params = known(width, n_y, start_ref, params_ref, known_ref)

    def window(low, tile_ref, high):
        return joined((-HALO, low), (0, rows_of(tile_ref, width, 0)), (n_y, high))

    def pair(tile_ref, place):
        low, high = (
            flat_rows(ref, width, place * HALO, first, HALO) for ref, first in ((pair_low, -HALO), (pair_high, n_y))
        )
        return window(low, tile_ref, high)

    ones, twos = pair(one_ref, 0), pair(two_ref, 2)
    old_zero = rows_of(zero_ref, width, -RATE_HALO)
    got = window(rows_of(got_low, width, -HALO), got_ref, rows_of(got_high, width, n_y))
    results = later_iteration(
        width, n_y, first_ref[0] == 1, kept, params, got, lambda feed, feed_kill: old_zero, ones, twos
    )
    if out_x is None:
        write_nodes(results, width, n_y, [(0, HALO), (n_y - HALO, HALO)], *outs)
    else:
        out_ref, scratch = outs
        for r in range(n_y):
            for field, value in enumerate(results[2](r)):
                scratch[field, pl.ds(r * width, width), :] = value
        for x in range(out_x):
            for field in range(2):
                out_ref[field, x] = scratch[field, pl.ds(x, n_y, stride=width), :]


def call(kernel, name, n_scalars, operands, shapes, scratch=()):
    specs = [pl.BlockSpec(memory_space=pltpu.SMEM)] * n_scalars
    specs += [pl.BlockSpec(memory_space=pltpu.VMEM)] * (len(operands) - n_scalars)
    return pl.pallas_call(
        kernel,
        name=name,
        out_shape=[jax.ShapeDtypeStruct(shape, jnp.float32) for shape in shapes],
        in_specs=specs,
        out_specs=[pl.BlockSpec(memory_space=pltpu.VMEM)] * len(shapes),
        scratch_shapes=scratch,
        compiler_params=pltpu.CompilerParams(vmem_limit_bytes=32 * 1024 * 1024),
    )(*operands)


def shards(initial_state, slice_guess, feed_rate, kill_rate):
    n_gy, n_tm = lax.axis_size("gy"), lax.axis_size("tm")
    _, n_x, n_y, n_z = initial_state.shape
    width = n_gy * n_x
    place = lax.axis_index("tm")
    is_first = (place == 0).astype(jnp.int32)[None]

    sent = jnp.where(place == n_tm - 1, initial_state, slice_guess[0])
    state, local, high = call(
        pack_kernel,
        "pack",
        0,
        (jnp.concatenate([sent, feed_rate[None], kill_rate[None]]),),
        [(2, n_y * n_x, n_z), (4, n_y * n_x, n_z), (4, BELOW * n_x, n_z)],
    )
    got = [shifted(state, 1, 0, 0), local]
    got += [shifted(local, 1, -gy, 0) for gy in range(1, n_gy)]
    got += [shifted(high, 1, -gy, 1) for gy in range(n_gy)]

    tile, window = (2, n_y * width, n_z), (2, (TAKE + n_y) * width, n_z)
    nodes_only = [(2, (n_y + 2 * RATE_HALO) * width, n_z), tile, tile]
    edge = lambda rows, more=0: [(2, rows * width, n_z), ((4 * rows + more) * width, n_z)]
    start, params, *nodes = call(
        functools.partial(first_kernel, n_gy, n_x, n_y),
        "first",
        0,
        got,
        [window, window, *nodes_only, *edge(TAKE, 4 * HALO)],
    )
    zero, one, two, two_edge, pair_edge = nodes
    got = [shifted(two, 1, 0, 0), shifted(two_edge, 1, 0, -1), shifted(pair_edge, 0, 0, -1)]
    known_edge = got[-1]
    nodes = call(
        functools.partial(second_kernel, width, n_y),
        "second",
        1,
        (is_first, start, params, zero, one, two, *got),
        [*nodes_only, *edge(HALO), *edge(HALO)],
    )
    for sweep_index in range(2, ITERS):
        zero, one, two, two_low, pair_low, two_high, pair_high = nodes
        got = [shifted(two, 1, 0, 0), shifted(two_high, 1, 0, 1), shifted(two_low, 1, 0, -1)]
        got += [shifted(pair_high, 0, 0, 1), shifted(pair_low, 0, 0, -1)]
        done = sweep_index + 1 == ITERS
        nodes = call(
            functools.partial(later_kernel, width, n_y, n_x if done else None),
            "last" if done else "later",
            1,
            (is_first, start, params, known_edge, zero, one, two, *got),
            [initial_state.shape] if done else [*nodes_only, *edge(HALO), *edge(HALO)],
            [pltpu.VMEM(tile, jnp.float32)] if done else (),
        )
    return nodes[0][None]


def solution(mesh):
    in_specs = (
        P(None, "gy", "gx", None),
        P("tm", None, "gy", "gx", None),
        P("gy", "gx", None),
        P("gy", "gx", None),
    )
    out_specs = P("tm", None, "gy", "gx", None)
    return jax.shard_map(shards, mesh=mesh, in_specs=in_specs, out_specs=out_specs, check_vma=False)
```

```python
import functools

import jax
import jax.numpy as jnp
from jax import lax
from jax.experimental import pallas as pl
from jax.experimental.pallas import tpu as pltpu
from jax.sharding import PartitionSpec as P

DIFF_U = 0.2
DIFF_V = 0.1
HALF_STEP = 0.5
WEIGHTS = ((5.0 / 24.0, 8.0 / 24.0, -1.0 / 24.0), (-1.0 / 24.0, 8.0 / 24.0, 5.0 / 24.0))

AXES = ("tm", "gy", "gx")
HALO = 5
RATE_HALO = 4
LOW, DROP, SHIFT = 9, 6, 4
BELOW = 16


def shifted(value, by_tm, by_gy, by_gx):
    n_tm, n_gy, n_gx = (lax.axis_size(axis) for axis in AXES)
    pairs = []
    for t in range(n_tm):
        for y in range(n_gy):
            for x in range(n_gx):
                target = ((t + by_tm) % n_tm * n_gy + (y + by_gy) % n_gy) * n_gx + (x + by_gx) % n_gx
                pairs.append(((t * n_gy + y) * n_gx + x, target))
    return lax.ppermute(value, AXES, pairs)


def near(row, distance, axis):
    size = row.shape[axis]
    return pltpu.roll(row, distance % size, axis) + pltpu.roll(row, -distance % size, axis)


def rates_of(state, feed, feed_kill, spacing):
    scale = 1.0 / (spacing * spacing)

    @functools.cache
    def at(r):
        (u, v), (ub, vb), (ua, va) = state(r), state(r - 1), state(r + 1)
        around_u = (ub + ua) + near(u, int(spacing), 0) + near(u, int(spacing), 1)
        around_v = (vb + va) + near(v, int(spacing), 0) + near(v, int(spacing), 1)
        reaction = u * (v * v)
        rate_u = (DIFF_U * scale) * around_u + feed(r) - (6.0 * DIFF_U * scale + feed(r)) * u - reaction
        rate_v = (DIFF_V * scale) * around_v - (6.0 * DIFF_V * scale + feed_kill(r)) * v + reaction
        return rate_u, rate_v

    return at


def half_sum(low, high):
    x, z = low.shape
    total = low + high
    total = total + pltpu.roll(total, z - 1, 1)
    total = total + pltpu.roll(total, x - 1, 0)
    return 0.125 * total


def restricted(state):
    @functools.cache
    def at(c):
        return tuple(half_sum(a, b) for a, b in zip(state(2 * c), state(2 * c + 1)))

    return at


def spread(row):
    even_x = lax.broadcasted_iota(jnp.int32, row.shape, 0) % 2 == 0
    even_z = lax.broadcasted_iota(jnp.int32, row.shape, 1) % 2 == 0
    row = jnp.where(even_z, row, pltpu.roll(row, 1, 1))
    return jnp.where(even_x, row, pltpu.roll(row, 1, 0))


def quadrature(values, interval):
    def at(r):
        zero, one, two = (value(r) for value in values)
        w = WEIGHTS[interval]
        return tuple(w[0] * a + w[1] * b + w[2] * c for a, b, c in zip(zero, one, two))

    return at


def iteration(start, feed, kill, old_rates):
    feed_kill = functools.cache(lambda r: feed(r) + kill(r))
    coarse_feed = functools.cache(lambda c: half_sum(feed(2 * c), feed(2 * c + 1)))
    coarse_sum = functools.cache(lambda c: half_sum(feed_kill(2 * c), feed_kill(2 * c + 1)))

    def stepped(state, rate, interval):
        @functools.cache
        def at(r):
            out = [s + HALF_STEP * f for s, f in zip(state(r), rate(r))]
            if old_rates is not None:
                integral = quadrature(old_rates, interval)(r)
                old = old_rates[interval](r)
                out = [o + (q - HALF_STEP * f) for o, q, f in zip(out, integral, old)]
            return tuple(out)

        return at

    fine = lambda state: rates_of(state, feed, feed_kill, 1.0)
    coarse = lambda state: rates_of(state, coarse_feed, coarse_sum, 2.0)
    rate_zero = fine(start)
    node_one = stepped(start, rate_zero, 0)
    rate_one = fine(node_one)
    node_two = stepped(node_one, rate_one, 1)
    rate_two = fine(node_two)
    fresh = (rate_zero, rate_one, rate_two)
    rest_zero, rest_one, rest_two = restricted(start), restricted(node_one), restricted(node_two)
    rest_integral = [restricted(quadrature(fresh, interval)) for interval in (0, 1)]
    coarse_start = rest_zero

    def coarse_stepped(state, rate, rest_rate, integral):
        @functools.cache
        def at(c):
            return tuple(
                s + HALF_STEP * (f - g) + q for s, f, g, q in zip(state(c), rate(c), rest_rate(c), integral(c))
            )

        return at

    coarse_one = coarse_stepped(coarse_start, coarse(coarse_start), coarse(rest_zero), rest_integral[0])
    coarse_two = coarse_stepped(coarse_one, coarse(coarse_one), coarse(rest_one), rest_integral[1])

    def corrected(node, coarse_node, rest):
        change = functools.cache(lambda c: tuple(spread(w - m) for w, m in zip(coarse_node(c), rest(c))))

        @functools.cache
        def at(r):
            return tuple(n + d for n, d in zip(node(r), change(r // 2)))

        return at

    return rate_zero, corrected(node_one, coarse_one, rest_one), corrected(node_two, coarse_two, rest_two)


def rows_of(ref, width, first):
    @functools.cache
    def at(r):
        assert 0 <= (r - first) * width < ref.shape[1]
        return tuple(ref[field, pl.ds((r - first) * width, width), :] for field in range(2))

    return at


def pack_kernel(tiles_ref, state_ref, all_ref, high_ref):
    n_fields, n_x, n_y, _ = tiles_ref.shape
    for field in range(n_fields):
        for x in range(n_x):
            all_ref[field, pl.ds(x, n_y, stride=n_x), :] = tiles_ref[field, x]
        high_ref[field] = all_ref[field, pl.ds((n_y - BELOW) * n_x, BELOW * n_x), :]
    for field in range(2):
        state_ref[field] = all_ref[field]


def collect(out_ref, field, source_field, n_x, lowest, pieces):
    width = n_x * len(pieces[0][1])
    for first, refs, count in pieces:
        for gy, ref in enumerate(refs):
            for k in range(count):
                if first + k >= lowest:
                    place = pl.ds((first + k - lowest) * width + gy * n_x, n_x)
                    out_ref[field, place, :] = ref[source_field, pl.ds(k * n_x, n_x), :]


def emit(width, sinks):
    for r in range(min(sink[0] for sink in sinks), max(sink[1] for sink in sinks)):
        for low, high, values, ref, place in sinks:
            if low <= r < high:
                for field, value in enumerate(values(r)):
                    if place is None:
                        ref[field, pl.ds((r - low) * width, width), :] = value
                    else:
                        ref[pl.ds((place + field * (high - low) + r - low) * width, width), :] = value


def first_kernel(n_gy, n_x, n_y, *refs):
    state_ref, local_ref = refs[:2]
    others, lows = refs[2 : 1 + n_gy], refs[1 + n_gy : 1 + 2 * n_gy]
    start_ref, params_ref, zero_ref, one_ref, two_ref, two_edge, pair_edge = refs[1 + 2 * n_gy :]
    width = n_gy * n_x
    for field in range(2):
        collect(start_ref, field, field, n_x, -BELOW, [(-BELOW, lows, BELOW), (0, [state_ref, *others], n_y)])
        collect(params_ref, field, 2 + field, n_x, -BELOW, [(-BELOW, lows, BELOW), (0, [local_ref, *others], n_y)])
    start = rows_of(start_ref, width, -BELOW)
    params = rows_of(params_ref, width, -BELOW)
    zero, one, two = iteration(start, lambda r: params(r)[0], lambda r: params(r)[1], None)
    high = n_y - DROP
    edge = (-DROP, HALO - SHIFT)
    count = edge[1] - edge[0]
    emit(
        width,
        [
            (-SHIFT - RATE_HALO, n_y - 1, zero, zero_ref, None),
            (-LOW, high, one, one_ref, None),
            (-LOW, high, two, two_ref, None),
            (*edge, two, two_edge, None),
            (*edge, one, pair_edge, 0),
            (*edge, two, pair_edge, 2 * count),
            (0, edge[1], start, pair_edge, 4 * count),
        ],
    )


def joined(*parts):
    def at(r):
        return [rows for first, rows in parts if first <= r][-1](r)

    return at


def flat_rows(ref, width, place, first, count):
    @functools.cache
    def at(r):
        assert 0 <= r - first < count
        return tuple(ref[pl.ds((place + field * count + r - first) * width, width), :] for field in range(2))

    return at


def later_iteration(is_first, kept, params, got, old_zero, ones, twos):
    feed, kill = (lambda r: params(r)[0]), (lambda r: params(r)[1])
    feed_kill = functools.cache(lambda r: feed(r) + kill(r))

    @functools.cache
    def start(r):
        return tuple(jnp.where(is_first, a, b) for a, b in zip(kept(r), got(r)))

    old_rates = (
        old_zero(feed, feed_kill),
        rates_of(ones, feed, feed_kill, 1.0),
        rates_of(twos, feed, feed_kill, 1.0),
    )
    return start, iteration(start, feed, kill, old_rates)


def second_kernel(width, n_y, first_ref, start_ref, params_ref, *refs):
    zero_ref, one_ref, two_ref, got_ref, got_edge, pair_edge, *outs = refs
    high = n_y - DROP
    top = n_y - SHIFT + HALO
    count = top - high
    kept = joined(
        (-BELOW, rows_of(start_ref, width, -BELOW)), (n_y, flat_rows(pair_edge, width, 4 * count, n_y, top - n_y))
    )
    params = rows_of(params_ref, width, -BELOW)

    def moved(tile_ref, beside):
        return joined((-LOW, rows_of(tile_ref, width, -LOW)), (high, beside))

    def old_zero(feed, feed_kill):
        inside = rows_of(zero_ref, width, -SHIFT - RATE_HALO)
        return joined((-SHIFT - RATE_HALO, inside), (n_y - 1, rates_of(kept, feed, feed_kill, 1.0)))

    ones = moved(one_ref, flat_rows(pair_edge, width, 0, high, count))
    twos = moved(two_ref, flat_rows(pair_edge, width, 2 * count, high, count))
    got = moved(got_ref, rows_of(got_edge, width, high))
    start, (zero, one, two) = later_iteration(first_ref[0] == 1, kept, params, got, old_zero, ones, twos)
    zero_ref, one_ref, two_ref, two_up, pair_up, two_down, pair_down = outs
    up, down = (-SHIFT, HALO), (n_y - HALO, n_y - SHIFT)
    count = up[1] - up[0]
    emit(
        width,
        [
            (-RATE_HALO, n_y, zero, zero_ref, None),
            (-SHIFT, n_y - SHIFT, one, one_ref, None),
            (-SHIFT, n_y - SHIFT, two, two_ref, None),
            (*up, two, two_up, None),
            (*up, one, pair_up, 0),
            (*up, two, pair_up, 2 * count),
            (-1, HALO, start, pair_up, 4 * count),
            (-1, HALO, params, pair_up, 4 * count + 2 * (HALO + 1)),
            (*down, two, two_down, None),
            (*down, one, pair_down, 0),
            (*down, two, pair_down, 2 * (down[1] - down[0])),
        ],
    )


def third_kernel(width, n_y, out_x, first_ref, start_ref, params_ref, *refs):
    zero_ref, one_ref, two_ref, got_ref, got_high, got_low, pair_high, pair_low, out_ref, scratch = refs
    high = n_y - SHIFT
    count, under = n_y + HALO - high, HALO - SHIFT
    last_start, last_params = (
        flat_rows(pair_high, width, 4 * count + place * (HALO + 1), n_y - 1, HALO + 1) for place in (0, 2)
    )
    kept = joined((-BELOW, rows_of(start_ref, width, -BELOW)), (n_y, last_start))
    params = joined((-BELOW, rows_of(params_ref, width, -BELOW)), (n_y, last_params))

    def window(low, tile_ref, beside):
        return joined((-HALO, low), (-SHIFT, rows_of(tile_ref, width, -SHIFT)), (high, beside))

    def pair(tile_ref, place):
        low = flat_rows(pair_low, width, place * under, -HALO, under)
        return window(low, tile_ref, flat_rows(pair_high, width, place * count, high, count))

    def old_zero(feed, feed_kill):
        inside = rows_of(zero_ref, width, -RATE_HALO)
        return joined((-RATE_HALO, inside), (n_y, rates_of(last_start, feed, feed_kill, 1.0)))

    got = window(rows_of(got_low, width, -HALO), got_ref, rows_of(got_high, width, high))
    _, (_, _, two) = later_iteration(
        first_ref[0] == 1, kept, params, got, old_zero, pair(one_ref, 0), pair(two_ref, 2)
    )
    emit(width, [(0, n_y, two, scratch, None)])
    for x in range(out_x):
        for field in range(2):
            out_ref[field, x] = scratch[field, pl.ds(x, n_y, stride=width), :]


def call(kernel, name, n_scalars, operands, shapes, scratch=()):
    specs = [pl.BlockSpec(memory_space=pltpu.SMEM)] * n_scalars
    specs += [pl.BlockSpec(memory_space=pltpu.VMEM)] * (len(operands) - n_scalars)
    return pl.pallas_call(
        kernel,
        name=name,
        out_shape=[jax.ShapeDtypeStruct(shape, jnp.float32) for shape in shapes],
        in_specs=specs,
        out_specs=[pl.BlockSpec(memory_space=pltpu.VMEM)] * len(shapes),
        scratch_shapes=scratch,
        compiler_params=pltpu.CompilerParams(vmem_limit_bytes=32 * 1024 * 1024),
    )(*operands)


def shards(initial_state, slice_guess, feed_rate, kill_rate):
    n_gy, n_tm = lax.axis_size("gy"), lax.axis_size("tm")
    _, n_x, n_y, n_z = initial_state.shape
    width = n_gy * n_x
    place = lax.axis_index("tm")
    is_first = (place == 0).astype(jnp.int32)[None]

    sent = jnp.where(place == n_tm - 1, initial_state, slice_guess[0])
    state, local, high = call(
        pack_kernel,
        "pack",
        0,
        (jnp.concatenate([sent, feed_rate[None], kill_rate[None]]),),
        [(2, n_y * n_x, n_z), (4, n_y * n_x, n_z), (4, BELOW * n_x, n_z)],
    )
    got = [shifted(state, 1, 0, 0), local]
    got += [shifted(local, 1, -gy, 0) for gy in range(1, n_gy)]
    got += [shifted(high, 1, -gy, 1) for gy in range(n_gy)]

    rows = lambda count: (2, count * width, n_z)
    flat = lambda count: (count * width, n_z)
    window, nodes = rows(BELOW + n_y), rows(LOW + n_y - DROP)
    count = DROP + HALO - SHIFT
    start, params, *nodes, two_edge, pair_edge = call(
        functools.partial(first_kernel, n_gy, n_x, n_y),
        "first",
        0,
        got,
        [
            *(window, window, rows(SHIFT + RATE_HALO + n_y - 1), nodes, nodes),
            *(rows(count), flat(4 * count + 2 * (HALO - SHIFT))),
        ],
    )
    got = [shifted(nodes[2], 1, 0, 0), shifted(two_edge, 1, 0, -1), shifted(pair_edge, 0, 0, -1)]
    count, under = SHIFT + HALO, HALO - SHIFT
    *nodes, two_up, pair_up, two_down, pair_down = call(
        functools.partial(second_kernel, width, n_y),
        "second",
        1,
        (is_first, start, params, *nodes, *got),
        [
            *(rows(RATE_HALO + n_y), rows(n_y), rows(n_y)),
            *(rows(count), flat(4 * count + 4 * (HALO + 1)), rows(under), flat(4 * under)),
        ],
    )
    got = [shifted(nodes[2], 1, 0, 0), shifted(two_up, 1, 0, -1), shifted(two_down, 1, 0, 1)]
    got += [shifted(pair_up, 0, 0, -1), shifted(pair_down, 0, 0, 1)]
    (final,) = call(
        functools.partial(third_kernel, width, n_y, n_x),
        "third",
        1,
        (is_first, start, params, *nodes, *got),
        [initial_state.shape],
        [pltpu.VMEM(rows(n_y), jnp.float32)],
    )
    return final[None]


def solution(mesh):
    in_specs = (
        P(None, "gy", "gx", None),
        P("tm", None, "gy", "gx", None),
        P("gy", "gx", None),
        P("gy", "gx", None),
    )
    out_specs = P("tm", None, "gy", "gx", None)
    return jax.shard_map(shards, mesh=mesh, in_specs=in_specs, out_specs=out_specs, check_vma=False)
```

```python
import functools

import jax
import jax.numpy as jnp
from jax import lax
from jax.experimental import pallas as pl
from jax.experimental.pallas import tpu as pltpu
from jax.sharding import PartitionSpec as P

ITERS = 3
DIFF_U = 0.2
DIFF_V = 0.1
HALF_STEP = 0.5
WEIGHTS = ((5.0 / 24.0, 8.0 / 24.0, -1.0 / 24.0), (-1.0 / 24.0, 8.0 / 24.0, 5.0 / 24.0))

AXES = ("tm", "gy", "gx")
HALO = 5
RATE_HALO = 4
DRIFT = 6
TAKE = HALO + DRIFT
BELOW = TAKE + 1


def shifted(value, by_tm, by_gy, by_gx):
    n_tm, n_gy, n_gx = (lax.axis_size(axis) for axis in AXES)
    pairs = []
    for t in range(n_tm):
        for y in range(n_gy):
            for x in range(n_gx):
                target = ((t + by_tm) % n_tm * n_gy + (y + by_gy) % n_gy) * n_gx + (x + by_gx) % n_gx
                pairs.append(((t * n_gy + y) * n_gx + x, target))
    return lax.ppermute(value, AXES, pairs)


def near(row, distance, axis):
    size = row.shape[axis]
    return pltpu.roll(row, distance % size, axis) + pltpu.roll(row, -distance % size, axis)


def rates_of(state, feed, feed_kill, spacing):
    scale = 1.0 / (spacing * spacing)

    @functools.cache
    def at(r):
        (u, v), (ub, vb), (ua, va) = state(r), state(r - 1), state(r + 1)
        around_u = (ub + ua) + near(u, int(spacing), 0) + near(u, int(spacing), 1)
        around_v = (vb + va) + near(v, int(spacing), 0) + near(v, int(spacing), 1)
        reaction = u * (v * v)
        rate_u = (DIFF_U * scale) * around_u + feed(r) - (6.0 * DIFF_U * scale + feed(r)) * u - reaction
        rate_v = (DIFF_V * scale) * around_v - (6.0 * DIFF_V * scale + feed_kill(r)) * v + reaction
        return rate_u, rate_v

    return at


def half_sum(low, high):
    x, z = low.shape
    total = low + high
    total = total + pltpu.roll(total, z - 1, 1)
    total = total + pltpu.roll(total, x - 1, 0)
    return 0.125 * total


def restricted(state):
    @functools.cache
    def at(c):
        return tuple(half_sum(a, b) for a, b in zip(state(2 * c), state(2 * c + 1)))

    return at


def spread(row):
    even_x = lax.broadcasted_iota(jnp.int32, row.shape, 0) % 2 == 0
    even_z = lax.broadcasted_iota(jnp.int32, row.shape, 1) % 2 == 0
    row = jnp.where(even_z, row, pltpu.roll(row, 1, 1))
    return jnp.where(even_x, row, pltpu.roll(row, 1, 0))


def quadrature(values, interval):
    def at(r):
        zero, one, two = (value(r) for value in values)
        w = WEIGHTS[interval]
        return tuple(w[0] * a + w[1] * b + w[2] * c for a, b, c in zip(zero, one, two))

    return at


def inner_rows(n_y, tile_first):
    low, high = max(tile_first + 1, -RATE_HALO), tile_first + n_y - 1
    return [(low + k, high - k) for k in (0, 0, 1, 1, 2)]


def iteration(start, feed, kill, old_rates, inner=()):
    inner = iter(inner)

    def known_or(values):
        low, high, known = next(inner, (0, 0, None))
        return lambda r: (known if low <= r < high else values)(r)

    feed_kill = functools.cache(lambda r: feed(r) + kill(r))
    coarse_feed = functools.cache(lambda c: half_sum(feed(2 * c), feed(2 * c + 1)))
    coarse_sum = functools.cache(lambda c: half_sum(feed_kill(2 * c), feed_kill(2 * c + 1)))

    def stepped(state, rate, interval):
        @functools.cache
        def at(r):
            out = [s + HALF_STEP * f for s, f in zip(state(r), rate(r))]
            if old_rates is not None:
                integral = quadrature(old_rates, interval)(r)
                old = old_rates[interval](r)
                out = [o + (q - HALF_STEP * f) for o, q, f in zip(out, integral, old)]
            return tuple(out)

        return at

    fine = lambda state: rates_of(state, feed, feed_kill, 1.0)
    coarse = lambda state: rates_of(state, coarse_feed, coarse_sum, 2.0)
    rate_zero = known_or(fine(start))
    node_one = known_or(stepped(start, rate_zero, 0))
    rate_one = known_or(fine(node_one))
    node_two = known_or(stepped(node_one, rate_one, 1))
    rate_two = known_or(fine(node_two))
    fresh = (rate_zero, rate_one, rate_two)
    rest_zero, rest_one, rest_two = restricted(start), restricted(node_one), restricted(node_two)
    rest_integral = [restricted(quadrature(fresh, interval)) for interval in (0, 1)]
    coarse_start = rest_zero

    def coarse_stepped(state, rate, rest_rate, integral):
        @functools.cache
        def at(c):
            return tuple(
                s + HALF_STEP * (f - g) + q for s, f, g, q in zip(state(c), rate(c), rest_rate(c), integral(c))
            )

        return at

    coarse_one = coarse_stepped(coarse_start, coarse(coarse_start), coarse(rest_zero), rest_integral[0])
    coarse_two = coarse_stepped(coarse_one, coarse(coarse_one), coarse(rest_one), rest_integral[1])

    def corrected(node, coarse_node, rest):
        change = functools.cache(lambda c: tuple(spread(w - m) for w, m in zip(coarse_node(c), rest(c))))

        @functools.cache
        def at(r):
            return tuple(n + d for n, d in zip(node(r), change(r // 2)))

        return at

    nodes = corrected(node_one, coarse_one, rest_one), corrected(node_two, coarse_two, rest_two)
    return (rate_zero, *nodes), (rate_zero, node_one, rate_one, node_two, rate_two)


def rows_of(ref, width, first):
    @functools.cache
    def at(r):
        assert 0 <= (r - first) * width < ref.shape[1]
        return tuple(ref[field, pl.ds((r - first) * width, width), :] for field in range(2))

    return at


def pack_kernel(tiles_ref, state_ref, all_ref, high_ref):
    n_fields, n_x, n_y, _ = tiles_ref.shape
    for field in range(n_fields):
        for x in range(n_x):
            all_ref[field, pl.ds(x, n_y, stride=n_x), :] = tiles_ref[field, x]
        high_ref[field] = all_ref[field, pl.ds((n_y - BELOW) * n_x, BELOW * n_x), :]
    for field in range(2):
        state_ref[field] = all_ref[field]


def collect(out_ref, field, source_field, n_x, lowest, pieces):
    width = n_x * len(pieces[0][1])
    for first, refs, count in pieces:
        for gy, ref in enumerate(refs):
            for k in range(count):
                if first + k >= lowest:
                    place = pl.ds((first + k - lowest) * width + gy * n_x, n_x)
                    out_ref[field, place, :] = ref[source_field, pl.ds(k * n_x, n_x), :]


def first_kernel(n_gy, n_x, n_y, *refs):
    state_ref, local_ref = refs[:2]
    others, lows = refs[2 : 1 + n_gy], refs[1 + n_gy : 1 + 2 * n_gy]
    start_ref, params_ref, *outs = refs[1 + 2 * n_gy :]
    width = n_gy * n_x
    for field in range(2):
        collect(start_ref, field, field, n_x, -TAKE, [(-BELOW, lows, BELOW), (0, [state_ref, *others], n_y)])
        collect(params_ref, field, 2 + field, n_x, -TAKE, [(-BELOW, lows, BELOW), (0, [local_ref, *others], n_y)])
    start = rows_of(start_ref, width, -HALO)
    params = rows_of(params_ref, width, -HALO)
    results, _ = iteration(start, lambda r: params(r)[0], lambda r: params(r)[1], None)
    write_nodes(results, width, n_y, [(0, TAKE)], *outs)
    for r in range(HALO):
        for field, value in enumerate((*start(r + DRIFT), *params(r + DRIFT))):
            outs[-1][pl.ds((4 * TAKE + field * HALO + r) * width, width), :] = value


def write_nodes(results, width, n_y, edges, zero_ref, one_ref, two_ref, *edge_refs):
    rate_zero, node_one, node_two = results
    for r in range(-RATE_HALO, n_y + RATE_HALO):
        if 0 <= r < n_y:
            place = pl.ds(r * width, width)
            for field, (one, two) in enumerate(zip(node_one(r), node_two(r))):
                one_ref[field, place, :] = one
                two_ref[field, place, :] = two
                for i, (first, count) in enumerate(edges):
                    if first <= r < first + count:
                        beside = pl.ds((r - first) * width, width)
                        edge_refs[2 * i][field, beside, :] = two
                        for at, value in ((field, one), (2 + field, two)):
                            edge_refs[2 * i + 1][pl.ds((at * count + r - first) * width, width), :] = value
        for field, zero in enumerate(rate_zero(r)):
            zero_ref[field, pl.ds((r + RATE_HALO) * width, width), :] = zero


def joined(*parts):
    def at(r):
        return [rows for first, rows in parts if first <= r][-1](r)

    return at


def flat_rows(ref, width, place, first, count):
    @functools.cache
    def at(r):
        assert 0 <= r - first < count
        return tuple(ref[pl.ds((place + field * count + r - first) * width, width), :] for field in range(2))

    return at


def known(width, n_y, start_ref, params_ref, edge_ref):
    return (
        joined(
            (-TAKE, rows_of(ref, width, -TAKE)), (n_y, flat_rows(edge_ref, width, 4 * TAKE + place * HALO, n_y, HALO))
        )
        for ref, place in ((start_ref, 0), (params_ref, 2))
    )


def later_iteration(is_first, kept, params, got, old_zero, ones, twos, inner=()):
    feed, kill = (lambda r: params(r)[0]), (lambda r: params(r)[1])
    feed_kill = functools.cache(lambda r: feed(r) + kill(r))

    @functools.cache
    def start(r):
        return tuple(jnp.where(is_first, a, b) for a, b in zip(kept(r), got(r)))

    old_rates = (
        old_zero(feed, feed_kill),
        rates_of(ones, feed, feed_kill, 1.0),
        rates_of(twos, feed, feed_kill, 1.0),
    )
    return iteration(start, feed, kill, old_rates, inner)


def inner_kernel(width, n_y, tile_first, first_ref, start_ref, params_ref, zero_ref, one_ref, two_ref, got_ref, *outs):
    kept, params = rows_of(start_ref, width, -TAKE), rows_of(params_ref, width, -TAKE)
    old_zero = rows_of(zero_ref, width, tile_first - RATE_HALO)
    ones, twos, got = (rows_of(ref, width, tile_first) for ref in (one_ref, two_ref, got_ref))
    _, values = later_iteration(first_ref[0] == 1, kept, params, got, lambda feed, feed_kill: old_zero, ones, twos)
    ranges = inner_rows(n_y, tile_first)
    for r in range(ranges[0][0], ranges[0][1] + 2):
        for k, (low, high), rows, ref in zip((0, 0, 1, 1, 2), ranges, values, outs):
            if low <= r - k < high:
                for field, value in enumerate(rows(r - k)):
                    ref[field, pl.ds((r - k - low) * width, width), :] = value


def inner_of(refs, width, n_y, tile_first):
    return [(low, high, rows_of(ref, width, low)) for (low, high), ref in zip(inner_rows(n_y, tile_first), refs)]


def second_kernel(width, n_y, first_ref, start_ref, params_ref, *refs):
    zero_ref, one_ref, two_ref, got_ref, got_edge, pair_edge, *outs = refs[5:]
    inner = inner_of(refs, width, n_y, -DRIFT)
    kept, params = known(width, n_y, start_ref, params_ref, pair_edge)
    end = n_y - DRIFT

    def moved(tile_ref, beside):
        return joined((-DRIFT, rows_of(tile_ref, width, -DRIFT)), (end, beside))

    def pair(place):
        return flat_rows(pair_edge, width, place * TAKE, end, TAKE)

    def old_zero(feed, feed_kill):
        inside = rows_of(zero_ref, width, -RATE_HALO - DRIFT)
        return joined((-RATE_HALO - DRIFT, inside), (end + RATE_HALO, rates_of(kept, feed, feed_kill, 1.0)))

    ones, twos = moved(one_ref, pair(0)), moved(two_ref, pair(2))
    got = moved(got_ref, rows_of(got_edge, width, end))
    results, _ = later_iteration(first_ref[0] == 1, kept, params, got, old_zero, ones, twos, inner)
    write_nodes(results, width, n_y, [(0, HALO), (n_y - HALO, HALO)], *outs)


def later_kernel(width, n_y, out_x, first_ref, start_ref, params_ref, known_ref, *refs):
    zero_ref, one_ref, two_ref, got_ref, got_low, got_high, pair_low, pair_high, *outs = refs[5:]
    inner = inner_of(refs, width, n_y, 0)
    kept, params = known(width, n_y, start_ref, params_ref, known_ref)

    def window(low, tile_ref, high):
        return joined((-HALO, low), (0, rows_of(tile_ref, width, 0)), (n_y, high))

    def pair(tile_ref, place):
        low, high = (
            flat_rows(ref, width, place * HALO, first, HALO) for ref, first in ((pair_low, -HALO), (pair_high, n_y))
        )
        return window(low, tile_ref, high)

    ones, twos = pair(one_ref, 0), pair(two_ref, 2)
    old_zero = rows_of(zero_ref, width, -RATE_HALO)
    got = window(rows_of(got_low, width, -HALO), got_ref, rows_of(got_high, width, n_y))
    results, _ = later_iteration(
        first_ref[0] == 1, kept, params, got, lambda feed, feed_kill: old_zero, ones, twos, inner
    )
    if out_x is None:
        write_nodes(results, width, n_y, [(0, HALO), (n_y - HALO, HALO)], *outs)
    else:
        out_ref, scratch = outs
        for r in range(n_y):
            for field, value in enumerate(results[2](r)):
                scratch[field, pl.ds(r * width, width), :] = value
        for x in range(out_x):
            for field in range(2):
                out_ref[field, x] = scratch[field, pl.ds(x, n_y, stride=width), :]


def call(kernel, name, n_scalars, operands, shapes, scratch=()):
    specs = [pl.BlockSpec(memory_space=pltpu.SMEM)] * n_scalars
    specs += [pl.BlockSpec(memory_space=pltpu.VMEM)] * (len(operands) - n_scalars)
    return pl.pallas_call(
        kernel,
        name=name,
        out_shape=[jax.ShapeDtypeStruct(shape, jnp.float32) for shape in shapes],
        in_specs=specs,
        out_specs=[pl.BlockSpec(memory_space=pltpu.VMEM)] * len(shapes),
        scratch_shapes=scratch,
        compiler_params=pltpu.CompilerParams(vmem_limit_bytes=32 * 1024 * 1024),
    )(*operands)


def shards(initial_state, slice_guess, feed_rate, kill_rate):
    n_gy, n_tm = lax.axis_size("gy"), lax.axis_size("tm")
    _, n_x, n_y, n_z = initial_state.shape
    width = n_gy * n_x
    place = lax.axis_index("tm")
    is_first = (place == 0).astype(jnp.int32)[None]

    sent = jnp.where(place == n_tm - 1, initial_state, slice_guess[0])
    state, local, high = call(
        pack_kernel,
        "pack",
        0,
        (jnp.concatenate([sent, feed_rate[None], kill_rate[None]]),),
        [(2, n_y * n_x, n_z), (4, n_y * n_x, n_z), (4, BELOW * n_x, n_z)],
    )
    got = [shifted(state, 1, 0, 0), local]
    got += [shifted(local, 1, -gy, 0) for gy in range(1, n_gy)]
    got += [shifted(high, 1, -gy, 1) for gy in range(n_gy)]

    tile, window = (2, n_y * width, n_z), (2, (TAKE + n_y) * width, n_z)
    nodes_only = [(2, (n_y + 2 * RATE_HALO) * width, n_z), tile, tile]
    edge = lambda rows, more=0: [(2, rows * width, n_z), ((4 * rows + more) * width, n_z)]
    start, params, *nodes = call(
        functools.partial(first_kernel, n_gy, n_x, n_y),
        "first",
        0,
        got,
        [window, window, *nodes_only, *edge(TAKE, 4 * HALO)],
    )
    zero, one, two, two_edge, pair_edge = nodes
    got = [shifted(two, 1, 0, 0), shifted(two_edge, 1, 0, -1), shifted(pair_edge, 0, 0, -1)]
    known_edge = got[-1]

    def inner(tile_first):
        return call(
            functools.partial(inner_kernel, width, n_y, tile_first),
            "inner",
            1,
            (is_first, start, params, *nodes[:3], got[0]),
            [(2, (high - low) * width, n_z) for low, high in inner_rows(n_y, tile_first)],
        )

    nodes = call(
        functools.partial(second_kernel, width, n_y),
        "second",
        1,
        (is_first, start, params, *inner(-DRIFT), zero, one, two, *got),
        [*nodes_only, *edge(HALO), *edge(HALO)],
    )
    for sweep_index in range(2, ITERS):
        zero, one, two, two_low, pair_low, two_high, pair_high = nodes
        got = [shifted(two, 1, 0, 0), shifted(two_high, 1, 0, 1), shifted(two_low, 1, 0, -1)]
        got += [shifted(pair_high, 0, 0, 1), shifted(pair_low, 0, 0, -1)]
        done = sweep_index + 1 == ITERS
        nodes = call(
            functools.partial(later_kernel, width, n_y, n_x if done else None),
            "last" if done else "later",
            1,
            (is_first, start, params, known_edge, *inner(0), zero, one, two, *got),
            [initial_state.shape] if done else [*nodes_only, *edge(HALO), *edge(HALO)],
            [pltpu.VMEM(tile, jnp.float32)] if done else (),
        )
    return nodes[0][None]


def solution(mesh):
    in_specs = (
        P(None, "gy", "gx", None),
        P("tm", None, "gy", "gx", None),
        P("gy", "gx", None),
        P("gy", "gx", None),
    )
    out_specs = P("tm", None, "gy", "gx", None)
    return jax.shard_map(shards, mesh=mesh, in_specs=in_specs, out_specs=out_specs, check_vma=False)
```

```python
import functools

import jax
import jax.numpy as jnp
from jax import lax
from jax.experimental import pallas as pl
from jax.experimental.pallas import tpu as pltpu
from jax.sharding import PartitionSpec as P

ITERS = 3
DIFF_U = 0.2
DIFF_V = 0.1
HALF_STEP = 0.5
WEIGHTS = ((5.0 / 24.0, 8.0 / 24.0, -1.0 / 24.0), (-1.0 / 24.0, 8.0 / 24.0, 5.0 / 24.0))

AXES = ("tm", "gy", "gx")
HALO = 5
RATE_HALO = 4
DRIFT = 6
TAKE = HALO + DRIFT
BELOW = TAKE + 1


def shifted(value, by_tm, by_gy, by_gx):
    n_tm, n_gy, n_gx = (lax.axis_size(axis) for axis in AXES)
    pairs = []
    for t in range(n_tm):
        for y in range(n_gy):
            for x in range(n_gx):
                target = ((t + by_tm) % n_tm * n_gy + (y + by_gy) % n_gy) * n_gx + (x + by_gx) % n_gx
                pairs.append(((t * n_gy + y) * n_gx + x, target))
    return lax.ppermute(value, AXES, pairs)


def near(row, distance, axis):
    size = row.shape[axis]
    return pltpu.roll(row, distance % size, axis) + pltpu.roll(row, -distance % size, axis)


def rates_of(state, feed, feed_kill, spacing):
    scale = 1.0 / (spacing * spacing)

    @functools.cache
    def at(r):
        (u, v), (ub, vb), (ua, va) = state(r), state(r - 1), state(r + 1)
        around_u = (ub + ua) + near(u, int(spacing), 0) + near(u, int(spacing), 1)
        around_v = (vb + va) + near(v, int(spacing), 0) + near(v, int(spacing), 1)
        reaction = u * (v * v)
        rate_u = (DIFF_U * scale) * around_u + feed(r) - (6.0 * DIFF_U * scale + feed(r)) * u - reaction
        rate_v = (DIFF_V * scale) * around_v - (6.0 * DIFF_V * scale + feed_kill(r)) * v + reaction
        return rate_u, rate_v

    return at


def half_sum(low, high):
    x, z = low.shape
    total = low + high
    total = total + pltpu.roll(total, z - 1, 1)
    total = total + pltpu.roll(total, x - 1, 0)
    return 0.125 * total


def restricted(state):
    @functools.cache
    def at(c):
        return tuple(half_sum(a, b) for a, b in zip(state(2 * c), state(2 * c + 1)))

    return at


def spread(row):
    even_x = lax.broadcasted_iota(jnp.int32, row.shape, 0) % 2 == 0
    even_z = lax.broadcasted_iota(jnp.int32, row.shape, 1) % 2 == 0
    row = jnp.where(even_z, row, pltpu.roll(row, 1, 1))
    return jnp.where(even_x, row, pltpu.roll(row, 1, 0))


def quadrature(values, interval):
    def at(r):
        zero, one, two = (value(r) for value in values)
        w = WEIGHTS[interval]
        return tuple(w[0] * a + w[1] * b + w[2] * c for a, b, c in zip(zero, one, two))

    return at


def inner_rows(n_y, tile_first):
    low, high = max(tile_first + 1, -RATE_HALO), min(tile_first + n_y - 1, n_y + RATE_HALO)
    return [(low + k, high - k) for k in (0, 0, 1, 1, 2)]


def inner_shapes(width, n_y, n_z, tile_first):
    return [(2, (high - low) * width, n_z) for low, high in inner_rows(n_y, tile_first)]


def inner_of(refs, width, n_y, tile_first):
    return [(low, high, rows_of(ref, width, low)) for (low, high), ref in zip(inner_rows(n_y, tile_first), refs)]


def write_inner(values, width, n_y, tile_first, refs):
    ranges = inner_rows(n_y, tile_first)
    for r in range(ranges[0][0], ranges[0][1] + 2):
        for k, (low, high), rows, ref in zip((0, 0, 1, 1, 2), ranges, values, refs):
            if low <= r - k < high:
                for field, value in enumerate(rows(r - k)):
                    ref[field, pl.ds((r - k - low) * width, width), :] = value


def iteration(start, feed, kill, old_rates, inner=()):
    inner = iter(inner)

    def known_or(values):
        low, high, known = next(inner, (0, 0, None))
        return lambda r: (known if low <= r < high else values)(r)

    feed_kill = functools.cache(lambda r: feed(r) + kill(r))
    coarse_feed = functools.cache(lambda c: half_sum(feed(2 * c), feed(2 * c + 1)))
    coarse_sum = functools.cache(lambda c: half_sum(feed_kill(2 * c), feed_kill(2 * c + 1)))

    def stepped(state, rate, interval):
        @functools.cache
        def at(r):
            out = [s + HALF_STEP * f for s, f in zip(state(r), rate(r))]
            if old_rates is not None:
                integral = quadrature(old_rates, interval)(r)
                old = old_rates[interval](r)
                out = [o + (q - HALF_STEP * f) for o, q, f in zip(out, integral, old)]
            return tuple(out)

        return at

    fine = lambda state: rates_of(state, feed, feed_kill, 1.0)
    coarse = lambda state: rates_of(state, coarse_feed, coarse_sum, 2.0)
    rate_zero = known_or(fine(start))
    node_one = known_or(stepped(start, rate_zero, 0))
    rate_one = known_or(fine(node_one))
    node_two = known_or(stepped(node_one, rate_one, 1))
    rate_two = known_or(fine(node_two))
    fresh = (rate_zero, rate_one, rate_two)
    rest_zero, rest_one, rest_two = restricted(start), restricted(node_one), restricted(node_two)
    rest_integral = [restricted(quadrature(fresh, interval)) for interval in (0, 1)]
    coarse_start = rest_zero

    def coarse_stepped(state, rate, rest_rate, integral):
        @functools.cache
        def at(c):
            return tuple(
                s + HALF_STEP * (f - g) + q for s, f, g, q in zip(state(c), rate(c), rest_rate(c), integral(c))
            )

        return at

    coarse_one = coarse_stepped(coarse_start, coarse(coarse_start), coarse(rest_zero), rest_integral[0])
    coarse_two = coarse_stepped(coarse_one, coarse(coarse_one), coarse(rest_one), rest_integral[1])

    def corrected(node, coarse_node, rest):
        change = functools.cache(lambda c: tuple(spread(w - m) for w, m in zip(coarse_node(c), rest(c))))

        @functools.cache
        def at(r):
            return tuple(n + d for n, d in zip(node(r), change(r // 2)))

        return at

    nodes = corrected(node_one, coarse_one, rest_one), corrected(node_two, coarse_two, rest_two)
    return (rate_zero, *nodes), (rate_zero, node_one, rate_one, node_two, rate_two)


def rows_of(ref, width, first):
    @functools.cache
    def at(r):
        assert 0 <= (r - first) * width < ref.shape[1]
        return tuple(ref[field, pl.ds((r - first) * width, width), :] for field in range(2))

    return at


def pack_kernel(tiles_ref, state_ref, all_ref, high_ref):
    n_fields, n_x, n_y, _ = tiles_ref.shape
    for field in range(n_fields):
        for x in range(n_x):
            all_ref[field, pl.ds(x, n_y, stride=n_x), :] = tiles_ref[field, x]
        high_ref[field] = all_ref[field, pl.ds((n_y - BELOW) * n_x, BELOW * n_x), :]
    for field in range(2):
        state_ref[field] = all_ref[field]


def collect(out_ref, field, source_field, n_x, lowest, pieces):
    width = n_x * len(pieces[0][1])
    for first, refs, count in pieces:
        for gy, ref in enumerate(refs):
            for k in range(count):
                if first + k >= lowest:
                    place = pl.ds((first + k - lowest) * width + gy * n_x, n_x)
                    out_ref[field, place, :] = ref[source_field, pl.ds(k * n_x, n_x), :]


def first_inner_kernel(n_gy, n_x, n_y, *refs):
    state_ref, local_ref = refs[:2]
    others = refs[2 : 1 + n_gy]
    start_ref, params_ref, *outs = refs[1 + n_gy :]
    width = n_gy * n_x
    for field in range(2):
        collect(start_ref, field, field, n_x, 0, [(0, [state_ref, *others], n_y)])
        collect(params_ref, field, 2 + field, n_x, 0, [(0, [local_ref, *others], n_y)])
    start, params = rows_of(start_ref, width, DRIFT), rows_of(params_ref, width, DRIFT)
    _, values = iteration(start, lambda r: params(r)[0], lambda r: params(r)[1], None)
    write_inner(values, width, n_y, DRIFT, outs)


def first_kernel(n_gy, n_x, n_y, *refs):
    tiles, inner_refs, lows = refs[:2], refs[2:7], refs[7 : 7 + n_gy]
    start_ref, params_ref, *outs = refs[7 + n_gy :]
    width = n_gy * n_x
    for field in range(2):
        for out_ref, tile_ref, place in zip((start_ref, params_ref), tiles, (0, 2)):
            collect(out_ref, field, place + field, n_x, -TAKE, [(-BELOW, lows, BELOW)])
            out_ref[field, pl.ds(TAKE * width, n_y * width), :] = tile_ref[field]
    start = rows_of(start_ref, width, -HALO)
    params = rows_of(params_ref, width, -HALO)
    inner = inner_of(inner_refs, width, n_y, DRIFT)
    results, _ = iteration(start, lambda r: params(r)[0], lambda r: params(r)[1], None, inner)
    write_nodes(results, width, n_y, [(0, TAKE)], *outs)
    for r in range(HALO):
        for field, value in enumerate((*start(r + DRIFT), *params(r + DRIFT))):
            outs[-1][pl.ds((4 * TAKE + field * HALO + r) * width, width), :] = value


def write_nodes(results, width, n_y, edges, zero_ref, one_ref, two_ref, *edge_refs):
    rate_zero, node_one, node_two = results
    for r in range(-RATE_HALO, n_y + RATE_HALO):
        if 0 <= r < n_y:
            place = pl.ds(r * width, width)
            for field, (one, two) in enumerate(zip(node_one(r), node_two(r))):
                one_ref[field, place, :] = one
                two_ref[field, place, :] = two
                for i, (first, count) in enumerate(edges):
                    if first <= r < first + count:
                        beside = pl.ds((r - first) * width, width)
                        edge_refs[2 * i][field, beside, :] = two
                        for at, value in ((field, one), (2 + field, two)):
                            edge_refs[2 * i + 1][pl.ds((at * count + r - first) * width, width), :] = value
        for field, zero in enumerate(rate_zero(r)):
            zero_ref[field, pl.ds((r + RATE_HALO) * width, width), :] = zero


def joined(*parts):
    def at(r):
        return [rows for first, rows in parts if first <= r][-1](r)

    return at


def flat_rows(ref, width, place, first, count):
    @functools.cache
    def at(r):
        assert 0 <= r - first < count
        return tuple(ref[pl.ds((place + field * count + r - first) * width, width), :] for field in range(2))

    return at


def known(width, n_y, start_ref, params_ref, edge_ref):
    return (
        joined(
            (-TAKE, rows_of(ref, width, -TAKE)), (n_y, flat_rows(edge_ref, width, 4 * TAKE + place * HALO, n_y, HALO))
        )
        for ref, place in ((start_ref, 0), (params_ref, 2))
    )


def later_iteration(is_first, kept, params, got, old_zero, ones, twos, inner=()):
    feed, kill = (lambda r: params(r)[0]), (lambda r: params(r)[1])
    feed_kill = functools.cache(lambda r: feed(r) + kill(r))

    @functools.cache
    def start(r):
        return tuple(jnp.where(is_first, a, b) for a, b in zip(kept(r), got(r)))

    old_rates = (
        old_zero(feed, feed_kill),
        rates_of(ones, feed, feed_kill, 1.0),
        rates_of(twos, feed, feed_kill, 1.0),
    )
    return iteration(start, feed, kill, old_rates, inner)


def inner_kernel(width, n_y, tile_first, first_ref, start_ref, params_ref, zero_ref, one_ref, two_ref, got_ref, *outs):
    kept, params = rows_of(start_ref, width, -TAKE), rows_of(params_ref, width, -TAKE)
    old_zero = rows_of(zero_ref, width, tile_first - RATE_HALO)
    ones, twos, got = (rows_of(ref, width, tile_first) for ref in (one_ref, two_ref, got_ref))
    _, values = later_iteration(first_ref[0] == 1, kept, params, got, lambda feed, feed_kill: old_zero, ones, twos)
    write_inner(values, width, n_y, tile_first, outs)


def second_kernel(width, n_y, first_ref, start_ref, params_ref, *refs):
    zero_ref, one_ref, two_ref, got_ref, got_edge, pair_edge, *outs = refs[5:]
    inner = inner_of(refs, width, n_y, -DRIFT)
    kept, params = known(width, n_y, start_ref, params_ref, pair_edge)
    end = n_y - DRIFT

    def moved(tile_ref, beside):
        return joined((-DRIFT, rows_of(tile_ref, width, -DRIFT)), (end, beside))

    def pair(place):
        return flat_rows(pair_edge, width, place * TAKE, end, TAKE)

    def old_zero(feed, feed_kill):
        inside = rows_of(zero_ref, width, -RATE_HALO - DRIFT)
        return joined((-RATE_HALO - DRIFT, inside), (end + RATE_HALO, rates_of(kept, feed, feed_kill, 1.0)))

    ones, twos = moved(one_ref, pair(0)), moved(two_ref, pair(2))
    got = moved(got_ref, rows_of(got_edge, width, end))
    results, _ = later_iteration(first_ref[0] == 1, kept, params, got, old_zero, ones, twos, inner)
    write_nodes(results, width, n_y, [(0, HALO), (n_y - HALO, HALO)], *outs)


def later_kernel(width, n_y, out_x, first_ref, start_ref, params_ref, known_ref, *refs):
    zero_ref, one_ref, two_ref, got_ref, got_low, got_high, pair_low, pair_high, *outs = refs[5:]
    inner = inner_of(refs, width, n_y, 0)
    kept, params = known(width, n_y, start_ref, params_ref, known_ref)

    def window(low, tile_ref, high):
        return joined((-HALO, low), (0, rows_of(tile_ref, width, 0)), (n_y, high))

    def pair(tile_ref, place):
        low, high = (
            flat_rows(ref, width, place * HALO, first, HALO) for ref, first in ((pair_low, -HALO), (pair_high, n_y))
        )
        return window(low, tile_ref, high)

    ones, twos = pair(one_ref, 0), pair(two_ref, 2)
    old_zero = rows_of(zero_ref, width, -RATE_HALO)
    got = window(rows_of(got_low, width, -HALO), got_ref, rows_of(got_high, width, n_y))
    results, _ = later_iteration(
        first_ref[0] == 1, kept, params, got, lambda feed, feed_kill: old_zero, ones, twos, inner
    )
    if out_x is None:
        write_nodes(results, width, n_y, [(0, HALO), (n_y - HALO, HALO)], *outs)
    else:
        out_ref, scratch = outs
        for r in range(n_y):
            for field, value in enumerate(results[2](r)):
                scratch[field, pl.ds(r * width, width), :] = value
        for x in range(out_x):
            for field in range(2):
                out_ref[field, x] = scratch[field, pl.ds(x, n_y, stride=width), :]


def call(kernel, name, n_scalars, operands, shapes, scratch=()):
    specs = [pl.BlockSpec(memory_space=pltpu.SMEM)] * n_scalars
    specs += [pl.BlockSpec(memory_space=pltpu.VMEM)] * (len(operands) - n_scalars)
    return pl.pallas_call(
        kernel,
        name=name,
        out_shape=[jax.ShapeDtypeStruct(shape, jnp.float32) for shape in shapes],
        in_specs=specs,
        out_specs=[pl.BlockSpec(memory_space=pltpu.VMEM)] * len(shapes),
        scratch_shapes=scratch,
        compiler_params=pltpu.CompilerParams(vmem_limit_bytes=32 * 1024 * 1024),
    )(*operands)


def shards(initial_state, slice_guess, feed_rate, kill_rate):
    n_gy, n_tm = lax.axis_size("gy"), lax.axis_size("tm")
    _, n_x, n_y, n_z = initial_state.shape
    width = n_gy * n_x
    place = lax.axis_index("tm")
    is_first = (place == 0).astype(jnp.int32)[None]

    sent = jnp.where(place == n_tm - 1, initial_state, slice_guess[0])
    state, local, high = call(
        pack_kernel,
        "pack",
        0,
        (jnp.concatenate([sent, feed_rate[None], kill_rate[None]]),),
        [(2, n_y * n_x, n_z), (4, n_y * n_x, n_z), (4, BELOW * n_x, n_z)],
    )
    got = [shifted(state, 1, 0, 0), local]
    got += [shifted(local, 1, -gy, 0) for gy in range(1, n_gy)]
    below = [shifted(high, 1, -gy, 1) for gy in range(n_gy)]

    tile, window = (2, n_y * width, n_z), (2, (TAKE + n_y) * width, n_z)
    nodes_only = [(2, (n_y + 2 * RATE_HALO) * width, n_z), tile, tile]
    edge = lambda rows, more=0: [(2, rows * width, n_z), ((4 * rows + more) * width, n_z)]
    inner_first = call(
        functools.partial(first_inner_kernel, n_gy, n_x, n_y),
        "inner_first",
        0,
        got,
        [tile, tile, *inner_shapes(width, n_y, n_z, DRIFT)],
    )
    start, params, *nodes = call(
        functools.partial(first_kernel, n_gy, n_x, n_y),
        "first",
        0,
        [*inner_first, *below],
        [window, window, *nodes_only, *edge(TAKE, 4 * HALO)],
    )
    zero, one, two, two_edge, pair_edge = nodes
    got = [shifted(two, 1, 0, 0), shifted(two_edge, 1, 0, -1), shifted(pair_edge, 0, 0, -1)]
    known_edge = got[-1]

    def inner(tile_first):
        return call(
            functools.partial(inner_kernel, width, n_y, tile_first),
            "inner",
            1,
            (is_first, start, params, *nodes[:3], got[0]),
            inner_shapes(width, n_y, n_z, tile_first),
        )

    nodes = call(
        functools.partial(second_kernel, width, n_y),
        "second",
        1,
        (is_first, start, params, *inner(-DRIFT), zero, one, two, *got),
        [*nodes_only, *edge(HALO), *edge(HALO)],
    )
    for sweep_index in range(2, ITERS):
        zero, one, two, two_low, pair_low, two_high, pair_high = nodes
        got = [shifted(two, 1, 0, 0), shifted(two_high, 1, 0, 1), shifted(two_low, 1, 0, -1)]
        got += [shifted(pair_high, 0, 0, 1), shifted(pair_low, 0, 0, -1)]
        done = sweep_index + 1 == ITERS
        nodes = call(
            functools.partial(later_kernel, width, n_y, n_x if done else None),
            "last" if done else "later",
            1,
            (is_first, start, params, known_edge, *inner(0), zero, one, two, *got),
            [initial_state.shape] if done else [*nodes_only, *edge(HALO), *edge(HALO)],
            [pltpu.VMEM(tile, jnp.float32)] if done else (),
        )
    return nodes[0][None]


def solution(mesh):
    in_specs = (
        P(None, "gy", "gx", None),
        P("tm", None, "gy", "gx", None),
        P("gy", "gx", None),
        P("gy", "gx", None),
    )
    out_specs = P("tm", None, "gy", "gx", None)
    return jax.shard_map(shards, mesh=mesh, in_specs=in_specs, out_specs=out_specs, check_vma=False)
```

```python
import functools

import jax
import jax.numpy as jnp
from jax import lax
from jax.experimental import pallas as pl
from jax.experimental.pallas import tpu as pltpu
from jax.sharding import PartitionSpec as P

ITERS = 3
DIFF_U = 0.2
DIFF_V = 0.1
HALF_STEP = 0.5
WEIGHTS = ((5.0 / 24.0, 8.0 / 24.0, -1.0 / 24.0), (-1.0 / 24.0, 8.0 / 24.0, 5.0 / 24.0))

AXES = ("tm", "gy", "gx")
HALO = 5
RATE_HALO = 4
DRIFT = 6
TAKE = HALO + DRIFT
BELOW = TAKE + 1


def shifted(value, by_tm, by_gy, by_gx):
    n_tm, n_gy, n_gx = (lax.axis_size(axis) for axis in AXES)
    pairs = []
    for t in range(n_tm):
        for y in range(n_gy):
            for x in range(n_gx):
                target = ((t + by_tm) % n_tm * n_gy + (y + by_gy) % n_gy) * n_gx + (x + by_gx) % n_gx
                pairs.append(((t * n_gy + y) * n_gx + x, target))
    return lax.ppermute(value, AXES, pairs)


def near(row, distance, axis):
    size = row.shape[axis]
    return pltpu.roll(row, distance % size, axis) + pltpu.roll(row, -distance % size, axis)


def rates_of(state, feed, feed_kill, spacing):
    scale = 1.0 / (spacing * spacing)

    @functools.cache
    def at(r):
        (u, v), (ub, vb), (ua, va) = state(r), state(r - 1), state(r + 1)
        around_u = (ub + ua) + near(u, int(spacing), 0) + near(u, int(spacing), 1)
        around_v = (vb + va) + near(v, int(spacing), 0) + near(v, int(spacing), 1)
        reaction = u * (v * v)
        rate_u = (DIFF_U * scale) * around_u + feed(r) - (6.0 * DIFF_U * scale + feed(r)) * u - reaction
        rate_v = (DIFF_V * scale) * around_v - (6.0 * DIFF_V * scale + feed_kill(r)) * v + reaction
        return rate_u, rate_v

    return at


def half_sum(low, high):
    x, z = low.shape
    total = low + high
    total = total + pltpu.roll(total, z - 1, 1)
    total = total + pltpu.roll(total, x - 1, 0)
    return 0.125 * total


def restricted(state):
    @functools.cache
    def at(c):
        return tuple(half_sum(a, b) for a, b in zip(state(2 * c), state(2 * c + 1)))

    return at


def spread(row):
    even_x = lax.broadcasted_iota(jnp.int32, row.shape, 0) % 2 == 0
    even_z = lax.broadcasted_iota(jnp.int32, row.shape, 1) % 2 == 0
    row = jnp.where(even_z, row, pltpu.roll(row, 1, 1))
    return jnp.where(even_x, row, pltpu.roll(row, 1, 0))


def quadrature(values, interval):
    def at(r):
        zero, one, two = (value(r) for value in values)
        w = WEIGHTS[interval]
        return tuple(w[0] * a + w[1] * b + w[2] * c for a, b, c in zip(zero, one, two))

    return at


INNER_COUNT = 11


def inner_rows(n_y, tile_first):
    low, high = max(tile_first, -HALO), min(tile_first + n_y, n_y + HALO)
    halves = lambda first, last: (-(-first // 2), last // 2)
    clip = lambda rows, by: (max(rows[0], -by), min(rows[1], n_y // 2 + by))
    inside = lambda rows: (rows[0] + 1, rows[1] - 1)
    fine = [(low + k, high - k) for k in (1, 1, 2, 2, 3)]
    start, one, integral = halves(low, high), halves(*fine[1]), halves(*fine[4])
    coarse = [clip(start, 2), clip(one, 1), clip(integral, 1), clip(integral, 0)]
    return [*fine, *coarse, clip(inside(start), 1), clip(inside(one), 0)]


def inner_shapes(width, n_y, n_z, tile_first):
    return [(2, (high - low) * width, n_z) for low, high in inner_rows(n_y, tile_first)]


def inner_of(refs, width, n_y, tile_first):
    return [(low, high, rows_of(ref, width, low)) for (low, high), ref in zip(inner_rows(n_y, tile_first), refs)]


def write_inner(values, width, n_y, tile_first, refs):
    items = []
    for i, ((low, high), rows, ref) in enumerate(zip(inner_rows(n_y, tile_first), values, refs)):
        for r in range(low, high):
            ready = r + (0, 0, 1, 1, 2)[i] if i < 5 else 2 * r + (1, 1, 3, 3, 3, 3)[i - 5]
            items.append((ready, i, r, rows, ref, low))
    for _, _, r, rows, ref, low in sorted(items, key=lambda item: item[:3]):
        for field, value in enumerate(rows(r)):
            ref[field, pl.ds((r - low) * width, width), :] = value


def iteration(start, feed, kill, old_rates, inner=()):
    inner = iter(inner)

    def known_or(values):
        low, high, known = next(inner, (0, 0, None))
        return lambda r: (known if low <= r < high else values)(r)

    feed_kill = functools.cache(lambda r: feed(r) + kill(r))
    coarse_feed = functools.cache(lambda c: half_sum(feed(2 * c), feed(2 * c + 1)))
    coarse_sum = functools.cache(lambda c: half_sum(feed_kill(2 * c), feed_kill(2 * c + 1)))

    def stepped(state, rate, interval):
        @functools.cache
        def at(r):
            out = [s + HALF_STEP * f for s, f in zip(state(r), rate(r))]
            if old_rates is not None:
                integral = quadrature(old_rates, interval)(r)
                old = old_rates[interval](r)
                out = [o + (q - HALF_STEP * f) for o, q, f in zip(out, integral, old)]
            return tuple(out)

        return at

    fine = lambda state: rates_of(state, feed, feed_kill, 1.0)
    coarse = lambda state: rates_of(state, coarse_feed, coarse_sum, 2.0)
    rate_zero = known_or(fine(start))
    node_one = known_or(stepped(start, rate_zero, 0))
    rate_one = known_or(fine(node_one))
    node_two = known_or(stepped(node_one, rate_one, 1))
    rate_two = known_or(fine(node_two))
    fresh = (rate_zero, rate_one, rate_two)
    rest_zero, rest_one, rest_two = known_or(restricted(start)), known_or(restricted(node_one)), restricted(node_two)
    rest_integral = [known_or(restricted(quadrature(fresh, interval))) for interval in (0, 1)]
    rate_rest_zero, rate_rest_one = known_or(coarse(rest_zero)), known_or(coarse(rest_one))
    coarse_start, rate_coarse_start = rest_zero, rate_rest_zero

    def coarse_stepped(state, rate, rest_rate, integral):
        @functools.cache
        def at(c):
            return tuple(
                s + HALF_STEP * (f - g) + q for s, f, g, q in zip(state(c), rate(c), rest_rate(c), integral(c))
            )

        return at

    coarse_one = coarse_stepped(coarse_start, rate_coarse_start, rate_rest_zero, rest_integral[0])
    coarse_two = coarse_stepped(coarse_one, coarse(coarse_one), rate_rest_one, rest_integral[1])

    def corrected(node, coarse_node, rest):
        change = functools.cache(lambda c: tuple(spread(w - m) for w, m in zip(coarse_node(c), rest(c))))

        @functools.cache
        def at(r):
            return tuple(n + d for n, d in zip(node(r), change(r // 2)))

        return at

    nodes = corrected(node_one, coarse_one, rest_one), corrected(node_two, coarse_two, rest_two)
    fine_rows = (rate_zero, node_one, rate_one, node_two, rate_two)
    return (rate_zero, *nodes), (*fine_rows, rest_zero, rest_one, *rest_integral, rate_rest_zero, rate_rest_one)


def rows_of(ref, width, first):
    @functools.cache
    def at(r):
        assert 0 <= (r - first) * width < ref.shape[1]
        return tuple(ref[field, pl.ds((r - first) * width, width), :] for field in range(2))

    return at


def pack_kernel(tiles_ref, state_ref, all_ref, high_ref):
    n_fields, n_x, n_y, _ = tiles_ref.shape
    for field in range(n_fields):
        for x in range(n_x):
            all_ref[field, pl.ds(x, n_y, stride=n_x), :] = tiles_ref[field, x]
        high_ref[field] = all_ref[field, pl.ds((n_y - BELOW) * n_x, BELOW * n_x), :]
    for field in range(2):
        state_ref[field] = all_ref[field]


def collect(out_ref, field, source_field, n_x, lowest, pieces):
    width = n_x * len(pieces[0][1])
    for first, refs, count in pieces:
        for gy, ref in enumerate(refs):
            for k in range(count):
                if first + k >= lowest:
                    place = pl.ds((first + k - lowest) * width + gy * n_x, n_x)
                    out_ref[field, place, :] = ref[source_field, pl.ds(k * n_x, n_x), :]


def first_inner_kernel(n_gy, n_x, n_y, *refs):
    state_ref, local_ref = refs[:2]
    others = refs[2 : 1 + n_gy]
    start_ref, params_ref, *outs = refs[1 + n_gy :]
    width = n_gy * n_x
    for field in range(2):
        collect(start_ref, field, field, n_x, 0, [(0, [state_ref, *others], n_y)])
        collect(params_ref, field, 2 + field, n_x, 0, [(0, [local_ref, *others], n_y)])
    start, params = rows_of(start_ref, width, DRIFT), rows_of(params_ref, width, DRIFT)
    _, values = iteration(start, lambda r: params(r)[0], lambda r: params(r)[1], None)
    write_inner(values, width, n_y, DRIFT, outs)


def first_kernel(n_gy, n_x, n_y, *refs):
    tiles, inner_refs, refs = refs[:2], refs[2 : 2 + INNER_COUNT], refs[2 + INNER_COUNT :]
    lows, (start_ref, params_ref, *outs) = refs[:n_gy], refs[n_gy:]
    width = n_gy * n_x
    for field in range(2):
        for out_ref, tile_ref, place in zip((start_ref, params_ref), tiles, (0, 2)):
            collect(out_ref, field, place + field, n_x, -TAKE, [(-BELOW, lows, BELOW)])
            out_ref[field, pl.ds(TAKE * width, n_y * width), :] = tile_ref[field]
    start = rows_of(start_ref, width, -HALO)
    params = rows_of(params_ref, width, -HALO)
    inner = inner_of(inner_refs, width, n_y, DRIFT)
    results, _ = iteration(start, lambda r: params(r)[0], lambda r: params(r)[1], None, inner)
    write_nodes(results, width, n_y, [(0, TAKE)], *outs)
    for r in range(HALO):
        for field, value in enumerate((*start(r + DRIFT), *params(r + DRIFT))):
            outs[-1][pl.ds((4 * TAKE + field * HALO + r) * width, width), :] = value


def write_nodes(results, width, n_y, edges, zero_ref, one_ref, two_ref, *edge_refs):
    rate_zero, node_one, node_two = results
    for r in range(-RATE_HALO, n_y + RATE_HALO):
        if 0 <= r < n_y:
            place = pl.ds(r * width, width)
            for field, (one, two) in enumerate(zip(node_one(r), node_two(r))):
                one_ref[field, place, :] = one
                two_ref[field, place, :] = two
                for i, (first, count) in enumerate(edges):
                    if first <= r < first + count:
                        beside = pl.ds((r - first) * width, width)
                        edge_refs[2 * i][field, beside, :] = two
                        for at, value in ((field, one), (2 + field, two)):
                            edge_refs[2 * i + 1][pl.ds((at * count + r - first) * width, width), :] = value
        for field, zero in enumerate(rate_zero(r)):
            zero_ref[field, pl.ds((r + RATE_HALO) * width, width), :] = zero


def joined(*parts):
    def at(r):
        return [rows for first, rows in parts if first <= r][-1](r)

    return at


def flat_rows(ref, width, place, first, count):
    @functools.cache
    def at(r):
        assert 0 <= r - first < count
        return tuple(ref[pl.ds((place + field * count + r - first) * width, width), :] for field in range(2))

    return at


def known(width, n_y, start_ref, params_ref, edge_ref):
    return (
        joined(
            (-TAKE, rows_of(ref, width, -TAKE)), (n_y, flat_rows(edge_ref, width, 4 * TAKE + place * HALO, n_y, HALO))
        )
        for ref, place in ((start_ref, 0), (params_ref, 2))
    )


def later_iteration(is_first, kept, params, got, old_zero, ones, twos, inner=()):
    feed, kill = (lambda r: params(r)[0]), (lambda r: params(r)[1])
    feed_kill = functools.cache(lambda r: feed(r) + kill(r))

    @functools.cache
    def start(r):
        return tuple(jnp.where(is_first, a, b) for a, b in zip(kept(r), got(r)))

    old_rates = (
        old_zero(feed, feed_kill),
        rates_of(ones, feed, feed_kill, 1.0),
        rates_of(twos, feed, feed_kill, 1.0),
    )
    return iteration(start, feed, kill, old_rates, inner)


def inner_kernel(width, n_y, tile_first, first_ref, start_ref, params_ref, zero_ref, one_ref, two_ref, got_ref, *outs):
    kept, params = rows_of(start_ref, width, -TAKE), rows_of(params_ref, width, -TAKE)
    old_zero = rows_of(zero_ref, width, tile_first - RATE_HALO)
    ones, twos, got = (rows_of(ref, width, tile_first) for ref in (one_ref, two_ref, got_ref))
    _, values = later_iteration(first_ref[0] == 1, kept, params, got, lambda feed, feed_kill: old_zero, ones, twos)
    write_inner(values, width, n_y, tile_first, outs)


def second_kernel(width, n_y, first_ref, start_ref, params_ref, *refs):
    zero_ref, one_ref, two_ref, got_ref, got_edge, pair_edge, *outs = refs[INNER_COUNT:]
    inner = inner_of(refs, width, n_y, -DRIFT)
    kept, params = known(width, n_y, start_ref, params_ref, pair_edge)
    end = n_y - DRIFT

    def moved(tile_ref, beside):
        return joined((-DRIFT, rows_of(tile_ref, width, -DRIFT)), (end, beside))

    def pair(place):
        return flat_rows(pair_edge, width, place * TAKE, end, TAKE)

    def old_zero(feed, feed_kill):
        inside = rows_of(zero_ref, width, -RATE_HALO - DRIFT)
        return joined((-RATE_HALO - DRIFT, inside), (end + RATE_HALO, rates_of(kept, feed, feed_kill, 1.0)))

    ones, twos = moved(one_ref, pair(0)), moved(two_ref, pair(2))
    got = moved(got_ref, rows_of(got_edge, width, end))
    results, _ = later_iteration(first_ref[0] == 1, kept, params, got, old_zero, ones, twos, inner)
    write_nodes(results, width, n_y, [(0, HALO), (n_y - HALO, HALO)], *outs)


def later_kernel(width, n_y, out_x, first_ref, start_ref, params_ref, known_ref, *refs):
    zero_ref, one_ref, two_ref, got_ref, got_low, got_high, pair_low, pair_high, *outs = refs[INNER_COUNT:]
    inner = inner_of(refs, width, n_y, 0)
    kept, params = known(width, n_y, start_ref, params_ref, known_ref)

    def window(low, tile_ref, high):
        return joined((-HALO, low), (0, rows_of(tile_ref, width, 0)), (n_y, high))

    def pair(tile_ref, place):
        low, high = (
            flat_rows(ref, width, place * HALO, first, HALO) for ref, first in ((pair_low, -HALO), (pair_high, n_y))
        )
        return window(low, tile_ref, high)

    ones, twos = pair(one_ref, 0), pair(two_ref, 2)
    old_zero = rows_of(zero_ref, width, -RATE_HALO)
    got = window(rows_of(got_low, width, -HALO), got_ref, rows_of(got_high, width, n_y))
    results, _ = later_iteration(
        first_ref[0] == 1, kept, params, got, lambda feed, feed_kill: old_zero, ones, twos, inner
    )
    if out_x is None:
        write_nodes(results, width, n_y, [(0, HALO), (n_y - HALO, HALO)], *outs)
    else:
        out_ref, scratch = outs
        for r in range(n_y):
            for field, value in enumerate(results[2](r)):
                scratch[field, pl.ds(r * width, width), :] = value
        for x in range(out_x):
            for field in range(2):
                out_ref[field, x] = scratch[field, pl.ds(x, n_y, stride=width), :]


def call(kernel, name, n_scalars, operands, shapes, scratch=()):
    specs = [pl.BlockSpec(memory_space=pltpu.SMEM)] * n_scalars
    specs += [pl.BlockSpec(memory_space=pltpu.VMEM)] * (len(operands) - n_scalars)
    return pl.pallas_call(
        kernel,
        name=name,
        out_shape=[jax.ShapeDtypeStruct(shape, jnp.float32) for shape in shapes],
        in_specs=specs,
        out_specs=[pl.BlockSpec(memory_space=pltpu.VMEM)] * len(shapes),
        scratch_shapes=scratch,
        compiler_params=pltpu.CompilerParams(vmem_limit_bytes=32 * 1024 * 1024),
    )(*operands)


def shards(initial_state, slice_guess, feed_rate, kill_rate):
    n_gy, n_tm = lax.axis_size("gy"), lax.axis_size("tm")
    _, n_x, n_y, n_z = initial_state.shape
    width = n_gy * n_x
    place = lax.axis_index("tm")
    is_first = (place == 0).astype(jnp.int32)[None]

    sent = jnp.where(place == n_tm - 1, initial_state, slice_guess[0])
    state, local, high = call(
        pack_kernel,
        "pack",
        0,
        (jnp.concatenate([sent, feed_rate[None], kill_rate[None]]),),
        [(2, n_y * n_x, n_z), (4, n_y * n_x, n_z), (4, BELOW * n_x, n_z)],
    )
    got = [shifted(state, 1, 0, 0), local]
    got += [shifted(local, 1, -gy, 0) for gy in range(1, n_gy)]
    below = [shifted(high, 1, -gy, 1) for gy in range(n_gy)]

    tile, window = (2, n_y * width, n_z), (2, (TAKE + n_y) * width, n_z)
    nodes_only = [(2, (n_y + 2 * RATE_HALO) * width, n_z), tile, tile]
    edge = lambda rows, more=0: [(2, rows * width, n_z), ((4 * rows + more) * width, n_z)]
    inner_first = call(
        functools.partial(first_inner_kernel, n_gy, n_x, n_y),
        "inner_first",
        0,
        got,
        [tile, tile, *inner_shapes(width, n_y, n_z, DRIFT)],
    )
    start, params, *nodes = call(
        functools.partial(first_kernel, n_gy, n_x, n_y),
        "first",
        0,
        [*inner_first, *below],
        [window, window, *nodes_only, *edge(TAKE, 4 * HALO)],
    )
    zero, one, two, two_edge, pair_edge = nodes
    got = [shifted(two, 1, 0, 0), shifted(two_edge, 1, 0, -1), shifted(pair_edge, 0, 0, -1)]
    known_edge = got[-1]

    def inner(tile_first):
        return call(
            functools.partial(inner_kernel, width, n_y, tile_first),
            "inner",
            1,
            (is_first, start, params, *nodes[:3], got[0]),
            inner_shapes(width, n_y, n_z, tile_first),
        )

    nodes = call(
        functools.partial(second_kernel, width, n_y),
        "second",
        1,
        (is_first, start, params, *inner(-DRIFT), zero, one, two, *got),
        [*nodes_only, *edge(HALO), *edge(HALO)],
    )
    for sweep_index in range(2, ITERS):
        zero, one, two, two_low, pair_low, two_high, pair_high = nodes
        got = [shifted(two, 1, 0, 0), shifted(two_high, 1, 0, 1), shifted(two_low, 1, 0, -1)]
        got += [shifted(pair_high, 0, 0, 1), shifted(pair_low, 0, 0, -1)]
        done = sweep_index + 1 == ITERS
        nodes = call(
            functools.partial(later_kernel, width, n_y, n_x if done else None),
            "last" if done else "later",
            1,
            (is_first, start, params, known_edge, *inner(0), zero, one, two, *got),
            [initial_state.shape] if done else [*nodes_only, *edge(HALO), *edge(HALO)],
            [pltpu.VMEM(tile, jnp.float32)] if done else (),
        )
    return nodes[0][None]


def solution(mesh):
    in_specs = (
        P(None, "gy", "gx", None),
        P("tm", None, "gy", "gx", None),
        P("gy", "gx", None),
        P("gy", "gx", None),
    )
    out_specs = P("tm", None, "gy", "gx", None)
    return jax.shard_map(shards, mesh=mesh, in_specs=in_specs, out_specs=out_specs, check_vma=False)
```

```python
import functools

import jax
import jax.numpy as jnp
from jax import lax
from jax.experimental import pallas as pl
from jax.experimental.pallas import tpu as pltpu
from jax.sharding import PartitionSpec as P

ITERS = 3
DIFF_U = 0.2
DIFF_V = 0.1
HALF_STEP = 0.5
WEIGHTS = ((5.0 / 24.0, 8.0 / 24.0, -1.0 / 24.0), (-1.0 / 24.0, 8.0 / 24.0, 5.0 / 24.0))

AXES = ("tm", "gy", "gx")
HALO = 5
RATE_HALO = 4
DRIFT = 6
TAKE = HALO + DRIFT
BELOW = TAKE + 1


def shifted(value, by_tm, by_gy, by_gx):
    n_tm, n_gy, n_gx = (lax.axis_size(axis) for axis in AXES)
    pairs = []
    for t in range(n_tm):
        for y in range(n_gy):
            for x in range(n_gx):
                target = ((t + by_tm) % n_tm * n_gy + (y + by_gy) % n_gy) * n_gx + (x + by_gx) % n_gx
                pairs.append(((t * n_gy + y) * n_gx + x, target))
    return lax.ppermute(value, AXES, pairs)


def near(row, distance, axis):
    size = row.shape[axis]
    return pltpu.roll(row, distance % size, axis) + pltpu.roll(row, -distance % size, axis)


def rates_of(state, feed, feed_kill, spacing):
    scale = 1.0 / (spacing * spacing)

    @functools.cache
    def at(r):
        (u, v), (ub, vb), (ua, va) = state(r), state(r - 1), state(r + 1)
        around_u = (ub + ua) + near(u, int(spacing), 0) + near(u, int(spacing), 1)
        around_v = (vb + va) + near(v, int(spacing), 0) + near(v, int(spacing), 1)
        reaction = u * (v * v)
        rate_u = (DIFF_U * scale) * around_u + feed(r) - (6.0 * DIFF_U * scale + feed(r)) * u - reaction
        rate_v = (DIFF_V * scale) * around_v - (6.0 * DIFF_V * scale + feed_kill(r)) * v + reaction
        return rate_u, rate_v

    return at


def half_sum(low, high):
    x, z = low.shape
    total = low + high
    total = total + pltpu.roll(total, z - 1, 1)
    total = total + pltpu.roll(total, x - 1, 0)
    return 0.125 * total


def restricted(state):
    @functools.cache
    def at(c):
        return tuple(half_sum(a, b) for a, b in zip(state(2 * c), state(2 * c + 1)))

    return at


def spread(row):
    even_x = lax.broadcasted_iota(jnp.int32, row.shape, 0) % 2 == 0
    even_z = lax.broadcasted_iota(jnp.int32, row.shape, 1) % 2 == 0
    row = jnp.where(even_z, row, pltpu.roll(row, 1, 1))
    return jnp.where(even_x, row, pltpu.roll(row, 1, 0))


def quadrature(values, interval):
    def at(r):
        zero, one, two = (value(r) for value in values)
        w = WEIGHTS[interval]
        return tuple(w[0] * a + w[1] * b + w[2] * c for a, b, c in zip(zero, one, two))

    return at


INNER_COUNT = 11


def inner_rows(n_y, tile_first):
    low, high = max(tile_first, -HALO), min(tile_first + n_y, n_y + HALO)
    halves = lambda first, last: (-(-first // 2), last // 2)
    clip = lambda rows, by: (max(rows[0], -by), min(rows[1], n_y // 2 + by))
    inside = lambda rows: (rows[0] + 1, rows[1] - 1)
    fine = [(low + k, high - k) for k in (1, 1, 2, 2, 3)]
    start, one, integral = halves(low, high), halves(*fine[1]), halves(*fine[4])
    coarse = [clip(start, 2), clip(one, 1), clip(integral, 1), clip(integral, 0)]
    return [*fine, *coarse, clip(inside(start), 1), clip(inside(one), 0)]


def inner_shapes(width, n_y, n_z, tile_first):
    return [(2, (high - low) * width, n_z) for low, high in inner_rows(n_y, tile_first)]


def inner_of(refs, width, n_y, tile_first):
    return [(low, high, rows_of(ref, width, low)) for (low, high), ref in zip(inner_rows(n_y, tile_first), refs)]


def write_inner(values, width, n_y, tile_first, refs):
    items = []
    for i, ((low, high), rows, ref) in enumerate(zip(inner_rows(n_y, tile_first), values, refs)):
        for r in range(low, high):
            ready = r + (0, 0, 1, 1, 2)[i] if i < 5 else 2 * r + (1, 1, 3, 3, 3, 3)[i - 5]
            items.append((ready, i, r, rows, ref, low))
    for _, _, r, rows, ref, low in sorted(items, key=lambda item: item[:3]):
        for field, value in enumerate(rows(r)):
            ref[field, pl.ds((r - low) * width, width), :] = value


def old_terms(rates):
    def term(interval):
        @functools.cache
        def at(r):
            return tuple(q - HALF_STEP * f for q, f in zip(quadrature(rates, interval)(r), rates[interval](r)))

        return at

    return term(0), term(1)


def rim_rows(n_y, tile_first):
    needed = ((-RATE_HALO, n_y + RATE_HALO), (1 - RATE_HALO, n_y + RATE_HALO - 1))
    inner = (inner_rows(n_y, tile_first)[place] for place in (1, 3))
    return [[r for r in range(*every) if not low <= r < high] for every, (low, high) in zip(needed, inner)]


def write_rim(terms, width, n_y, tile_first, refs):
    places = [(r, i, k) for i, rows in enumerate(rim_rows(n_y, tile_first)) for k, r in enumerate(rows)]
    for r, i, k in sorted(places):
        for field, value in enumerate(terms[i](r)):
            refs[i][field, pl.ds(k * width, width), :] = value


def rim_of(refs, width, n_y, tile_first):
    def one(ref, rows):
        return lambda r: rows_of(ref, width, 0)(rows.index(r))

    return [one(ref, rows) for ref, rows in zip(refs, rim_rows(n_y, tile_first))]


def iteration(start, feed, kill, terms, inner=()):
    inner = iter(inner)

    def known_or(values):
        low, high, known = next(inner, (0, 0, None))
        return lambda r: (known if low <= r < high else values)(r)

    feed_kill = functools.cache(lambda r: feed(r) + kill(r))
    coarse_feed = functools.cache(lambda c: half_sum(feed(2 * c), feed(2 * c + 1)))
    coarse_sum = functools.cache(lambda c: half_sum(feed_kill(2 * c), feed_kill(2 * c + 1)))

    def stepped(state, rate, interval):
        @functools.cache
        def at(r):
            out = [s + HALF_STEP * f for s, f in zip(state(r), rate(r))]
            if terms is not None:
                out = [o + term for o, term in zip(out, terms[interval](r))]
            return tuple(out)

        return at

    fine = lambda state: rates_of(state, feed, feed_kill, 1.0)
    coarse = lambda state: rates_of(state, coarse_feed, coarse_sum, 2.0)
    rate_zero = known_or(fine(start))
    node_one = known_or(stepped(start, rate_zero, 0))
    rate_one = known_or(fine(node_one))
    node_two = known_or(stepped(node_one, rate_one, 1))
    rate_two = known_or(fine(node_two))
    fresh = (rate_zero, rate_one, rate_two)
    rest_zero, rest_one, rest_two = known_or(restricted(start)), known_or(restricted(node_one)), restricted(node_two)
    rest_integral = [known_or(restricted(quadrature(fresh, interval))) for interval in (0, 1)]
    rate_rest_zero, rate_rest_one = known_or(coarse(rest_zero)), known_or(coarse(rest_one))
    coarse_start, rate_coarse_start = rest_zero, rate_rest_zero

    def coarse_stepped(state, rate, rest_rate, integral):
        @functools.cache
        def at(c):
            return tuple(
                s + HALF_STEP * (f - g) + q for s, f, g, q in zip(state(c), rate(c), rest_rate(c), integral(c))
            )

        return at

    coarse_one = coarse_stepped(coarse_start, rate_coarse_start, rate_rest_zero, rest_integral[0])
    coarse_two = coarse_stepped(coarse_one, coarse(coarse_one), rate_rest_one, rest_integral[1])

    def corrected(node, coarse_node, rest):
        change = functools.cache(lambda c: tuple(spread(w - m) for w, m in zip(coarse_node(c), rest(c))))

        @functools.cache
        def at(r):
            return tuple(n + d for n, d in zip(node(r), change(r // 2)))

        return at

    nodes = corrected(node_one, coarse_one, rest_one), corrected(node_two, coarse_two, rest_two)
    fine_rows = (rate_zero, node_one, rate_one, node_two, rate_two)
    return (rate_zero, *nodes), (*fine_rows, rest_zero, rest_one, *rest_integral, rate_rest_zero, rate_rest_one)


def rows_of(ref, width, first):
    @functools.cache
    def at(r):
        assert 0 <= (r - first) * width < ref.shape[1]
        return tuple(ref[field, pl.ds((r - first) * width, width), :] for field in range(2))

    return at


def pack_kernel(tiles_ref, state_ref, all_ref, high_ref):
    n_fields, n_x, n_y, _ = tiles_ref.shape
    for field in range(n_fields):
        for x in range(n_x):
            all_ref[field, pl.ds(x, n_y, stride=n_x), :] = tiles_ref[field, x]
        high_ref[field] = all_ref[field, pl.ds((n_y - BELOW) * n_x, BELOW * n_x), :]
    for field in range(2):
        state_ref[field] = all_ref[field]


def collect(out_ref, field, source_field, n_x, lowest, pieces):
    width = n_x * len(pieces[0][1])
    for first, refs, count in pieces:
        for gy, ref in enumerate(refs):
            for k in range(count):
                if first + k >= lowest:
                    place = pl.ds((first + k - lowest) * width + gy * n_x, n_x)
                    out_ref[field, place, :] = ref[source_field, pl.ds(k * n_x, n_x), :]


def first_inner_kernel(n_gy, n_x, n_y, *refs):
    state_ref, local_ref = refs[:2]
    others = refs[2 : 1 + n_gy]
    start_ref, params_ref, *outs = refs[1 + n_gy :]
    width = n_gy * n_x
    for field in range(2):
        collect(start_ref, field, field, n_x, 0, [(0, [state_ref, *others], n_y)])
        collect(params_ref, field, 2 + field, n_x, 0, [(0, [local_ref, *others], n_y)])
    start, params = rows_of(start_ref, width, DRIFT), rows_of(params_ref, width, DRIFT)
    _, values = iteration(start, lambda r: params(r)[0], lambda r: params(r)[1], None)
    write_inner(values, width, n_y, DRIFT, outs)


def first_kernel(n_gy, n_x, n_y, *refs):
    tiles, inner_refs, refs = refs[:2], refs[2 : 2 + INNER_COUNT], refs[2 + INNER_COUNT :]
    lows, (start_ref, params_ref, *outs) = refs[:n_gy], refs[n_gy:]
    width = n_gy * n_x
    for field in range(2):
        for out_ref, tile_ref, place in zip((start_ref, params_ref), tiles, (0, 2)):
            collect(out_ref, field, place + field, n_x, -TAKE, [(-BELOW, lows, BELOW)])
            out_ref[field, pl.ds(TAKE * width, n_y * width), :] = tile_ref[field]
    start = rows_of(start_ref, width, -HALO)
    params = rows_of(params_ref, width, -HALO)
    inner = inner_of(inner_refs, width, n_y, DRIFT)
    results, _ = iteration(start, lambda r: params(r)[0], lambda r: params(r)[1], None, inner)
    write_nodes(results, width, n_y, [(0, TAKE)], *outs)
    for r in range(HALO):
        for field, value in enumerate((*start(r + DRIFT), *params(r + DRIFT))):
            outs[-1][pl.ds((4 * TAKE + field * HALO + r) * width, width), :] = value


def write_nodes(results, width, n_y, edges, zero_ref, one_ref, two_ref, *edge_refs):
    rate_zero, node_one, node_two = results
    for r in range(-RATE_HALO, n_y + RATE_HALO):
        if 0 <= r < n_y:
            place = pl.ds(r * width, width)
            for field, (one, two) in enumerate(zip(node_one(r), node_two(r))):
                one_ref[field, place, :] = one
                two_ref[field, place, :] = two
                for i, (first, count) in enumerate(edges):
                    if first <= r < first + count:
                        beside = pl.ds((r - first) * width, width)
                        edge_refs[2 * i][field, beside, :] = two
                        for at, value in ((field, one), (2 + field, two)):
                            edge_refs[2 * i + 1][pl.ds((at * count + r - first) * width, width), :] = value
        for field, zero in enumerate(rate_zero(r)):
            zero_ref[field, pl.ds((r + RATE_HALO) * width, width), :] = zero


def joined(*parts):
    def at(r):
        return [rows for first, rows in parts if first <= r][-1](r)

    return at


def flat_rows(ref, width, place, first, count):
    @functools.cache
    def at(r):
        assert 0 <= r - first < count
        return tuple(ref[pl.ds((place + field * count + r - first) * width, width), :] for field in range(2))

    return at


def known(width, n_y, start_ref, params_ref, edge_ref):
    return (
        joined(
            (-TAKE, rows_of(ref, width, -TAKE)), (n_y, flat_rows(edge_ref, width, 4 * TAKE + place * HALO, n_y, HALO))
        )
        for ref, place in ((start_ref, 0), (params_ref, 2))
    )


def later_iteration(is_first, kept, params, got, terms, inner=()):
    @functools.cache
    def start(r):
        return tuple(jnp.where(is_first, a, b) for a, b in zip(kept(r), got(r)))

    return iteration(start, lambda r: params(r)[0], lambda r: params(r)[1], terms, inner)


def terms_of(params, old_zero, ones, twos):
    feed = lambda r: params(r)[0]
    feed_kill = functools.cache(lambda r: params(r)[0] + params(r)[1])
    return old_terms((old_zero(feed, feed_kill), *(rates_of(rows, feed, feed_kill, 1.0) for rows in (ones, twos))))


def inner_kernel(width, n_y, tile_first, first_ref, start_ref, params_ref, zero_ref, one_ref, two_ref, got_ref, *outs):
    kept, params = rows_of(start_ref, width, -TAKE), rows_of(params_ref, width, -TAKE)
    old_zero = rows_of(zero_ref, width, tile_first - RATE_HALO)
    ones, twos, got = (rows_of(ref, width, tile_first) for ref in (one_ref, two_ref, got_ref))
    terms = terms_of(params, lambda feed, feed_kill: old_zero, ones, twos)
    _, values = later_iteration(first_ref[0] == 1, kept, params, got, terms)
    write_inner(values, width, n_y, tile_first, outs)


def moved(width, n_y, tile_ref, beside):
    return joined((-DRIFT, rows_of(tile_ref, width, -DRIFT)), (n_y - DRIFT, beside))


def second_rim_kernel(width, n_y, start_ref, params_ref, zero_ref, one_ref, two_ref, pair_edge, *outs):
    kept, params = known(width, n_y, start_ref, params_ref, pair_edge)
    end = n_y - DRIFT
    ones, twos = (
        moved(width, n_y, ref, flat_rows(pair_edge, width, place * TAKE, end, TAKE))
        for ref, place in ((one_ref, 0), (two_ref, 2))
    )

    def old_zero(feed, feed_kill):
        inside = rows_of(zero_ref, width, -RATE_HALO - DRIFT)
        return joined((-RATE_HALO - DRIFT, inside), (end + RATE_HALO, rates_of(kept, feed, feed_kill, 1.0)))

    write_rim(terms_of(params, old_zero, ones, twos), width, n_y, -DRIFT, outs)


def second_kernel(width, n_y, first_ref, start_ref, params_ref, *refs):
    inner = inner_of(refs, width, n_y, -DRIFT)
    terms = rim_of(refs[INNER_COUNT:], width, n_y, -DRIFT)
    got_ref, got_edge, pair_edge, *outs = refs[INNER_COUNT + 2 :]
    kept, params = known(width, n_y, start_ref, params_ref, pair_edge)
    got = moved(width, n_y, got_ref, rows_of(got_edge, width, n_y - DRIFT))
    results, _ = later_iteration(first_ref[0] == 1, kept, params, got, terms, inner)
    write_nodes(results, width, n_y, [(0, HALO), (n_y - HALO, HALO)], *outs)


def window(width, n_y, low, tile_ref, high):
    return joined((-HALO, low), (0, rows_of(tile_ref, width, 0)), (n_y, high))


def later_rim_kernel(
    width, n_y, start_ref, params_ref, known_ref, zero_ref, one_ref, two_ref, pair_low, pair_high, *outs
):
    _, params = known(width, n_y, start_ref, params_ref, known_ref)

    def pair(tile_ref, place):
        low, high = (
            flat_rows(ref, width, place * HALO, first, HALO) for ref, first in ((pair_low, -HALO), (pair_high, n_y))
        )
        return window(width, n_y, low, tile_ref, high)

    old_zero = rows_of(zero_ref, width, -RATE_HALO)
    terms = terms_of(params, lambda feed, feed_kill: old_zero, pair(one_ref, 0), pair(two_ref, 2))
    write_rim(terms, width, n_y, 0, outs)


def later_kernel(width, n_y, out_x, first_ref, start_ref, params_ref, known_ref, *refs):
    inner = inner_of(refs, width, n_y, 0)
    terms = rim_of(refs[INNER_COUNT:], width, n_y, 0)
    got_ref, got_low, got_high, *outs = refs[INNER_COUNT + 2 :]
    kept, params = known(width, n_y, start_ref, params_ref, known_ref)
    got = window(width, n_y, rows_of(got_low, width, -HALO), got_ref, rows_of(got_high, width, n_y))
    results, _ = later_iteration(first_ref[0] == 1, kept, params, got, terms, inner)
    if out_x is None:
        write_nodes(results, width, n_y, [(0, HALO), (n_y - HALO, HALO)], *outs)
    else:
        out_ref, scratch = outs
        for r in range(n_y):
            for field, value in enumerate(results[2](r)):
                scratch[field, pl.ds(r * width, width), :] = value
        for x in range(out_x):
            for field in range(2):
                out_ref[field, x] = scratch[field, pl.ds(x, n_y, stride=width), :]


def call(kernel, name, n_scalars, operands, shapes, scratch=()):
    specs = [pl.BlockSpec(memory_space=pltpu.SMEM)] * n_scalars
    specs += [pl.BlockSpec(memory_space=pltpu.VMEM)] * (len(operands) - n_scalars)
    return pl.pallas_call(
        kernel,
        name=name,
        out_shape=[jax.ShapeDtypeStruct(shape, jnp.float32) for shape in shapes],
        in_specs=specs,
        out_specs=[pl.BlockSpec(memory_space=pltpu.VMEM)] * len(shapes),
        scratch_shapes=scratch,
        compiler_params=pltpu.CompilerParams(vmem_limit_bytes=32 * 1024 * 1024),
    )(*operands)


def shards(initial_state, slice_guess, feed_rate, kill_rate):
    n_gy, n_tm = lax.axis_size("gy"), lax.axis_size("tm")
    _, n_x, n_y, n_z = initial_state.shape
    width = n_gy * n_x
    place = lax.axis_index("tm")
    is_first = (place == 0).astype(jnp.int32)[None]

    sent = jnp.where(place == n_tm - 1, initial_state, slice_guess[0])
    state, local, high = call(
        pack_kernel,
        "pack",
        0,
        (jnp.concatenate([sent, feed_rate[None], kill_rate[None]]),),
        [(2, n_y * n_x, n_z), (4, n_y * n_x, n_z), (4, BELOW * n_x, n_z)],
    )
    got = [shifted(state, 1, 0, 0), local]
    got += [shifted(local, 1, -gy, 0) for gy in range(1, n_gy)]
    below = [shifted(high, 1, -gy, 1) for gy in range(n_gy)]

    tile, window = (2, n_y * width, n_z), (2, (TAKE + n_y) * width, n_z)
    nodes_only = [(2, (n_y + 2 * RATE_HALO) * width, n_z), tile, tile]
    edge = lambda rows, more=0: [(2, rows * width, n_z), ((4 * rows + more) * width, n_z)]
    inner_first = call(
        functools.partial(first_inner_kernel, n_gy, n_x, n_y),
        "inner_first",
        0,
        got,
        [tile, tile, *inner_shapes(width, n_y, n_z, DRIFT)],
    )
    start, params, *nodes = call(
        functools.partial(first_kernel, n_gy, n_x, n_y),
        "first",
        0,
        [*inner_first, *below],
        [window, window, *nodes_only, *edge(TAKE, 4 * HALO)],
    )
    zero, one, two, two_edge, pair_edge = nodes
    got = [shifted(two, 1, 0, 0), shifted(two_edge, 1, 0, -1), shifted(pair_edge, 0, 0, -1)]
    known_edge = got[-1]

    def inner(tile_first):
        return call(
            functools.partial(inner_kernel, width, n_y, tile_first),
            "inner",
            1,
            (is_first, start, params, *nodes[:3], got[0]),
            inner_shapes(width, n_y, n_z, tile_first),
        )

    def rim(kernel, name, tile_first, operands):
        shapes = [(2, len(rows) * width, n_z) for rows in rim_rows(n_y, tile_first)]
        return call(functools.partial(kernel, width, n_y), name, 0, operands, shapes)

    zero, one, two = nodes[:3]
    second_rim = rim(second_rim_kernel, "second_rim", -DRIFT, (start, params, zero, one, two, known_edge))
    nodes = call(
        functools.partial(second_kernel, width, n_y),
        "second",
        1,
        (is_first, start, params, *inner(-DRIFT), *second_rim, *got),
        [*nodes_only, *edge(HALO), *edge(HALO)],
    )
    for sweep_index in range(2, ITERS):
        zero, one, two, two_low, pair_low, two_high, pair_high = nodes
        got = [shifted(two, 1, 0, 0), shifted(two_high, 1, 0, 1), shifted(two_low, 1, 0, -1)]
        got += [shifted(pair_high, 0, 0, 1), shifted(pair_low, 0, 0, -1)]
        done = sweep_index + 1 == ITERS
        later_rim = rim(later_rim_kernel, "later_rim", 0, (start, params, known_edge, zero, one, two, *got[3:]))
        nodes = call(
            functools.partial(later_kernel, width, n_y, n_x if done else None),
            "last" if done else "later",
            1,
            (is_first, start, params, known_edge, *inner(0), *later_rim, *got[:3]),
            [initial_state.shape] if done else [*nodes_only, *edge(HALO), *edge(HALO)],
            [pltpu.VMEM(tile, jnp.float32)] if done else (),
        )
    return nodes[0][None]


def solution(mesh):
    in_specs = (
        P(None, "gy", "gx", None),
        P("tm", None, "gy", "gx", None),
        P("gy", "gx", None),
        P("gy", "gx", None),
    )
    out_specs = P("tm", None, "gy", "gx", None)
    return jax.shard_map(shards, mesh=mesh, in_specs=in_specs, out_specs=out_specs, check_vma=False)
```

```python
import functools

import jax
import jax.numpy as jnp
from jax import lax
from jax.experimental import pallas as pl
from jax.experimental.pallas import tpu as pltpu
from jax.sharding import PartitionSpec as P

ITERS = 3
DIFF_U = 0.2
DIFF_V = 0.1
HALF_STEP = 0.5
WEIGHTS = ((5.0 / 24.0, 8.0 / 24.0, -1.0 / 24.0), (-1.0 / 24.0, 8.0 / 24.0, 5.0 / 24.0))

AXES = ("tm", "gy", "gx")
HALO = 5
RATE_HALO = 4
DRIFT = 6
TAKE = HALO + DRIFT
BELOW = (TAKE, TAKE, TAKE - 1, TAKE - 1)


def shifted(value, by_tm, by_gy, by_gx):
    n_tm, n_gy, n_gx = (lax.axis_size(axis) for axis in AXES)
    pairs = []
    for t in range(n_tm):
        for y in range(n_gy):
            for x in range(n_gx):
                target = ((t + by_tm) % n_tm * n_gy + (y + by_gy) % n_gy) * n_gx + (x + by_gx) % n_gx
                pairs.append(((t * n_gy + y) * n_gx + x, target))
    return lax.ppermute(value, AXES, pairs)


def near(row, distance, axis):
    size = row.shape[axis]
    return pltpu.roll(row, distance % size, axis) + pltpu.roll(row, -distance % size, axis)


def rates_of(state, feed, feed_kill, spacing):
    scale = 1.0 / (spacing * spacing)

    @functools.cache
    def at(r):
        (u, v), (ub, vb), (ua, va) = state(r), state(r - 1), state(r + 1)
        around_u = (ub + ua) + near(u, int(spacing), 0) + near(u, int(spacing), 1)
        around_v = (vb + va) + near(v, int(spacing), 0) + near(v, int(spacing), 1)
        reaction = u * (v * v)
        rate_u = (DIFF_U * scale) * around_u + feed(r) - (6.0 * DIFF_U * scale + feed(r)) * u - reaction
        rate_v = (DIFF_V * scale) * around_v - (6.0 * DIFF_V * scale + feed_kill(r)) * v + reaction
        return rate_u, rate_v

    return at


def half_sum(low, high):
    x, z = low.shape
    total = low + high
    total = total + pltpu.roll(total, z - 1, 1)
    total = total + pltpu.roll(total, x - 1, 0)
    return 0.125 * total


def restricted(state):
    @functools.cache
    def at(c):
        return tuple(half_sum(a, b) for a, b in zip(state(2 * c), state(2 * c + 1)))

    return at


def spread(row):
    even_x = lax.broadcasted_iota(jnp.int32, row.shape, 0) % 2 == 0
    even_z = lax.broadcasted_iota(jnp.int32, row.shape, 1) % 2 == 0
    row = jnp.where(even_z, row, pltpu.roll(row, 1, 1))
    return jnp.where(even_x, row, pltpu.roll(row, 1, 0))


def quadrature(values, interval):
    def at(r):
        zero, one, two = (value(r) for value in values)
        w = WEIGHTS[interval]
        return tuple(w[0] * a + w[1] * b + w[2] * c for a, b, c in zip(zero, one, two))

    return at


INNER_COUNT = 11


def inner_rows(n_y, tile_first):
    low, high = max(tile_first, -HALO), min(tile_first + n_y, n_y + HALO)
    halves = lambda first, last: (-(-first // 2), last // 2)
    clip = lambda rows, by: (max(rows[0], -by), min(rows[1], n_y // 2 + by))
    inside = lambda rows: (rows[0] + 1, rows[1] - 1)
    fine = [(low + k, high - k) for k in (1, 1, 2, 2, 3)]
    start, one, integral = halves(low, high), halves(*fine[1]), halves(*fine[4])
    coarse = [clip(start, 2), clip(one, 1), clip(integral, 1), clip(integral, 0)]
    return [*fine, *coarse, clip(inside(start), 1), clip(inside(one), 0)]


def inner_shapes(width, n_y, n_z, tile_first):
    return [(2, (high - low) * width, n_z) for low, high in inner_rows(n_y, tile_first)]


def inner_of(refs, width, n_y, tile_first):
    return [(low, high, rows_of(ref, width, low)) for (low, high), ref in zip(inner_rows(n_y, tile_first), refs)]


def write_inner(values, width, n_y, tile_first, refs):
    items = []
    for i, ((low, high), rows, ref) in enumerate(zip(inner_rows(n_y, tile_first), values, refs)):
        for r in range(low, high):
            ready = r + (0, 0, 1, 1, 2)[i] if i < 5 else 2 * r + (1, 1, 3, 3, 3, 3)[i - 5]
            items.append((ready, i, r, rows, ref, low))
    for _, _, r, rows, ref, low in sorted(items, key=lambda item: item[:3]):
        for field, value in enumerate(rows(r)):
            ref[field, pl.ds((r - low) * width, width), :] = value


def old_terms(rates):
    def term(interval):
        @functools.cache
        def at(r):
            return tuple(q - HALF_STEP * f for q, f in zip(quadrature(rates, interval)(r), rates[interval](r)))

        return at

    return term(0), term(1)


def rim_rows(n_y, tile_first):
    needed = ((-RATE_HALO, n_y + RATE_HALO), (1 - RATE_HALO, n_y + RATE_HALO - 1))
    inner = (inner_rows(n_y, tile_first)[place] for place in (1, 3))
    return [[r for r in range(*every) if not low <= r < high] for every, (low, high) in zip(needed, inner)]


def write_rim(terms, width, n_y, tile_first, refs):
    places = [(r, i, k) for i, rows in enumerate(rim_rows(n_y, tile_first)) for k, r in enumerate(rows)]
    for r, i, k in sorted(places):
        for field, value in enumerate(terms[i](r)):
            refs[i][field, pl.ds(k * width, width), :] = value


def rim_of(refs, width, n_y, tile_first):
    def one(ref, rows):
        return lambda r: rows_of(ref, width, 0)(rows.index(r))

    return [one(ref, rows) for ref, rows in zip(refs, rim_rows(n_y, tile_first))]


def iteration(start, feed, kill, terms, inner=()):
    inner = iter(inner)

    def known_or(values):
        low, high, known = next(inner, (0, 0, None))
        return lambda r: (known if low <= r < high else values)(r)

    feed_kill = functools.cache(lambda r: feed(r) + kill(r))
    coarse_feed = functools.cache(lambda c: half_sum(feed(2 * c), feed(2 * c + 1)))
    coarse_sum = functools.cache(lambda c: half_sum(feed_kill(2 * c), feed_kill(2 * c + 1)))

    def stepped(state, rate, interval):
        @functools.cache
        def at(r):
            out = [s + HALF_STEP * f for s, f in zip(state(r), rate(r))]
            if terms is not None:
                out = [o + term for o, term in zip(out, terms[interval](r))]
            return tuple(out)

        return at

    fine = lambda state: rates_of(state, feed, feed_kill, 1.0)
    coarse = lambda state: rates_of(state, coarse_feed, coarse_sum, 2.0)
    rate_zero = known_or(fine(start))
    node_one = known_or(stepped(start, rate_zero, 0))
    rate_one = known_or(fine(node_one))
    node_two = known_or(stepped(node_one, rate_one, 1))
    rate_two = known_or(fine(node_two))
    fresh = (rate_zero, rate_one, rate_two)
    rest_zero, rest_one, rest_two = known_or(restricted(start)), known_or(restricted(node_one)), restricted(node_two)
    rest_integral = [known_or(restricted(quadrature(fresh, interval))) for interval in (0, 1)]
    rate_rest_zero, rate_rest_one = known_or(coarse(rest_zero)), known_or(coarse(rest_one))
    coarse_start, rate_coarse_start = rest_zero, rate_rest_zero

    def coarse_stepped(state, rate, rest_rate, integral):
        @functools.cache
        def at(c):
            return tuple(
                s + HALF_STEP * (f - g) + q for s, f, g, q in zip(state(c), rate(c), rest_rate(c), integral(c))
            )

        return at

    coarse_one = coarse_stepped(coarse_start, rate_coarse_start, rate_rest_zero, rest_integral[0])
    coarse_two = coarse_stepped(coarse_one, coarse(coarse_one), rate_rest_one, rest_integral[1])

    def corrected(node, coarse_node, rest):
        change = functools.cache(lambda c: tuple(spread(w - m) for w, m in zip(coarse_node(c), rest(c))))

        @functools.cache
        def at(r):
            return tuple(n + d for n, d in zip(node(r), change(r // 2)))

        return at

    nodes = corrected(node_one, coarse_one, rest_one), corrected(node_two, coarse_two, rest_two)
    fine_rows = (rate_zero, node_one, rate_one, node_two, rate_two)
    return (rate_zero, *nodes), (*fine_rows, rest_zero, rest_one, *rest_integral, rate_rest_zero, rate_rest_one)


def rows_of(ref, width, first):
    @functools.cache
    def at(r):
        assert 0 <= (r - first) * width < ref.shape[1]
        return tuple(ref[field, pl.ds((r - first) * width, width), :] for field in range(2))

    return at


def pack_kernel(tiles_ref, state_ref, all_ref, high_ref):
    n_fields, n_x, n_y, _ = tiles_ref.shape
    for field in range(n_fields):
        for x in range(n_x):
            all_ref[field, pl.ds(x, n_y, stride=n_x), :] = tiles_ref[field, x]
        count = BELOW[field]
        rows = all_ref[field, pl.ds((n_y - count) * n_x, count * n_x), :]
        high_ref[pl.ds(sum(BELOW[:field]) * n_x, count * n_x), :] = rows
    for field in range(2):
        state_ref[field] = all_ref[field]


def collect(out_ref, field, source_field, n_x, lowest, pieces):
    width = n_x * len(pieces[0][1])
    for first, refs, count in pieces:
        for gy, ref in enumerate(refs):
            for k in range(count):
                if first + k >= lowest:
                    place = pl.ds((first + k - lowest) * width + gy * n_x, n_x)
                    out_ref[field, place, :] = ref[source_field, pl.ds(k * n_x, n_x), :]


def first_inner_kernel(n_gy, n_x, n_y, *refs):
    state_ref, local_ref = refs[:2]
    others = refs[2 : 1 + n_gy]
    start_ref, params_ref, *outs = refs[1 + n_gy :]
    width = n_gy * n_x
    for field in range(2):
        collect(start_ref, field, field, n_x, 0, [(0, [state_ref, *others], n_y)])
        collect(params_ref, field, 2 + field, n_x, 0, [(0, [local_ref, *others], n_y)])
    start, params = rows_of(start_ref, width, DRIFT), rows_of(params_ref, width, DRIFT)
    _, values = iteration(start, lambda r: params(r)[0], lambda r: params(r)[1], None)
    write_inner(values, width, n_y, DRIFT, outs)


def first_kernel(n_gy, n_x, n_y, *refs):
    tiles, inner_refs, refs = refs[:2], refs[2 : 2 + INNER_COUNT], refs[2 + INNER_COUNT :]
    lows, (start_ref, params_ref, *outs) = refs[:n_gy], refs[n_gy:]
    width = n_gy * n_x
    for field in range(2):
        for out_ref, tile_ref, place in zip((start_ref, params_ref), tiles, (0, 2)):
            count, begin = BELOW[place + field], sum(BELOW[: place + field])
            for gy, low_ref in enumerate(lows):
                for k in range(count):
                    row = pl.ds((TAKE - count + k) * width + gy * n_x, n_x)
                    out_ref[field, row, :] = low_ref[pl.ds((begin + k) * n_x, n_x), :]
            out_ref[field, pl.ds(TAKE * width, n_y * width), :] = tile_ref[field]
    start = rows_of(start_ref, width, -HALO)
    params = rows_of(params_ref, width, -HALO)
    inner = inner_of(inner_refs, width, n_y, DRIFT)
    results, _ = iteration(start, lambda r: params(r)[0], lambda r: params(r)[1], None, inner)
    write_nodes(results, width, n_y, [(0, TAKE)], *outs)
    for rows, place, count in ((start, 4 * TAKE, HALO), (params, 4 * TAKE + 2 * HALO, RATE_HALO)):
        for r in range(count):
            for field, value in enumerate(rows(r + DRIFT)):
                outs[-1][pl.ds((place + field * count + r) * width, width), :] = value


def write_nodes(results, width, n_y, edges, zero_ref, one_ref, two_ref, *edge_refs):
    rate_zero, node_one, node_two = results
    for r in range(-RATE_HALO, n_y + RATE_HALO):
        if 0 <= r < n_y:
            place = pl.ds(r * width, width)
            for field, (one, two) in enumerate(zip(node_one(r), node_two(r))):
                one_ref[field, place, :] = one
                two_ref[field, place, :] = two
                for i, (first, count) in enumerate(edges):
                    if first <= r < first + count:
                        beside = pl.ds((r - first) * width, width)
                        edge_refs[2 * i][field, beside, :] = two
                        for at, value in ((field, one), (2 + field, two)):
                            edge_refs[2 * i + 1][pl.ds((at * count + r - first) * width, width), :] = value
        for field, zero in enumerate(rate_zero(r)):
            zero_ref[field, pl.ds((r + RATE_HALO) * width, width), :] = zero


def joined(*parts):
    def at(r):
        return [rows for first, rows in parts if first <= r][-1](r)

    return at


def flat_rows(ref, width, place, first, count):
    @functools.cache
    def at(r):
        assert 0 <= r - first < count
        return tuple(ref[pl.ds((place + field * count + r - first) * width, width), :] for field in range(2))

    return at


def known(width, n_y, start_ref, params_ref, edge_ref):
    return (
        joined((-TAKE, rows_of(ref, width, -TAKE)), (n_y, flat_rows(edge_ref, width, place, n_y, count)))
        for ref, place, count in ((start_ref, 4 * TAKE, HALO), (params_ref, 4 * TAKE + 2 * HALO, RATE_HALO))
    )


def later_iteration(is_first, kept, params, got, terms, inner=()):
    @functools.cache
    def start(r):
        return tuple(jnp.where(is_first, a, b) for a, b in zip(kept(r), got(r)))

    return iteration(start, lambda r: params(r)[0], lambda r: params(r)[1], terms, inner)


def terms_of(params, old_zero, ones, twos):
    feed = lambda r: params(r)[0]
    feed_kill = functools.cache(lambda r: params(r)[0] + params(r)[1])
    return old_terms((old_zero(feed, feed_kill), *(rates_of(rows, feed, feed_kill, 1.0) for rows in (ones, twos))))


def inner_kernel(width, n_y, tile_first, first_ref, start_ref, params_ref, zero_ref, one_ref, two_ref, got_ref, *outs):
    kept, params = rows_of(start_ref, width, -TAKE), rows_of(params_ref, width, -TAKE)
    old_zero = rows_of(zero_ref, width, tile_first - RATE_HALO)
    ones, twos, got = (rows_of(ref, width, tile_first) for ref in (one_ref, two_ref, got_ref))
    terms = terms_of(params, lambda feed, feed_kill: old_zero, ones, twos)
    _, values = later_iteration(first_ref[0] == 1, kept, params, got, terms)
    write_inner(values, width, n_y, tile_first, outs)


def moved(width, n_y, tile_ref, beside):
    return joined((-DRIFT, rows_of(tile_ref, width, -DRIFT)), (n_y - DRIFT, beside))


def second_rim_kernel(width, n_y, start_ref, params_ref, zero_ref, one_ref, two_ref, pair_edge, *outs):
    kept, params = known(width, n_y, start_ref, params_ref, pair_edge)
    end = n_y - DRIFT
    ones, twos = (
        moved(width, n_y, ref, flat_rows(pair_edge, width, place * TAKE, end, TAKE))
        for ref, place in ((one_ref, 0), (two_ref, 2))
    )

    def old_zero(feed, feed_kill):
        inside = rows_of(zero_ref, width, -RATE_HALO - DRIFT)
        return joined((-RATE_HALO - DRIFT, inside), (end + RATE_HALO, rates_of(kept, feed, feed_kill, 1.0)))

    write_rim(terms_of(params, old_zero, ones, twos), width, n_y, -DRIFT, outs)


def second_kernel(width, n_y, first_ref, start_ref, params_ref, *refs):
    inner = inner_of(refs, width, n_y, -DRIFT)
    terms = rim_of(refs[INNER_COUNT:], width, n_y, -DRIFT)
    got_ref, got_edge, pair_edge, *outs = refs[INNER_COUNT + 2 :]
    kept, params = known(width, n_y, start_ref, params_ref, pair_edge)
    got = moved(width, n_y, got_ref, rows_of(got_edge, width, n_y - DRIFT))
    results, _ = later_iteration(first_ref[0] == 1, kept, params, got, terms, inner)
    write_nodes(results, width, n_y, [(0, HALO), (n_y - HALO, HALO)], *outs)


def window(width, n_y, low, tile_ref, high):
    return joined((-HALO, low), (0, rows_of(tile_ref, width, 0)), (n_y, high))


def later_rim_kernel(
    width, n_y, start_ref, params_ref, known_ref, zero_ref, one_ref, two_ref, pair_low, pair_high, *outs
):
    _, params = known(width, n_y, start_ref, params_ref, known_ref)

    def pair(tile_ref, place):
        low, high = (
            flat_rows(ref, width, place * HALO, first, HALO) for ref, first in ((pair_low, -HALO), (pair_high, n_y))
        )
        return window(width, n_y, low, tile_ref, high)

    old_zero = rows_of(zero_ref, width, -RATE_HALO)
    terms = terms_of(params, lambda feed, feed_kill: old_zero, pair(one_ref, 0), pair(two_ref, 2))
    write_rim(terms, width, n_y, 0, outs)


def later_kernel(width, n_y, out_x, first_ref, start_ref, params_ref, known_ref, *refs):
    inner = inner_of(refs, width, n_y, 0)
    terms = rim_of(refs[INNER_COUNT:], width, n_y, 0)
    got_ref, got_low, got_high, *outs = refs[INNER_COUNT + 2 :]
    kept, params = known(width, n_y, start_ref, params_ref, known_ref)
    got = window(width, n_y, rows_of(got_low, width, -HALO), got_ref, rows_of(got_high, width, n_y))
    results, _ = later_iteration(first_ref[0] == 1, kept, params, got, terms, inner)
    if out_x is None:
        write_nodes(results, width, n_y, [(0, HALO), (n_y - HALO, HALO)], *outs)
    else:
        out_ref, scratch = outs
        for r in range(n_y):
            for field, value in enumerate(results[2](r)):
                scratch[field, pl.ds(r * width, width), :] = value
        for x in range(out_x):
            for field in range(2):
                out_ref[field, x] = scratch[field, pl.ds(x, n_y, stride=width), :]


def call(kernel, name, n_scalars, operands, shapes, scratch=()):
    specs = [pl.BlockSpec(memory_space=pltpu.SMEM)] * n_scalars
    specs += [pl.BlockSpec(memory_space=pltpu.VMEM)] * (len(operands) - n_scalars)
    return pl.pallas_call(
        kernel,
        name=name,
        out_shape=[jax.ShapeDtypeStruct(shape, jnp.float32) for shape in shapes],
        in_specs=specs,
        out_specs=[pl.BlockSpec(memory_space=pltpu.VMEM)] * len(shapes),
        scratch_shapes=scratch,
        compiler_params=pltpu.CompilerParams(vmem_limit_bytes=32 * 1024 * 1024),
    )(*operands)


def shards(initial_state, slice_guess, feed_rate, kill_rate):
    n_gy, n_tm = lax.axis_size("gy"), lax.axis_size("tm")
    _, n_x, n_y, n_z = initial_state.shape
    width = n_gy * n_x
    place = lax.axis_index("tm")
    is_first = (place == 0).astype(jnp.int32)[None]

    sent = jnp.where(place == n_tm - 1, initial_state, slice_guess[0])
    state, local, high = call(
        pack_kernel,
        "pack",
        0,
        (jnp.concatenate([sent, feed_rate[None], kill_rate[None]]),),
        [(2, n_y * n_x, n_z), (4, n_y * n_x, n_z), (sum(BELOW) * n_x, n_z)],
    )
    got = [shifted(state, 1, 0, 0), local]
    got += [shifted(local, 1, -gy, 0) for gy in range(1, n_gy)]
    below = [shifted(high, 1, -gy, 1) for gy in range(n_gy)]

    tile, window = (2, n_y * width, n_z), (2, (TAKE + n_y) * width, n_z)
    nodes_only = [(2, (n_y + 2 * RATE_HALO) * width, n_z), tile, tile]
    edge = lambda rows, more=0: [(2, rows * width, n_z), ((4 * rows + more) * width, n_z)]
    inner_first = call(
        functools.partial(first_inner_kernel, n_gy, n_x, n_y),
        "inner_first",
        0,
        got,
        [tile, tile, *inner_shapes(width, n_y, n_z, DRIFT)],
    )
    start, params, *nodes = call(
        functools.partial(first_kernel, n_gy, n_x, n_y),
        "first",
        0,
        [*inner_first, *below],
        [window, window, *nodes_only, *edge(TAKE, 2 * HALO + 2 * RATE_HALO)],
    )
    zero, one, two, two_edge, pair_edge = nodes
    got = [shifted(two, 1, 0, 0), shifted(two_edge, 1, 0, -1), shifted(pair_edge, 0, 0, -1)]
    known_edge = got[-1]

    def inner(tile_first):
        return call(
            functools.partial(inner_kernel, width, n_y, tile_first),
            "inner",
            1,
            (is_first, start, params, *nodes[:3], got[0]),
            inner_shapes(width, n_y, n_z, tile_first),
        )

    def rim(kernel, name, tile_first, operands):
        shapes = [(2, len(rows) * width, n_z) for rows in rim_rows(n_y, tile_first)]
        return call(functools.partial(kernel, width, n_y), name, 0, operands, shapes)

    zero, one, two = nodes[:3]
    second_rim = rim(second_rim_kernel, "second_rim", -DRIFT, (start, params, zero, one, two, known_edge))
    nodes = call(
        functools.partial(second_kernel, width, n_y),
        "second",
        1,
        (is_first, start, params, *inner(-DRIFT), *second_rim, *got),
        [*nodes_only, *edge(HALO), *edge(HALO)],
    )
    for sweep_index in range(2, ITERS):
        zero, one, two, two_low, pair_low, two_high, pair_high = nodes
        got = [shifted(two, 1, 0, 0), shifted(two_high, 1, 0, 1), shifted(two_low, 1, 0, -1)]
        got += [shifted(pair_high, 0, 0, 1), shifted(pair_low, 0, 0, -1)]
        done = sweep_index + 1 == ITERS
        later_rim = rim(later_rim_kernel, "later_rim", 0, (start, params, known_edge, zero, one, two, *got[3:]))
        nodes = call(
            functools.partial(later_kernel, width, n_y, n_x if done else None),
            "last" if done else "later",
            1,
            (is_first, start, params, known_edge, *inner(0), *later_rim, *got[:3]),
            [initial_state.shape] if done else [*nodes_only, *edge(HALO), *edge(HALO)],
            [pltpu.VMEM(tile, jnp.float32)] if done else (),
        )
    return nodes[0][None]


def solution(mesh):
    in_specs = (
        P(None, "gy", "gx", None),
        P("tm", None, "gy", "gx", None),
        P("gy", "gx", None),
        P("gy", "gx", None),
    )
    out_specs = P("tm", None, "gy", "gx", None)
    return jax.shard_map(shards, mesh=mesh, in_specs=in_specs, out_specs=out_specs, check_vma=False)
```

```python
import functools

import jax
import jax.numpy as jnp
from jax import lax
from jax.experimental import pallas as pl
from jax.experimental.pallas import tpu as pltpu
from jax.sharding import PartitionSpec as P

ITERS = 3
DIFF_U = 0.2
DIFF_V = 0.1
HALF_STEP = 0.5
WEIGHTS = ((5.0 / 24.0, 8.0 / 24.0, -1.0 / 24.0), (-1.0 / 24.0, 8.0 / 24.0, 5.0 / 24.0))

AXES = ("tm", "gy", "gx")
HALO = 5
RATE_HALO = 4
DRIFT = 6
TAKE = HALO + DRIFT
BELOW = (TAKE, TAKE, TAKE - 1, TAKE - 1)


def shifted(value, by_tm, by_gy, by_gx):
    n_tm, n_gy, n_gx = (lax.axis_size(axis) for axis in AXES)
    pairs = []
    for t in range(n_tm):
        for y in range(n_gy):
            for x in range(n_gx):
                target = ((t + by_tm) % n_tm * n_gy + (y + by_gy) % n_gy) * n_gx + (x + by_gx) % n_gx
                pairs.append(((t * n_gy + y) * n_gx + x, target))
    return lax.ppermute(value, AXES, pairs)


def from_beside(to_above, to_below, by_tm):
    n_tm, n_gy, n_gx = (lax.axis_size(axis) for axis in AXES)
    if n_gx % 2:
        return shifted(to_above, by_tm, 0, 1), shifted(to_below, by_tm, 0, -1)
    even = lax.axis_index("gx") % 2 == 0
    got = []
    for value, odd in ((jnp.where(even, to_above, to_below), 0), (jnp.where(even, to_below, to_above), 1)):
        pairs = []
        for t in range(n_tm):
            for y in range(n_gy):
                for x in range(n_gx):
                    beside = (x + (1 if x % 2 == odd else -1)) % n_gx
                    target = ((t + by_tm) % n_tm * n_gy + y) * n_gx + beside
                    pairs.append(((t * n_gy + y) * n_gx + x, target))
        got.append(lax.ppermute(value, AXES, pairs))
    return jnp.where(even, got[1], got[0]), jnp.where(even, got[0], got[1])


def near(row, distance, axis):
    size = row.shape[axis]
    return pltpu.roll(row, distance % size, axis) + pltpu.roll(row, -distance % size, axis)


def rates_of(state, feed, feed_kill, spacing):
    scale = 1.0 / (spacing * spacing)

    @functools.cache
    def at(r):
        (u, v), (ub, vb), (ua, va) = state(r), state(r - 1), state(r + 1)
        around_u = (ub + ua) + near(u, int(spacing), 0) + near(u, int(spacing), 1)
        around_v = (vb + va) + near(v, int(spacing), 0) + near(v, int(spacing), 1)
        reaction = u * (v * v)
        rate_u = (DIFF_U * scale) * around_u + feed(r) - (6.0 * DIFF_U * scale + feed(r)) * u - reaction
        rate_v = (DIFF_V * scale) * around_v - (6.0 * DIFF_V * scale + feed_kill(r)) * v + reaction
        return rate_u, rate_v

    return at


def half_sum(low, high):
    x, z = low.shape
    total = low + high
    total = total + pltpu.roll(total, z - 1, 1)
    total = total + pltpu.roll(total, x - 1, 0)
    return 0.125 * total


def restricted(state):
    @functools.cache
    def at(c):
        return tuple(half_sum(a, b) for a, b in zip(state(2 * c), state(2 * c + 1)))

    return at


def spread(row):
    even_x = lax.broadcasted_iota(jnp.int32, row.shape, 0) % 2 == 0
    even_z = lax.broadcasted_iota(jnp.int32, row.shape, 1) % 2 == 0
    row = jnp.where(even_z, row, pltpu.roll(row, 1, 1))
    return jnp.where(even_x, row, pltpu.roll(row, 1, 0))


def quadrature(values, interval):
    def at(r):
        zero, one, two = (value(r) for value in values)
        w = WEIGHTS[interval]
        return tuple(w[0] * a + w[1] * b + w[2] * c for a, b, c in zip(zero, one, two))

    return at


INNER_COUNT = 11


def inner_rows(n_y, tile_first):
    low, high = max(tile_first, -HALO), min(tile_first + n_y, n_y + HALO)
    halves = lambda first, last: (-(-first // 2), last // 2)
    clip = lambda rows, by: (max(rows[0], -by), min(rows[1], n_y // 2 + by))
    inside = lambda rows: (rows[0] + 1, rows[1] - 1)
    fine = [(low + k, high - k) for k in (1, 1, 2, 2, 3)]
    start, one, integral = halves(low, high), halves(*fine[1]), halves(*fine[4])
    coarse = [clip(start, 2), clip(one, 1), clip(integral, 1), clip(integral, 0)]
    return [*fine, *coarse, clip(inside(start), 1), clip(inside(one), 0)]


def inner_shapes(width, n_y, n_z, tile_first):
    return [(2, (high - low) * width, n_z) for low, high in inner_rows(n_y, tile_first)]


def inner_of(refs, width, n_y, tile_first):
    return [(low, high, rows_of(ref, width, low)) for (low, high), ref in zip(inner_rows(n_y, tile_first), refs)]


def write_inner(values, width, n_y, tile_first, refs):
    items = []
    for i, ((low, high), rows, ref) in enumerate(zip(inner_rows(n_y, tile_first), values, refs)):
        for r in range(low, high):
            ready = r + (0, 0, 1, 1, 2)[i] if i < 5 else 2 * r + (1, 1, 3, 3, 3, 3)[i - 5]
            items.append((ready, i, r, rows, ref, low))
    for _, _, r, rows, ref, low in sorted(items, key=lambda item: item[:3]):
        for field, value in enumerate(rows(r)):
            ref[field, pl.ds((r - low) * width, width), :] = value


def old_terms(rates):
    def term(interval):
        @functools.cache
        def at(r):
            return tuple(q - HALF_STEP * f for q, f in zip(quadrature(rates, interval)(r), rates[interval](r)))

        return at

    return term(0), term(1)


def rim_rows(n_y, tile_first):
    needed = ((-RATE_HALO, n_y + RATE_HALO), (1 - RATE_HALO, n_y + RATE_HALO - 1))
    inner = (inner_rows(n_y, tile_first)[place] for place in (1, 3))
    return [[r for r in range(*every) if not low <= r < high] for every, (low, high) in zip(needed, inner)]


def write_rim(terms, width, n_y, tile_first, refs):
    places = [(r, i, k) for i, rows in enumerate(rim_rows(n_y, tile_first)) for k, r in enumerate(rows)]
    for r, i, k in sorted(places):
        for field, value in enumerate(terms[i](r)):
            refs[i][field, pl.ds(k * width, width), :] = value


def rim_of(refs, width, n_y, tile_first):
    def one(ref, rows):
        return lambda r: rows_of(ref, width, 0)(rows.index(r))

    return [one(ref, rows) for ref, rows in zip(refs, rim_rows(n_y, tile_first))]


def iteration(start, feed, kill, terms, inner=()):
    inner = iter(inner)

    def known_or(values):
        low, high, known = next(inner, (0, 0, None))
        return lambda r: (known if low <= r < high else values)(r)

    feed_kill = functools.cache(lambda r: feed(r) + kill(r))
    coarse_feed = functools.cache(lambda c: half_sum(feed(2 * c), feed(2 * c + 1)))
    coarse_sum = functools.cache(lambda c: half_sum(feed_kill(2 * c), feed_kill(2 * c + 1)))

    def stepped(state, rate, interval):
        @functools.cache
        def at(r):
            out = [s + HALF_STEP * f for s, f in zip(state(r), rate(r))]
            if terms is not None:
                out = [o + term for o, term in zip(out, terms[interval](r))]
            return tuple(out)

        return at

    fine = lambda state: rates_of(state, feed, feed_kill, 1.0)
    coarse = lambda state: rates_of(state, coarse_feed, coarse_sum, 2.0)
    rate_zero = known_or(fine(start))
    node_one = known_or(stepped(start, rate_zero, 0))
    rate_one = known_or(fine(node_one))
    node_two = known_or(stepped(node_one, rate_one, 1))
    rate_two = known_or(fine(node_two))
    fresh = (rate_zero, rate_one, rate_two)
    rest_zero, rest_one, rest_two = known_or(restricted(start)), known_or(restricted(node_one)), restricted(node_two)
    rest_integral = [known_or(restricted(quadrature(fresh, interval))) for interval in (0, 1)]
    rate_rest_zero, rate_rest_one = known_or(coarse(rest_zero)), known_or(coarse(rest_one))
    coarse_start, rate_coarse_start = rest_zero, rate_rest_zero

    def coarse_stepped(state, rate, rest_rate, integral):
        @functools.cache
        def at(c):
            return tuple(
                s + HALF_STEP * (f - g) + q for s, f, g, q in zip(state(c), rate(c), rest_rate(c), integral(c))
            )

        return at

    coarse_one = coarse_stepped(coarse_start, rate_coarse_start, rate_rest_zero, rest_integral[0])
    coarse_two = coarse_stepped(coarse_one, coarse(coarse_one), rate_rest_one, rest_integral[1])

    def corrected(node, coarse_node, rest):
        change = functools.cache(lambda c: tuple(spread(w - m) for w, m in zip(coarse_node(c), rest(c))))

        @functools.cache
        def at(r):
            return tuple(n + d for n, d in zip(node(r), change(r // 2)))

        return at

    nodes = corrected(node_one, coarse_one, rest_one), corrected(node_two, coarse_two, rest_two)
    fine_rows = (rate_zero, node_one, rate_one, node_two, rate_two)
    return (rate_zero, *nodes), (*fine_rows, rest_zero, rest_one, *rest_integral, rate_rest_zero, rate_rest_one)


def rows_of(ref, width, first):
    @functools.cache
    def at(r):
        assert 0 <= (r - first) * width < ref.shape[1]
        return tuple(ref[field, pl.ds((r - first) * width, width), :] for field in range(2))

    return at


def pack_kernel(tiles_ref, state_ref, all_ref, high_ref):
    n_fields, n_x, n_y, _ = tiles_ref.shape
    for field in range(n_fields):
        for x in range(n_x):
            all_ref[field, pl.ds(x, n_y, stride=n_x), :] = tiles_ref[field, x]
        count = BELOW[field]
        rows = all_ref[field, pl.ds((n_y - count) * n_x, count * n_x), :]
        high_ref[pl.ds(sum(BELOW[:field]) * n_x, count * n_x), :] = rows
    for field in range(2):
        state_ref[field] = all_ref[field]


def collect(out_ref, field, source_field, n_x, lowest, pieces):
    width = n_x * len(pieces[0][1])
    for first, refs, count in pieces:
        for gy, ref in enumerate(refs):
            for k in range(count):
                if first + k >= lowest:
                    place = pl.ds((first + k - lowest) * width + gy * n_x, n_x)
                    out_ref[field, place, :] = ref[source_field, pl.ds(k * n_x, n_x), :]


def first_inner_kernel(n_gy, n_x, n_y, *refs):
    state_ref, local_ref = refs[:2]
    others = refs[2 : 1 + n_gy]
    start_ref, params_ref, *outs = refs[1 + n_gy :]
    width = n_gy * n_x
    for field in range(2):
        collect(start_ref, field, field, n_x, 0, [(0, [state_ref, *others], n_y)])
        collect(params_ref, field, 2 + field, n_x, 0, [(0, [local_ref, *others], n_y)])
    start, params = rows_of(start_ref, width, DRIFT), rows_of(params_ref, width, DRIFT)
    _, values = iteration(start, lambda r: params(r)[0], lambda r: params(r)[1], None)
    write_inner(values, width, n_y, DRIFT, outs)


def first_kernel(n_gy, n_x, n_y, *refs):
    tiles, inner_refs, refs = refs[:2], refs[2 : 2 + INNER_COUNT], refs[2 + INNER_COUNT :]
    lows, (start_ref, params_ref, *outs) = refs[:n_gy], refs[n_gy:]
    width = n_gy * n_x
    for field in range(2):
        for out_ref, tile_ref, place in zip((start_ref, params_ref), tiles, (0, 2)):
            count, begin = BELOW[place + field], sum(BELOW[: place + field])
            for gy, low_ref in enumerate(lows):
                for k in range(count):
                    row = pl.ds((TAKE - count + k) * width + gy * n_x, n_x)
                    out_ref[field, row, :] = low_ref[pl.ds((begin + k) * n_x, n_x), :]
            out_ref[field, pl.ds(TAKE * width, n_y * width), :] = tile_ref[field]
    start = rows_of(start_ref, width, -HALO)
    params = rows_of(params_ref, width, -HALO)
    inner = inner_of(inner_refs, width, n_y, DRIFT)
    results, _ = iteration(start, lambda r: params(r)[0], lambda r: params(r)[1], None, inner)
    write_nodes(results, width, n_y, [(0, TAKE)], *outs)
    for rows, place, count in ((start, 4 * TAKE, HALO), (params, 4 * TAKE + 2 * HALO, RATE_HALO)):
        for r in range(count):
            for field, value in enumerate(rows(r + DRIFT)):
                outs[-1][pl.ds((place + field * count + r) * width, width), :] = value


def write_nodes(results, width, n_y, edges, zero_ref, one_ref, two_ref, *edge_refs):
    rate_zero, node_one, node_two = results
    for r in range(-RATE_HALO, n_y + RATE_HALO):
        if 0 <= r < n_y:
            place = pl.ds(r * width, width)
            for field, (one, two) in enumerate(zip(node_one(r), node_two(r))):
                one_ref[field, place, :] = one
                two_ref[field, place, :] = two
                for i, (first, count) in enumerate(edges):
                    if first <= r < first + count:
                        beside = pl.ds((r - first) * width, width)
                        edge_refs[2 * i][field, beside, :] = two
                        for at, value in ((field, one), (2 + field, two)):
                            edge_refs[2 * i + 1][pl.ds((at * count + r - first) * width, width), :] = value
        for field, zero in enumerate(rate_zero(r)):
            zero_ref[field, pl.ds((r + RATE_HALO) * width, width), :] = zero


def joined(*parts):
    def at(r):
        return [rows for first, rows in parts if first <= r][-1](r)

    return at


def flat_rows(ref, width, place, first, count):
    @functools.cache
    def at(r):
        assert 0 <= r - first < count
        return tuple(ref[pl.ds((place + field * count + r - first) * width, width), :] for field in range(2))

    return at


def known(width, n_y, start_ref, params_ref, edge_ref):
    return (
        joined((-TAKE, rows_of(ref, width, -TAKE)), (n_y, flat_rows(edge_ref, width, place, n_y, count)))
        for ref, place, count in ((start_ref, 4 * TAKE, HALO), (params_ref, 4 * TAKE + 2 * HALO, RATE_HALO))
    )


def later_iteration(is_first, kept, params, got, terms, inner=()):
    @functools.cache
    def start(r):
        return tuple(jnp.where(is_first, a, b) for a, b in zip(kept(r), got(r)))

    return iteration(start, lambda r: params(r)[0], lambda r: params(r)[1], terms, inner)


def terms_of(params, old_zero, ones, twos):
    feed = lambda r: params(r)[0]
    feed_kill = functools.cache(lambda r: params(r)[0] + params(r)[1])
    return old_terms((old_zero(feed, feed_kill), *(rates_of(rows, feed, feed_kill, 1.0) for rows in (ones, twos))))


def inner_kernel(width, n_y, tile_first, first_ref, start_ref, params_ref, zero_ref, one_ref, two_ref, got_ref, *outs):
    kept, params = rows_of(start_ref, width, -TAKE), rows_of(params_ref, width, -TAKE)
    old_zero = rows_of(zero_ref, width, tile_first - RATE_HALO)
    ones, twos, got = (rows_of(ref, width, tile_first) for ref in (one_ref, two_ref, got_ref))
    terms = terms_of(params, lambda feed, feed_kill: old_zero, ones, twos)
    _, values = later_iteration(first_ref[0] == 1, kept, params, got, terms)
    write_inner(values, width, n_y, tile_first, outs)


def moved(width, n_y, tile_ref, beside):
    return joined((-DRIFT, rows_of(tile_ref, width, -DRIFT)), (n_y - DRIFT, beside))


def second_rim_kernel(width, n_y, start_ref, params_ref, zero_ref, one_ref, two_ref, pair_edge, *outs):
    kept, params = known(width, n_y, start_ref, params_ref, pair_edge)
    end = n_y - DRIFT
    ones, twos = (
        moved(width, n_y, ref, flat_rows(pair_edge, width, place * TAKE, end, TAKE))
        for ref, place in ((one_ref, 0), (two_ref, 2))
    )

    def old_zero(feed, feed_kill):
        inside = rows_of(zero_ref, width, -RATE_HALO - DRIFT)
        return joined((-RATE_HALO - DRIFT, inside), (end + RATE_HALO, rates_of(kept, feed, feed_kill, 1.0)))

    write_rim(terms_of(params, old_zero, ones, twos), width, n_y, -DRIFT, outs)


def second_kernel(width, n_y, first_ref, start_ref, params_ref, *refs):
    inner = inner_of(refs, width, n_y, -DRIFT)
    terms = rim_of(refs[INNER_COUNT:], width, n_y, -DRIFT)
    got_ref, got_edge, pair_edge, *outs = refs[INNER_COUNT + 2 :]
    kept, params = known(width, n_y, start_ref, params_ref, pair_edge)
    got = moved(width, n_y, got_ref, rows_of(got_edge, width, n_y - DRIFT))
    results, _ = later_iteration(first_ref[0] == 1, kept, params, got, terms, inner)
    write_nodes(results, width, n_y, [(0, HALO), (n_y - HALO, HALO)], *outs)


def window(width, n_y, low, tile_ref, high):
    return joined((-HALO, low), (0, rows_of(tile_ref, width, 0)), (n_y, high))


def later_rim_kernel(
    width, n_y, start_ref, params_ref, known_ref, zero_ref, one_ref, two_ref, pair_low, pair_high, *outs
):
    _, params = known(width, n_y, start_ref, params_ref, known_ref)

    def pair(tile_ref, place):
        low, high = (
            flat_rows(ref, width, place * HALO, first, HALO) for ref, first in ((pair_low, -HALO), (pair_high, n_y))
        )
        return window(width, n_y, low, tile_ref, high)

    old_zero = rows_of(zero_ref, width, -RATE_HALO)
    terms = terms_of(params, lambda feed, feed_kill: old_zero, pair(one_ref, 0), pair(two_ref, 2))
    write_rim(terms, width, n_y, 0, outs)


def later_kernel(width, n_y, out_x, first_ref, start_ref, params_ref, known_ref, *refs):
    inner = inner_of(refs, width, n_y, 0)
    terms = rim_of(refs[INNER_COUNT:], width, n_y, 0)
    got_ref, got_low, got_high, *outs = refs[INNER_COUNT + 2 :]
    kept, params = known(width, n_y, start_ref, params_ref, known_ref)
    got = window(width, n_y, rows_of(got_low, width, -HALO), got_ref, rows_of(got_high, width, n_y))
    results, _ = later_iteration(first_ref[0] == 1, kept, params, got, terms, inner)
    if out_x is None:
        write_nodes(results, width, n_y, [(0, HALO), (n_y - HALO, HALO)], *outs)
    else:
        out_ref, scratch = outs
        for r in range(n_y):
            for field, value in enumerate(results[2](r)):
                scratch[field, pl.ds(r * width, width), :] = value
        for x in range(out_x):
            for field in range(2):
                out_ref[field, x] = scratch[field, pl.ds(x, n_y, stride=width), :]


def call(kernel, name, n_scalars, operands, shapes, scratch=()):
    specs = [pl.BlockSpec(memory_space=pltpu.SMEM)] * n_scalars
    specs += [pl.BlockSpec(memory_space=pltpu.VMEM)] * (len(operands) - n_scalars)
    return pl.pallas_call(
        kernel,
        name=name,
        out_shape=[jax.ShapeDtypeStruct(shape, jnp.float32) for shape in shapes],
        in_specs=specs,
        out_specs=[pl.BlockSpec(memory_space=pltpu.VMEM)] * len(shapes),
        scratch_shapes=scratch,
        compiler_params=pltpu.CompilerParams(vmem_limit_bytes=32 * 1024 * 1024),
    )(*operands)


def shards(initial_state, slice_guess, feed_rate, kill_rate):
    n_gy, n_tm = lax.axis_size("gy"), lax.axis_size("tm")
    _, n_x, n_y, n_z = initial_state.shape
    width = n_gy * n_x
    place = lax.axis_index("tm")
    is_first = (place == 0).astype(jnp.int32)[None]

    sent = jnp.where(place == n_tm - 1, initial_state, slice_guess[0])
    state, local, high = call(
        pack_kernel,
        "pack",
        0,
        (jnp.concatenate([sent, feed_rate[None], kill_rate[None]]),),
        [(2, n_y * n_x, n_z), (4, n_y * n_x, n_z), (sum(BELOW) * n_x, n_z)],
    )
    got = [shifted(state, 1, 0, 0), local]
    got += [shifted(local, 1, -gy, 0) for gy in range(1, n_gy)]
    below = [shifted(high, 1, -gy, 1) for gy in range(n_gy)]

    tile, window = (2, n_y * width, n_z), (2, (TAKE + n_y) * width, n_z)
    nodes_only = [(2, (n_y + 2 * RATE_HALO) * width, n_z), tile, tile]
    edge = lambda rows, more=0: [(2, rows * width, n_z), ((4 * rows + more) * width, n_z)]
    inner_first = call(
        functools.partial(first_inner_kernel, n_gy, n_x, n_y),
        "inner_first",
        0,
        got,
        [tile, tile, *inner_shapes(width, n_y, n_z, DRIFT)],
    )
    start, params, *nodes = call(
        functools.partial(first_kernel, n_gy, n_x, n_y),
        "first",
        0,
        [*inner_first, *below],
        [window, window, *nodes_only, *edge(TAKE, 2 * HALO + 2 * RATE_HALO)],
    )
    zero, one, two, two_edge, pair_edge = nodes
    got = [shifted(two, 1, 0, 0), shifted(two_edge, 1, 0, -1), shifted(pair_edge, 0, 0, -1)]
    known_edge = got[-1]

    def inner(tile_first):
        return call(
            functools.partial(inner_kernel, width, n_y, tile_first),
            "inner",
            1,
            (is_first, start, params, *nodes[:3], got[0]),
            inner_shapes(width, n_y, n_z, tile_first),
        )

    def rim(kernel, name, tile_first, operands):
        shapes = [(2, len(rows) * width, n_z) for rows in rim_rows(n_y, tile_first)]
        return call(functools.partial(kernel, width, n_y), name, 0, operands, shapes)

    zero, one, two = nodes[:3]
    second_rim = rim(second_rim_kernel, "second_rim", -DRIFT, (start, params, zero, one, two, known_edge))
    nodes = call(
        functools.partial(second_kernel, width, n_y),
        "second",
        1,
        (is_first, start, params, *inner(-DRIFT), *second_rim, *got),
        [*nodes_only, *edge(HALO), *edge(HALO)],
    )
    for sweep_index in range(2, ITERS):
        zero, one, two, two_low, pair_low, two_high, pair_high = nodes
        got = [shifted(two, 1, 0, 0), *from_beside(two_high, two_low, 1), *from_beside(pair_high, pair_low, 0)]
        done = sweep_index + 1 == ITERS
        later_rim = rim(later_rim_kernel, "later_rim", 0, (start, params, known_edge, zero, one, two, *got[3:]))
        nodes = call(
            functools.partial(later_kernel, width, n_y, n_x if done else None),
            "last" if done else "later",
            1,
            (is_first, start, params, known_edge, *inner(0), *later_rim, *got[:3]),
            [initial_state.shape] if done else [*nodes_only, *edge(HALO), *edge(HALO)],
            [pltpu.VMEM(tile, jnp.float32)] if done else (),
        )
    return nodes[0][None]


def solution(mesh):
    in_specs = (
        P(None, "gy", "gx", None),
        P("tm", None, "gy", "gx", None),
        P("gy", "gx", None),
        P("gy", "gx", None),
    )
    out_specs = P("tm", None, "gy", "gx", None)
    return jax.shard_map(shards, mesh=mesh, in_specs=in_specs, out_specs=out_specs, check_vma=False)
```

```python
import functools

import jax
import jax.numpy as jnp
from jax import lax
from jax.experimental import pallas as pl
from jax.experimental.pallas import tpu as pltpu
from jax.sharding import PartitionSpec as P

ITERS = 3
DIFF_U = 0.2
DIFF_V = 0.1
HALF_STEP = 0.5
WEIGHTS = ((5.0 / 24.0, 8.0 / 24.0, -1.0 / 24.0), (-1.0 / 24.0, 8.0 / 24.0, 5.0 / 24.0))

AXES = ("tm", "gy", "gx")
HALO = 5
RATE_HALO = 4
DRIFT = 6
TAKE = HALO + DRIFT
BELOW = (TAKE, TAKE, TAKE - 1, TAKE - 1)


def shifted(value, by_tm, by_gy, by_gx):
    n_tm, n_gy, n_gx = (lax.axis_size(axis) for axis in AXES)
    pairs = []
    for t in range(n_tm):
        for y in range(n_gy):
            for x in range(n_gx):
                target = ((t + by_tm) % n_tm * n_gy + (y + by_gy) % n_gy) * n_gx + (x + by_gx) % n_gx
                pairs.append(((t * n_gy + y) * n_gx + x, target))
    return lax.ppermute(value, AXES, pairs)


def near(row, distance, axis):
    size = row.shape[axis]
    return pltpu.roll(row, distance % size, axis) + pltpu.roll(row, -distance % size, axis)


def rates_of(state, feed, feed_kill, spacing):
    scale = 1.0 / (spacing * spacing)

    @functools.cache
    def at(r):
        (u, v), (ub, vb), (ua, va) = state(r), state(r - 1), state(r + 1)
        around_u = (ub + ua) + near(u, int(spacing), 0) + near(u, int(spacing), 1)
        around_v = (vb + va) + near(v, int(spacing), 0) + near(v, int(spacing), 1)
        reaction = u * (v * v)
        rate_u = (DIFF_U * scale) * around_u + feed(r) - (6.0 * DIFF_U * scale + feed(r)) * u - reaction
        rate_v = (DIFF_V * scale) * around_v - (6.0 * DIFF_V * scale + feed_kill(r)) * v + reaction
        return rate_u, rate_v

    return at


def half_sum(low, high):
    x, z = low.shape
    total = low + high
    total = total + pltpu.roll(total, z - 1, 1)
    total = total + pltpu.roll(total, x - 1, 0)
    return 0.125 * total


def restricted(state):
    @functools.cache
    def at(c):
        return tuple(half_sum(a, b) for a, b in zip(state(2 * c), state(2 * c + 1)))

    return at


def spread(row):
    even_x = lax.broadcasted_iota(jnp.int32, row.shape, 0) % 2 == 0
    even_z = lax.broadcasted_iota(jnp.int32, row.shape, 1) % 2 == 0
    row = jnp.where(even_z, row, pltpu.roll(row, 1, 1))
    return jnp.where(even_x, row, pltpu.roll(row, 1, 0))


def quadrature(values, interval):
    def at(r):
        zero, one, two = (value(r) for value in values)
        w = WEIGHTS[interval]
        return tuple(w[0] * a + w[1] * b + w[2] * c for a, b, c in zip(zero, one, two))

    return at


INNER_COUNT = 11


def inner_rows(n_y, tile_first):
    low, high = max(tile_first, -HALO), min(tile_first + n_y, n_y + HALO)
    halves = lambda first, last: (-(-first // 2), last // 2)
    clip = lambda rows, by: (max(rows[0], -by), min(rows[1], n_y // 2 + by))
    inside = lambda rows: (rows[0] + 1, rows[1] - 1)
    fine = [(low + k, high - k) for k in (1, 1, 2, 2, 3)]
    start, one, integral = halves(low, high), halves(*fine[1]), halves(*fine[4])
    coarse = [clip(start, 2), clip(one, 1), clip(integral, 1), clip(integral, 0)]
    return [*fine, *coarse, clip(inside(start), 1), clip(inside(one), 0)]


def inner_shapes(width, n_y, n_z, tile_first):
    return [(2, (high - low) * width, n_z) for low, high in inner_rows(n_y, tile_first)]


def inner_of(refs, width, n_y, tile_first):
    return [(low, high, rows_of(ref, width, low)) for (low, high), ref in zip(inner_rows(n_y, tile_first), refs)]


def write_inner(values, width, n_y, tile_first, refs):
    items = []
    for i, ((low, high), rows, ref) in enumerate(zip(inner_rows(n_y, tile_first), values, refs)):
        for r in range(low, high):
            ready = r + (0, 0, 1, 1, 2)[i] if i < 5 else 2 * r + (1, 1, 3, 3, 3, 3)[i - 5]
            items.append((ready, i, r, rows, ref, low))
    for _, _, r, rows, ref, low in sorted(items, key=lambda item: item[:3]):
        for field, value in enumerate(rows(r)):
            ref[field, pl.ds((r - low) * width, width), :] = value


def old_terms(rates):
    def term(interval):
        @functools.cache
        def at(r):
            return tuple(q - HALF_STEP * f for q, f in zip(quadrature(rates, interval)(r), rates[interval](r)))

        return at

    return term(0), term(1)


def rim_rows(n_y, tile_first):
    needed = ((-RATE_HALO, n_y + RATE_HALO), (1 - RATE_HALO, n_y + RATE_HALO - 1))
    inner = (inner_rows(n_y, tile_first)[place] for place in (1, 3))
    return [[r for r in range(*every) if not low <= r < high] for every, (low, high) in zip(needed, inner)]


def write_rim(terms, width, n_y, tile_first, refs):
    places = [(r, i, k) for i, rows in enumerate(rim_rows(n_y, tile_first)) for k, r in enumerate(rows)]
    for r, i, k in sorted(places):
        for field, value in enumerate(terms[i](r)):
            refs[i][field, pl.ds(k * width, width), :] = value


def rim_of(refs, width, n_y, tile_first):
    def one(ref, rows):
        return lambda r: rows_of(ref, width, 0)(rows.index(r))

    return [one(ref, rows) for ref, rows in zip(refs, rim_rows(n_y, tile_first))]


def iteration(start, feed, kill, terms, inner=()):
    inner = iter(inner)

    def known_or(values):
        low, high, known = next(inner, (0, 0, None))
        return lambda r: (known if low <= r < high else values)(r)

    feed_kill = functools.cache(lambda r: feed(r) + kill(r))
    coarse_feed = functools.cache(lambda c: half_sum(feed(2 * c), feed(2 * c + 1)))
    coarse_sum = functools.cache(lambda c: half_sum(feed_kill(2 * c), feed_kill(2 * c + 1)))

    def stepped(state, rate, interval):
        @functools.cache
        def at(r):
            out = [s + HALF_STEP * f for s, f in zip(state(r), rate(r))]
            if terms is not None:
                out = [o + term for o, term in zip(out, terms[interval](r))]
            return tuple(out)

        return at

    fine = lambda state: rates_of(state, feed, feed_kill, 1.0)
    coarse = lambda state: rates_of(state, coarse_feed, coarse_sum, 2.0)
    rate_zero = known_or(fine(start))
    node_one = known_or(stepped(start, rate_zero, 0))
    rate_one = known_or(fine(node_one))
    node_two = known_or(stepped(node_one, rate_one, 1))
    rate_two = known_or(fine(node_two))
    fresh = (rate_zero, rate_one, rate_two)
    rest_zero, rest_one, rest_two = known_or(restricted(start)), known_or(restricted(node_one)), restricted(node_two)
    rest_integral = [known_or(restricted(quadrature(fresh, interval))) for interval in (0, 1)]
    rate_rest_zero, rate_rest_one = known_or(coarse(rest_zero)), known_or(coarse(rest_one))
    coarse_start, rate_coarse_start = rest_zero, rate_rest_zero

    def coarse_stepped(state, rate, rest_rate, integral):
        @functools.cache
        def at(c):
            return tuple(
                s + HALF_STEP * (f - g) + q for s, f, g, q in zip(state(c), rate(c), rest_rate(c), integral(c))
            )

        return at

    coarse_one = coarse_stepped(coarse_start, rate_coarse_start, rate_rest_zero, rest_integral[0])
    coarse_two = coarse_stepped(coarse_one, coarse(coarse_one), rate_rest_one, rest_integral[1])

    def corrected(node, coarse_node, rest):
        change = functools.cache(lambda c: tuple(spread(w - m) for w, m in zip(coarse_node(c), rest(c))))

        @functools.cache
        def at(r):
            return tuple(n + d for n, d in zip(node(r), change(r // 2)))

        return at

    nodes = corrected(node_one, coarse_one, rest_one), corrected(node_two, coarse_two, rest_two)
    fine_rows = (rate_zero, node_one, rate_one, node_two, rate_two)
    return (rate_zero, *nodes), (*fine_rows, rest_zero, rest_one, *rest_integral, rate_rest_zero, rate_rest_one)


def rows_of(ref, width, first):
    @functools.cache
    def at(r):
        assert 0 <= (r - first) * width < ref.shape[1]
        return tuple(ref[field, pl.ds((r - first) * width, width), :] for field in range(2))

    return at


def pack_kernel(tiles_ref, state_ref, rates_ref, high_ref):
    n_fields, n_x, n_y, _ = tiles_ref.shape
    for field in range(n_fields):
        out_ref = (state_ref, rates_ref)[field // 2].at[field % 2]
        for x in range(n_x):
            out_ref[pl.ds(x, n_y, stride=n_x), :] = tiles_ref[field, x]
        count = BELOW[field]
        rows = out_ref[pl.ds((n_y - count) * n_x, count * n_x), :]
        high_ref[pl.ds(sum(BELOW[:field]) * n_x, count * n_x), :] = rows


def collect(out_ref, field, source_field, n_x, lowest, pieces):
    width = n_x * len(pieces[0][1])
    for first, refs, count in pieces:
        for gy, ref in enumerate(refs):
            for k in range(count):
                if first + k >= lowest:
                    place = pl.ds((first + k - lowest) * width + gy * n_x, n_x)
                    out_ref[field, place, :] = ref[source_field, pl.ds(k * n_x, n_x), :]


def first_inner_kernel(n_gy, n_x, n_y, *refs):
    states, rates, (start_ref, params_ref, *outs) = refs[:n_gy], refs[n_gy : 2 * n_gy], refs[2 * n_gy :]
    width = n_gy * n_x
    for field in range(2):
        collect(start_ref, field, field, n_x, 0, [(0, states, n_y)])
        collect(params_ref, field, field, n_x, 0, [(0, rates, n_y)])
    start, params = rows_of(start_ref, width, DRIFT), rows_of(params_ref, width, DRIFT)
    _, values = iteration(start, lambda r: params(r)[0], lambda r: params(r)[1], None)
    write_inner(values, width, n_y, DRIFT, outs)


def first_kernel(n_gy, n_x, n_y, *refs):
    tiles, inner_refs, refs = refs[:2], refs[2 : 2 + INNER_COUNT], refs[2 + INNER_COUNT :]
    lows, (start_ref, params_ref, *outs) = refs[:n_gy], refs[n_gy:]
    width = n_gy * n_x
    for field in range(2):
        for out_ref, tile_ref, place in zip((start_ref, params_ref), tiles, (0, 2)):
            count, begin = BELOW[place + field], sum(BELOW[: place + field])
            for gy, low_ref in enumerate(lows):
                for k in range(count):
                    row = pl.ds((TAKE - count + k) * width + gy * n_x, n_x)
                    out_ref[field, row, :] = low_ref[pl.ds((begin + k) * n_x, n_x), :]
            out_ref[field, pl.ds(TAKE * width, n_y * width), :] = tile_ref[field]
    start = rows_of(start_ref, width, -HALO)
    params = rows_of(params_ref, width, -HALO)
    inner = inner_of(inner_refs, width, n_y, DRIFT)
    results, _ = iteration(start, lambda r: params(r)[0], lambda r: params(r)[1], None, inner)
    write_nodes(results, width, n_y, [(0, TAKE)], *outs)
    for rows, place, count in ((start, 4 * TAKE, HALO), (params, 4 * TAKE + 2 * HALO, RATE_HALO)):
        for r in range(count):
            for field, value in enumerate(rows(r + DRIFT)):
                outs[-1][pl.ds((place + field * count + r) * width, width), :] = value


def write_nodes(results, width, n_y, edges, zero_ref, one_ref, two_ref, *edge_refs):
    rate_zero, node_one, node_two = results
    for r in range(-RATE_HALO, n_y + RATE_HALO):
        if 0 <= r < n_y:
            place = pl.ds(r * width, width)
            for field, (one, two) in enumerate(zip(node_one(r), node_two(r))):
                one_ref[field, place, :] = one
                two_ref[field, place, :] = two
                for i, (first, count) in enumerate(edges):
                    if first <= r < first + count:
                        beside = pl.ds((r - first) * width, width)
                        edge_refs[2 * i][field, beside, :] = two
                        for at, value in ((field, one), (2 + field, two)):
                            edge_refs[2 * i + 1][pl.ds((at * count + r - first) * width, width), :] = value
        for field, zero in enumerate(rate_zero(r)):
            zero_ref[field, pl.ds((r + RATE_HALO) * width, width), :] = zero


def joined(*parts):
    def at(r):
        return [rows for first, rows in parts if first <= r][-1](r)

    return at


def flat_rows(ref, width, place, first, count):
    @functools.cache
    def at(r):
        assert 0 <= r - first < count
        return tuple(ref[pl.ds((place + field * count + r - first) * width, width), :] for field in range(2))

    return at


def known(width, n_y, start_ref, params_ref, edge_ref):
    return (
        joined((-TAKE, rows_of(ref, width, -TAKE)), (n_y, flat_rows(edge_ref, width, place, n_y, count)))
        for ref, place, count in ((start_ref, 4 * TAKE, HALO), (params_ref, 4 * TAKE + 2 * HALO, RATE_HALO))
    )


def later_iteration(is_first, kept, params, got, terms, inner=()):
    @functools.cache
    def start(r):
        return tuple(jnp.where(is_first, a, b) for a, b in zip(kept(r), got(r)))

    return iteration(start, lambda r: params(r)[0], lambda r: params(r)[1], terms, inner)


def terms_of(params, old_zero, ones, twos):
    feed = lambda r: params(r)[0]
    feed_kill = functools.cache(lambda r: params(r)[0] + params(r)[1])
    return old_terms((old_zero(feed, feed_kill), *(rates_of(rows, feed, feed_kill, 1.0) for rows in (ones, twos))))


def inner_kernel(width, n_y, tile_first, first_ref, start_ref, params_ref, zero_ref, one_ref, two_ref, got_ref, *outs):
    kept, params = rows_of(start_ref, width, -TAKE), rows_of(params_ref, width, -TAKE)
    old_zero = rows_of(zero_ref, width, tile_first - RATE_HALO)
    ones, twos, got = (rows_of(ref, width, tile_first) for ref in (one_ref, two_ref, got_ref))
    terms = terms_of(params, lambda feed, feed_kill: old_zero, ones, twos)
    _, values = later_iteration(first_ref[0] == 1, kept, params, got, terms)
    write_inner(values, width, n_y, tile_first, outs)


def moved(width, n_y, tile_ref, beside):
    return joined((-DRIFT, rows_of(tile_ref, width, -DRIFT)), (n_y - DRIFT, beside))


def second_rim_kernel(width, n_y, start_ref, params_ref, zero_ref, one_ref, two_ref, pair_edge, *outs):
    kept, params = known(width, n_y, start_ref, params_ref, pair_edge)
    end = n_y - DRIFT
    ones, twos = (
        moved(width, n_y, ref, flat_rows(pair_edge, width, place * TAKE, end, TAKE))
        for ref, place in ((one_ref, 0), (two_ref, 2))
    )

    def old_zero(feed, feed_kill):
        inside = rows_of(zero_ref, width, -RATE_HALO - DRIFT)
        return joined((-RATE_HALO - DRIFT, inside), (end + RATE_HALO, rates_of(kept, feed, feed_kill, 1.0)))

    write_rim(terms_of(params, old_zero, ones, twos), width, n_y, -DRIFT, outs)


def second_kernel(width, n_y, first_ref, start_ref, params_ref, *refs):
    inner = inner_of(refs, width, n_y, -DRIFT)
    terms = rim_of(refs[INNER_COUNT:], width, n_y, -DRIFT)
    got_ref, got_edge, pair_edge, *outs = refs[INNER_COUNT + 2 :]
    kept, params = known(width, n_y, start_ref, params_ref, pair_edge)
    got = moved(width, n_y, got_ref, rows_of(got_edge, width, n_y - DRIFT))
    results, _ = later_iteration(first_ref[0] == 1, kept, params, got, terms, inner)
    write_nodes(results, width, n_y, [(0, HALO), (n_y - HALO, HALO)], *outs)


def window(width, n_y, low, tile_ref, high):
    return joined((-HALO, low), (0, rows_of(tile_ref, width, 0)), (n_y, high))


def later_rim_kernel(
    width, n_y, start_ref, params_ref, known_ref, zero_ref, one_ref, two_ref, pair_low, pair_high, *outs
):
    _, params = known(width, n_y, start_ref, params_ref, known_ref)

    def pair(tile_ref, place):
        low, high = (
            flat_rows(ref, width, place * HALO, first, HALO) for ref, first in ((pair_low, -HALO), (pair_high, n_y))
        )
        return window(width, n_y, low, tile_ref, high)

    old_zero = rows_of(zero_ref, width, -RATE_HALO)
    terms = terms_of(params, lambda feed, feed_kill: old_zero, pair(one_ref, 0), pair(two_ref, 2))
    write_rim(terms, width, n_y, 0, outs)


def later_kernel(width, n_y, out_x, first_ref, start_ref, params_ref, known_ref, *refs):
    inner = inner_of(refs, width, n_y, 0)
    terms = rim_of(refs[INNER_COUNT:], width, n_y, 0)
    got_ref, got_low, got_high, *outs = refs[INNER_COUNT + 2 :]
    kept, params = known(width, n_y, start_ref, params_ref, known_ref)
    got = window(width, n_y, rows_of(got_low, width, -HALO), got_ref, rows_of(got_high, width, n_y))
    results, _ = later_iteration(first_ref[0] == 1, kept, params, got, terms, inner)
    if out_x is None:
        write_nodes(results, width, n_y, [(0, HALO), (n_y - HALO, HALO)], *outs)
    else:
        out_ref, scratch = outs
        for r in range(n_y):
            for field, value in enumerate(results[2](r)):
                scratch[field, pl.ds(r * width, width), :] = value
        for x in range(out_x):
            for field in range(2):
                out_ref[field, x] = scratch[field, pl.ds(x, n_y, stride=width), :]


def call(kernel, name, n_scalars, operands, shapes, scratch=()):
    specs = [pl.BlockSpec(memory_space=pltpu.SMEM)] * n_scalars
    specs += [pl.BlockSpec(memory_space=pltpu.VMEM)] * (len(operands) - n_scalars)
    return pl.pallas_call(
        kernel,
        name=name,
        out_shape=[jax.ShapeDtypeStruct(shape, jnp.float32) for shape in shapes],
        in_specs=specs,
        out_specs=[pl.BlockSpec(memory_space=pltpu.VMEM)] * len(shapes),
        scratch_shapes=scratch,
        compiler_params=pltpu.CompilerParams(vmem_limit_bytes=32 * 1024 * 1024),
    )(*operands)


def shards(initial_state, slice_guess, feed_rate, kill_rate):
    n_gy, n_tm = lax.axis_size("gy"), lax.axis_size("tm")
    _, n_x, n_y, n_z = initial_state.shape
    width = n_gy * n_x
    place = lax.axis_index("tm")
    is_first = (place == 0).astype(jnp.int32)[None]

    sent = jnp.where(place == n_tm - 1, initial_state, slice_guess[0])
    state, rates, high = call(
        pack_kernel,
        "pack",
        0,
        (jnp.concatenate([sent, feed_rate[None], kill_rate[None]]),),
        [(2, n_y * n_x, n_z), (2, n_y * n_x, n_z), (sum(BELOW) * n_x, n_z)],
    )
    got = [shifted(state, 1, -gy, 0) for gy in range(n_gy)]
    got += [rates, *(shifted(rates, 0, -gy, 0) for gy in range(1, n_gy))]
    below = [shifted(high, 1, -gy, 1) for gy in range(n_gy)]

    tile, window = (2, n_y * width, n_z), (2, (TAKE + n_y) * width, n_z)
    nodes_only = [(2, (n_y + 2 * RATE_HALO) * width, n_z), tile, tile]
    edge = lambda rows, more=0: [(2, rows * width, n_z), ((4 * rows + more) * width, n_z)]
    inner_first = call(
        functools.partial(first_inner_kernel, n_gy, n_x, n_y),
        "inner_first",
        0,
        got,
        [tile, tile, *inner_shapes(width, n_y, n_z, DRIFT)],
    )
    start, params, *nodes = call(
        functools.partial(first_kernel, n_gy, n_x, n_y),
        "first",
        0,
        [*inner_first, *below],
        [window, window, *nodes_only, *edge(TAKE, 2 * HALO + 2 * RATE_HALO)],
    )
    zero, one, two, two_edge, pair_edge = nodes
    got = [shifted(two, 1, 0, 0), shifted(two_edge, 1, 0, -1), shifted(pair_edge, 0, 0, -1)]
    known_edge = got[-1]

    def inner(tile_first):
        return call(
            functools.partial(inner_kernel, width, n_y, tile_first),
            "inner",
            1,
            (is_first, start, params, *nodes[:3], got[0]),
            inner_shapes(width, n_y, n_z, tile_first),
        )

    def rim(kernel, name, tile_first, operands):
        shapes = [(2, len(rows) * width, n_z) for rows in rim_rows(n_y, tile_first)]
        return call(functools.partial(kernel, width, n_y), name, 0, operands, shapes)

    zero, one, two = nodes[:3]
    second_rim = rim(second_rim_kernel, "second_rim", -DRIFT, (start, params, zero, one, two, known_edge))
    nodes = call(
        functools.partial(second_kernel, width, n_y),
        "second",
        1,
        (is_first, start, params, *inner(-DRIFT), *second_rim, *got),
        [*nodes_only, *edge(HALO), *edge(HALO)],
    )
    for sweep_index in range(2, ITERS):
        zero, one, two, two_low, pair_low, two_high, pair_high = nodes
        got = [shifted(two, 1, 0, 0), shifted(two_high, 1, 0, 1), shifted(two_low, 1, 0, -1)]
        got += [shifted(pair_high, 0, 0, 1), shifted(pair_low, 0, 0, -1)]
        done = sweep_index + 1 == ITERS
        later_rim = rim(later_rim_kernel, "later_rim", 0, (start, params, known_edge, zero, one, two, *got[3:]))
        nodes = call(
            functools.partial(later_kernel, width, n_y, n_x if done else None),
            "last" if done else "later",
            1,
            (is_first, start, params, known_edge, *inner(0), *later_rim, *got[:3]),
            [initial_state.shape] if done else [*nodes_only, *edge(HALO), *edge(HALO)],
            [pltpu.VMEM(tile, jnp.float32)] if done else (),
        )
    return nodes[0][None]


def solution(mesh):
    in_specs = (
        P(None, "gy", "gx", None),
        P("tm", None, "gy", "gx", None),
        P("gy", "gx", None),
        P("gy", "gx", None),
    )
    out_specs = P("tm", None, "gy", "gx", None)
    return jax.shard_map(shards, mesh=mesh, in_specs=in_specs, out_specs=out_specs, check_vma=False)
```

```python
import functools

import jax
import jax.numpy as jnp
from jax import lax
from jax.experimental import pallas as pl
from jax.experimental.pallas import tpu as pltpu
from jax.sharding import PartitionSpec as P

ITERS = 3
DIFF_U = 0.2
DIFF_V = 0.1
HALF_STEP = 0.5
WEIGHTS = ((5.0 / 24.0, 8.0 / 24.0, -1.0 / 24.0), (-1.0 / 24.0, 8.0 / 24.0, 5.0 / 24.0))

AXES = ("tm", "gy", "gx")
HALO = 5
RATE_HALO = 4
DRIFT = 6
TAKE = HALO + DRIFT
BELOW = (TAKE, TAKE, TAKE - 1, TAKE - 1)


def shifted(value, by_tm, by_gy, by_gx):
    n_tm, n_gy, n_gx = (lax.axis_size(axis) for axis in AXES)
    pairs = []
    for t in range(n_tm):
        for y in range(n_gy):
            for x in range(n_gx):
                target = ((t + by_tm) % n_tm * n_gy + (y + by_gy) % n_gy) * n_gx + (x + by_gx) % n_gx
                pairs.append(((t * n_gy + y) * n_gx + x, target))
    return lax.ppermute(value, AXES, pairs)


def near(row, distance, axis):
    size = row.shape[axis]
    return pltpu.roll(row, distance % size, axis) + pltpu.roll(row, -distance % size, axis)


def rates_of(state, feed, feed_kill, spacing):
    scale = 1.0 / (spacing * spacing)

    @functools.cache
    def at(r):
        (u, v), (ub, vb), (ua, va) = state(r), state(r - 1), state(r + 1)
        around_u = (ub + ua) + near(u, int(spacing), 0) + near(u, int(spacing), 1)
        around_v = (vb + va) + near(v, int(spacing), 0) + near(v, int(spacing), 1)
        reaction = u * (v * v)
        rate_u = (DIFF_U * scale) * around_u + feed(r) - (6.0 * DIFF_U * scale + feed(r)) * u - reaction
        rate_v = (DIFF_V * scale) * around_v - (6.0 * DIFF_V * scale + feed_kill(r)) * v + reaction
        return rate_u, rate_v

    return at


def half_sum(low, high):
    x, z = low.shape
    total = low + high
    total = total + pltpu.roll(total, z - 1, 1)
    total = total + pltpu.roll(total, x - 1, 0)
    return 0.125 * total


def restricted(state):
    @functools.cache
    def at(c):
        return tuple(half_sum(a, b) for a, b in zip(state(2 * c), state(2 * c + 1)))

    return at


def spread(row):
    even_x = lax.broadcasted_iota(jnp.int32, row.shape, 0) % 2 == 0
    even_z = lax.broadcasted_iota(jnp.int32, row.shape, 1) % 2 == 0
    row = jnp.where(even_z, row, pltpu.roll(row, 1, 1))
    return jnp.where(even_x, row, pltpu.roll(row, 1, 0))


def quadrature(values, interval):
    def at(r):
        zero, one, two = (value(r) for value in values)
        w = WEIGHTS[interval]
        return tuple(w[0] * a + w[1] * b + w[2] * c for a, b, c in zip(zero, one, two))

    return at


INNER_COUNT = 12


def inner_rows(n_y, tile_first):
    low, high = max(tile_first, -HALO), min(tile_first + n_y, n_y + HALO)
    halves = lambda first, last: (-(-first // 2), last // 2)
    clip = lambda rows, by: (max(rows[0], -by), min(rows[1], n_y // 2 + by))
    inside = lambda rows: (rows[0] + 1, rows[1] - 1)
    fine = [(low + k, high - k) for k in (1, 1, 2, 2, 3)]
    start, one, integral = halves(low, high), halves(*fine[1]), halves(*fine[4])
    coarse = [clip(start, 2), clip(one, 1), clip(integral, 1), clip(integral, 0)]
    return [*fine, *coarse, clip(inside(start), 1), clip(inside(one), 0), clip(halves(*fine[3]), 0)]


def inner_shapes(width, n_y, n_z, tile_first):
    return [(2, (high - low) * width, n_z) for low, high in inner_rows(n_y, tile_first)]


def inner_of(refs, width, n_y, tile_first):
    return [(low, high, rows_of(ref, width, low)) for (low, high), ref in zip(inner_rows(n_y, tile_first), refs)]


def write_inner(values, width, n_y, tile_first, refs):
    items = []
    for i, ((low, high), rows, ref) in enumerate(zip(inner_rows(n_y, tile_first), values, refs)):
        for r in range(low, high):
            ready = r + (0, 0, 1, 1, 2)[i] if i < 5 else 2 * r + (1, 1, 3, 3, 3, 3, 2)[i - 5]
            items.append((ready, i, r, rows, ref, low))
    for _, _, r, rows, ref, low in sorted(items, key=lambda item: item[:3]):
        for field, value in enumerate(rows(r)):
            ref[field, pl.ds((r - low) * width, width), :] = value


def old_terms(rates):
    def term(interval):
        @functools.cache
        def at(r):
            return tuple(q - HALF_STEP * f for q, f in zip(quadrature(rates, interval)(r), rates[interval](r)))

        return at

    return term(0), term(1)


def rim_rows(n_y, tile_first):
    needed = ((-RATE_HALO, n_y + RATE_HALO), (1 - RATE_HALO, n_y + RATE_HALO - 1))
    inner = (inner_rows(n_y, tile_first)[place] for place in (1, 3))
    return [[r for r in range(*every) if not low <= r < high] for every, (low, high) in zip(needed, inner)]


def write_rim(terms, width, n_y, tile_first, refs):
    places = [(r, i, k) for i, rows in enumerate(rim_rows(n_y, tile_first)) for k, r in enumerate(rows)]
    for r, i, k in sorted(places):
        for field, value in enumerate(terms[i](r)):
            refs[i][field, pl.ds(k * width, width), :] = value


def rim_of(refs, width, n_y, tile_first):
    def one(ref, rows):
        return lambda r: rows_of(ref, width, 0)(rows.index(r))

    return [one(ref, rows) for ref, rows in zip(refs, rim_rows(n_y, tile_first))]


def iteration(start, feed, kill, terms, inner=()):
    inner = iter(inner)

    def known_or(values):
        low, high, known = next(inner, (0, 0, None))
        return lambda r: (known if low <= r < high else values)(r)

    feed_kill = functools.cache(lambda r: feed(r) + kill(r))
    coarse_feed = functools.cache(lambda c: half_sum(feed(2 * c), feed(2 * c + 1)))
    coarse_sum = functools.cache(lambda c: half_sum(feed_kill(2 * c), feed_kill(2 * c + 1)))

    def stepped(state, rate, interval):
        @functools.cache
        def at(r):
            out = [s + HALF_STEP * f for s, f in zip(state(r), rate(r))]
            if terms is not None:
                out = [o + term for o, term in zip(out, terms[interval](r))]
            return tuple(out)

        return at

    fine = lambda state: rates_of(state, feed, feed_kill, 1.0)
    coarse = lambda state: rates_of(state, coarse_feed, coarse_sum, 2.0)
    rate_zero = known_or(fine(start))
    node_one = known_or(stepped(start, rate_zero, 0))
    rate_one = known_or(fine(node_one))
    node_two = known_or(stepped(node_one, rate_one, 1))
    rate_two = known_or(fine(node_two))
    fresh = (rate_zero, rate_one, rate_two)
    rest_zero, rest_one, rest_two = known_or(restricted(start)), known_or(restricted(node_one)), restricted(node_two)
    rest_integral = [known_or(restricted(quadrature(fresh, interval))) for interval in (0, 1)]
    rate_rest_zero, rate_rest_one = known_or(coarse(rest_zero)), known_or(coarse(rest_one))
    rest_two = known_or(rest_two)
    coarse_start, rate_coarse_start = rest_zero, rate_rest_zero

    def coarse_stepped(state, rate, rest_rate, integral):
        @functools.cache
        def at(c):
            return tuple(
                s + HALF_STEP * (f - g) + q for s, f, g, q in zip(state(c), rate(c), rest_rate(c), integral(c))
            )

        return at

    coarse_one = coarse_stepped(coarse_start, rate_coarse_start, rate_rest_zero, rest_integral[0])
    coarse_two = coarse_stepped(coarse_one, coarse(coarse_one), rate_rest_one, rest_integral[1])

    def corrected(node, coarse_node, rest):
        change = functools.cache(lambda c: tuple(spread(w - m) for w, m in zip(coarse_node(c), rest(c))))

        @functools.cache
        def at(r):
            return tuple(n + d for n, d in zip(node(r), change(r // 2)))

        return at

    nodes = corrected(node_one, coarse_one, rest_one), corrected(node_two, coarse_two, rest_two)
    fine_rows = (rate_zero, node_one, rate_one, node_two, rate_two)
    return (rate_zero, *nodes), (*fine_rows, rest_zero, rest_one, *rest_integral, rate_rest_zero, rate_rest_one, rest_two)


def rows_of(ref, width, first):
    @functools.cache
    def at(r):
        assert 0 <= (r - first) * width < ref.shape[1]
        return tuple(ref[field, pl.ds((r - first) * width, width), :] for field in range(2))

    return at


def pack_kernel(tiles_ref, state_ref, all_ref, high_ref):
    n_fields, n_x, n_y, _ = tiles_ref.shape
    for field in range(n_fields):
        for x in range(n_x):
            all_ref[field, pl.ds(x, n_y, stride=n_x), :] = tiles_ref[field, x]
        count = BELOW[field]
        rows = all_ref[field, pl.ds((n_y - count) * n_x, count * n_x), :]
        high_ref[pl.ds(sum(BELOW[:field]) * n_x, count * n_x), :] = rows
    for field in range(2):
        state_ref[field] = all_ref[field]


def collect(out_ref, field, source_field, n_x, lowest, pieces):
    width = n_x * len(pieces[0][1])
    for first, refs, count in pieces:
        for gy, ref in enumerate(refs):
            for k in range(count):
                if first + k >= lowest:
                    place = pl.ds((first + k - lowest) * width + gy * n_x, n_x)
                    out_ref[field, place, :] = ref[source_field, pl.ds(k * n_x, n_x), :]


def first_inner_kernel(n_gy, n_x, n_y, *refs):
    state_ref, local_ref = refs[:2]
    others = refs[2 : 1 + n_gy]
    start_ref, params_ref, *outs = refs[1 + n_gy :]
    width = n_gy * n_x
    for field in range(2):
        collect(start_ref, field, field, n_x, 0, [(0, [state_ref, *others], n_y)])
        collect(params_ref, field, 2 + field, n_x, 0, [(0, [local_ref, *others], n_y)])
    start, params = rows_of(start_ref, width, DRIFT), rows_of(params_ref, width, DRIFT)
    _, values = iteration(start, lambda r: params(r)[0], lambda r: params(r)[1], None)
    write_inner(values, width, n_y, DRIFT, outs)


def first_kernel(n_gy, n_x, n_y, *refs):
    tiles, inner_refs, refs = refs[:2], refs[2 : 2 + INNER_COUNT], refs[2 + INNER_COUNT :]
    lows, (start_ref, params_ref, *outs) = refs[:n_gy], refs[n_gy:]
    width = n_gy * n_x
    for field in range(2):
        for out_ref, tile_ref, place in zip((start_ref, params_ref), tiles, (0, 2)):
            count, begin = BELOW[place + field], sum(BELOW[: place + field])
            for gy, low_ref in enumerate(lows):
                for k in range(count):
                    row = pl.ds((TAKE - count + k) * width + gy * n_x, n_x)
                    out_ref[field, row, :] = low_ref[pl.ds((begin + k) * n_x, n_x), :]
            out_ref[field, pl.ds(TAKE * width, n_y * width), :] = tile_ref[field]
    start = rows_of(start_ref, width, -HALO)
    params = rows_of(params_ref, width, -HALO)
    inner = inner_of(inner_refs, width, n_y, DRIFT)
    results, _ = iteration(start, lambda r: params(r)[0], lambda r: params(r)[1], None, inner)
    write_nodes(results, width, n_y, [(0, TAKE)], *outs)
    for rows, place, count in ((start, 4 * TAKE, HALO), (params, 4 * TAKE + 2 * HALO, RATE_HALO)):
        for r in range(count):
            for field, value in enumerate(rows(r + DRIFT)):
                outs[-1][pl.ds((place + field * count + r) * width, width), :] = value


def write_nodes(results, width, n_y, edges, zero_ref, one_ref, two_ref, *edge_refs):
    rate_zero, node_one, node_two = results
    for r in range(-RATE_HALO, n_y + RATE_HALO):
        if 0 <= r < n_y:
            place = pl.ds(r * width, width)
            for field, (one, two) in enumerate(zip(node_one(r), node_two(r))):
                one_ref[field, place, :] = one
                two_ref[field, place, :] = two
                for i, (first, count) in enumerate(edges):
                    if first <= r < first + count:
                        beside = pl.ds((r - first) * width, width)
                        edge_refs[2 * i][field, beside, :] = two
                        for at, value in ((field, one), (2 + field, two)):
                            edge_refs[2 * i + 1][pl.ds((at * count + r - first) * width, width), :] = value
        for field, zero in enumerate(rate_zero(r)):
            zero_ref[field, pl.ds((r + RATE_HALO) * width, width), :] = zero


def joined(*parts):
    def at(r):
        return [rows for first, rows in parts if first <= r][-1](r)

    return at


def flat_rows(ref, width, place, first, count):
    @functools.cache
    def at(r):
        assert 0 <= r - first < count
        return tuple(ref[pl.ds((place + field * count + r - first) * width, width), :] for field in range(2))

    return at


def known(width, n_y, start_ref, params_ref, edge_ref):
    return (
        joined((-TAKE, rows_of(ref, width, -TAKE)), (n_y, flat_rows(edge_ref, width, place, n_y, count)))
        for ref, place, count in ((start_ref, 4 * TAKE, HALO), (params_ref, 4 * TAKE + 2 * HALO, RATE_HALO))
    )


def later_iteration(is_first, kept, params, got, terms, inner=()):
    @functools.cache
    def start(r):
        return tuple(jnp.where(is_first, a, b) for a, b in zip(kept(r), got(r)))

    return iteration(start, lambda r: params(r)[0], lambda r: params(r)[1], terms, inner)


def terms_of(params, old_zero, ones, twos):
    feed = lambda r: params(r)[0]
    feed_kill = functools.cache(lambda r: params(r)[0] + params(r)[1])
    return old_terms((old_zero(feed, feed_kill), *(rates_of(rows, feed, feed_kill, 1.0) for rows in (ones, twos))))


def inner_kernel(width, n_y, tile_first, first_ref, start_ref, params_ref, zero_ref, one_ref, two_ref, got_ref, *outs):
    kept, params = rows_of(start_ref, width, -TAKE), rows_of(params_ref, width, -TAKE)
    old_zero = rows_of(zero_ref, width, tile_first - RATE_HALO)
    ones, twos, got = (rows_of(ref, width, tile_first) for ref in (one_ref, two_ref, got_ref))
    terms = terms_of(params, lambda feed, feed_kill: old_zero, ones, twos)
    _, values = later_iteration(first_ref[0] == 1, kept, params, got, terms)
    write_inner(values, width, n_y, tile_first, outs)


def moved(width, n_y, tile_ref, beside):
    return joined((-DRIFT, rows_of(tile_ref, width, -DRIFT)), (n_y - DRIFT, beside))


def second_rim_kernel(width, n_y, start_ref, params_ref, zero_ref, one_ref, two_ref, pair_edge, *outs):
    kept, params = known(width, n_y, start_ref, params_ref, pair_edge)
    end = n_y - DRIFT
    ones, twos = (
        moved(width, n_y, ref, flat_rows(pair_edge, width, place * TAKE, end, TAKE))
        for ref, place in ((one_ref, 0), (two_ref, 2))
    )

    def old_zero(feed, feed_kill):
        inside = rows_of(zero_ref, width, -RATE_HALO - DRIFT)
        return joined((-RATE_HALO - DRIFT, inside), (end + RATE_HALO, rates_of(kept, feed, feed_kill, 1.0)))

    write_rim(terms_of(params, old_zero, ones, twos), width, n_y, -DRIFT, outs)


def second_kernel(width, n_y, first_ref, start_ref, params_ref, *refs):
    inner = inner_of(refs, width, n_y, -DRIFT)
    terms = rim_of(refs[INNER_COUNT:], width, n_y, -DRIFT)
    got_ref, got_edge, pair_edge, *outs = refs[INNER_COUNT + 2 :]
    kept, params = known(width, n_y, start_ref, params_ref, pair_edge)
    got = moved(width, n_y, got_ref, rows_of(got_edge, width, n_y - DRIFT))
    results, _ = later_iteration(first_ref[0] == 1, kept, params, got, terms, inner)
    write_nodes(results, width, n_y, [(0, HALO), (n_y - HALO, HALO)], *outs)


def window(width, n_y, low, tile_ref, high):
    return joined((-HALO, low), (0, rows_of(tile_ref, width, 0)), (n_y, high))


def later_rim_kernel(
    width, n_y, start_ref, params_ref, known_ref, zero_ref, one_ref, two_ref, pair_low, pair_high, *outs
):
    _, params = known(width, n_y, start_ref, params_ref, known_ref)

    def pair(tile_ref, place):
        low, high = (
            flat_rows(ref, width, place * HALO, first, HALO) for ref, first in ((pair_low, -HALO), (pair_high, n_y))
        )
        return window(width, n_y, low, tile_ref, high)

    old_zero = rows_of(zero_ref, width, -RATE_HALO)
    terms = terms_of(params, lambda feed, feed_kill: old_zero, pair(one_ref, 0), pair(two_ref, 2))
    write_rim(terms, width, n_y, 0, outs)


def later_kernel(width, n_y, out_x, first_ref, start_ref, params_ref, known_ref, *refs):
    inner = inner_of(refs, width, n_y, 0)
    terms = rim_of(refs[INNER_COUNT:], width, n_y, 0)
    got_ref, got_low, got_high, *outs = refs[INNER_COUNT + 2 :]
    kept, params = known(width, n_y, start_ref, params_ref, known_ref)
    got = window(width, n_y, rows_of(got_low, width, -HALO), got_ref, rows_of(got_high, width, n_y))
    results, _ = later_iteration(first_ref[0] == 1, kept, params, got, terms, inner)
    if out_x is None:
        write_nodes(results, width, n_y, [(0, HALO), (n_y - HALO, HALO)], *outs)
    else:
        out_ref, scratch = outs
        for r in range(n_y):
            for field, value in enumerate(results[2](r)):
                scratch[field, pl.ds(r * width, width), :] = value
        for x in range(out_x):
            for field in range(2):
                out_ref[field, x] = scratch[field, pl.ds(x, n_y, stride=width), :]


def call(kernel, name, n_scalars, operands, shapes, scratch=()):
    specs = [pl.BlockSpec(memory_space=pltpu.SMEM)] * n_scalars
    specs += [pl.BlockSpec(memory_space=pltpu.VMEM)] * (len(operands) - n_scalars)
    return pl.pallas_call(
        kernel,
        name=name,
        out_shape=[jax.ShapeDtypeStruct(shape, jnp.float32) for shape in shapes],
        in_specs=specs,
        out_specs=[pl.BlockSpec(memory_space=pltpu.VMEM)] * len(shapes),
        scratch_shapes=scratch,
        compiler_params=pltpu.CompilerParams(vmem_limit_bytes=32 * 1024 * 1024),
    )(*operands)


def shards(initial_state, slice_guess, feed_rate, kill_rate):
    n_gy, n_tm = lax.axis_size("gy"), lax.axis_size("tm")
    _, n_x, n_y, n_z = initial_state.shape
    width = n_gy * n_x
    place = lax.axis_index("tm")
    is_first = (place == 0).astype(jnp.int32)[None]

    sent = jnp.where(place == n_tm - 1, initial_state, slice_guess[0])
    state, local, high = call(
        pack_kernel,
        "pack",
        0,
        (jnp.concatenate([sent, feed_rate[None], kill_rate[None]]),),
        [(2, n_y * n_x, n_z), (4, n_y * n_x, n_z), (sum(BELOW) * n_x, n_z)],
    )
    got = [shifted(state, 1, 0, 0), local]
    got += [shifted(local, 1, -gy, 0) for gy in range(1, n_gy)]
    below = [shifted(high, 1, -gy, 1) for gy in range(n_gy)]

    tile, window = (2, n_y * width, n_z), (2, (TAKE + n_y) * width, n_z)
    nodes_only = [(2, (n_y + 2 * RATE_HALO) * width, n_z), tile, tile]
    edge = lambda rows, more=0: [(2, rows * width, n_z), ((4 * rows + more) * width, n_z)]
    inner_first = call(
        functools.partial(first_inner_kernel, n_gy, n_x, n_y),
        "inner_first",
        0,
        got,
        [tile, tile, *inner_shapes(width, n_y, n_z, DRIFT)],
    )
    start, params, *nodes = call(
        functools.partial(first_kernel, n_gy, n_x, n_y),
        "first",
        0,
        [*inner_first, *below],
        [window, window, *nodes_only, *edge(TAKE, 2 * HALO + 2 * RATE_HALO)],
    )
    zero, one, two, two_edge, pair_edge = nodes
    got = [shifted(two, 1, 0, 0), shifted(two_edge, 1, 0, -1), shifted(pair_edge, 0, 0, -1)]
    known_edge = got[-1]

    def inner(tile_first):
        return call(
            functools.partial(inner_kernel, width, n_y, tile_first),
            "inner",
            1,
            (is_first, start, params, *nodes[:3], got[0]),
            inner_shapes(width, n_y, n_z, tile_first),
        )

    def rim(kernel, name, tile_first, operands):
        shapes = [(2, len(rows) * width, n_z) for rows in rim_rows(n_y, tile_first)]
        return call(functools.partial(kernel, width, n_y), name, 0, operands, shapes)

    zero, one, two = nodes[:3]
    second_rim = rim(second_rim_kernel, "second_rim", -DRIFT, (start, params, zero, one, two, known_edge))
    nodes = call(
        functools.partial(second_kernel, width, n_y),
        "second",
        1,
        (is_first, start, params, *inner(-DRIFT), *second_rim, *got),
        [*nodes_only, *edge(HALO), *edge(HALO)],
    )
    for sweep_index in range(2, ITERS):
        zero, one, two, two_low, pair_low, two_high, pair_high = nodes
        got = [shifted(two, 1, 0, 0), shifted(two_high, 1, 0, 1), shifted(two_low, 1, 0, -1)]
        got += [shifted(pair_high, 0, 0, 1), shifted(pair_low, 0, 0, -1)]
        done = sweep_index + 1 == ITERS
        later_rim = rim(later_rim_kernel, "later_rim", 0, (start, params, known_edge, zero, one, two, *got[3:]))
        nodes = call(
            functools.partial(later_kernel, width, n_y, n_x if done else None),
            "last" if done else "later",
            1,
            (is_first, start, params, known_edge, *inner(0), *later_rim, *got[:3]),
            [initial_state.shape] if done else [*nodes_only, *edge(HALO), *edge(HALO)],
            [pltpu.VMEM(tile, jnp.float32)] if done else (),
        )
    return nodes[0][None]


def solution(mesh):
    in_specs = (
        P(None, "gy", "gx", None),
        P("tm", None, "gy", "gx", None),
        P("gy", "gx", None),
        P("gy", "gx", None),
    )
    out_specs = P("tm", None, "gy", "gx", None)
    return jax.shard_map(shards, mesh=mesh, in_specs=in_specs, out_specs=out_specs, check_vma=False)
```
